32 devices in a mesh: replica: 4 (over y, x), shard: 8 (over z, core).
Axes of the slice: x: 2, y: 2, z: 4, core: 2. Of those that a mesh axis runs over, the one named last changes fastest.
Arguments:
- tokens: bfloat16 [4096, 1600], P(('replica', 'shard')), may hold values from -6 to 6
- offsets: int32 [4, 8, 1], replicated, may hold values from 0 to 896, as said below
- qkv_weight: bfloat16 [1600, 4800], P('shard'), may hold values from -0.15625 to 0.15625
- out_weight: bfloat16 [1600, 1600], P('shard'), may hold values from -0.625 to 0.625
- fc_weight: bfloat16 [1600, 6400], P('shard'), may hold values from -0.15625 to 0.15625
- proj_weight: bfloat16 [6400, 1600], P('shard'), may hold values from -0.078125 to 0.078125
- query_bias: bfloat16 [1600], P('shard'), may hold values from -3 to 3
- value_bias: bfloat16 [1600], P('shard'), may hold values from -3 to 3
- out_bias: bfloat16 [1600], P('shard'), may hold values from -3 to 3
- fc_bias: bfloat16 [6400], P('shard'), may hold values from -3 to 3
- proj_bias: bfloat16 [1600], P('shard'), may hold values from -3 to 3
- gain_first: bfloat16 [1600], P('shard'), may hold values from 0.25 to 1.75
- shift_first: bfloat16 [1600], P('shard'), may hold values from -2 to 2
- gain_second: bfloat16 [1600], P('shard'), may hold values from 0.25 to 1.75
- shift_second: bfloat16 [1600], P('shard'), may hold values from -2 to 2
- cotangent: bfloat16 [4096, 1600], P(('replica', 'shard')), may hold values from -6 to 6
Outputs:
- output: bfloat16 [4096, 1600], P(('replica', 'shard'))
- tokens_grad: bfloat16 [4096, 1600], P(('replica', 'shard'))
- qkv_grad: float32 [1600, 4800], P('shard')
- outw_grad: float32 [1600, 1600], P('shard')
- fc_grad: float32 [1600, 6400], P('shard')
- proj_grad: float32 [6400, 1600], P('shard')
- qbias_grad: float32 [1600], P('shard')
- vbias_grad: float32 [1600], P('shard')
- obias_grad: float32 [1600], P('shard')
- fbias_grad: float32 [6400], P('shard')
- pbias_grad: float32 [1600], P('shard')
- gfirst_grad: float32 [1600], P('shard')
- sfirst_grad: float32 [1600], P('shard')
- gsecond_grad: float32 [1600], P('shard')
- ssecond_grad: float32 [1600], P('shard')
The draws below stay inside these ranges and needn't reach their ends.
Inputs may be any that keep to these rules, and one draw needn't show every extreme that they name: For every group and every sequence s, offsets[g, 0:8, s] are 0, 128, ..., 896 in some order, so the group's blocks cover the sequence once.
All inputs are finite; a program needn't handle non-finite values.
Results may differ from the reference program's by a relative error of at most 0.018.
Values may be sent and summed in bfloat16 or wider, within the bound.
No kernel may reach another device: no remote copies, remote signals or barrier semaphores. Data moves between devices by JAX's collectives and lax.ppermute only.
A program may use at most 320 MiB of HBM per device.

```python
import jax
import jax.numpy as jnp
from jax import lax

D = 1600
H = 25
HD = 64
FF = 6400
CP = 8
STRETCH = 128
SEQ_GRP = 1
GROUPS = 4
TOKENS = 4096


def draw_offsets(key, part):
    key = jax.random.fold_in(key, 11)
    orders = jax.vmap(lambda subkey: jax.random.permutation(subkey, CP))(jax.random.split(key, GROUPS * SEQ_GRP))
    return (orders.reshape(GROUPS, SEQ_GRP, CP).transpose(0, 2, 1) * STRETCH).astype(jnp.int32)


def block_scale(own_key, dims, cuts, smallest, high):
    loudness = 1.0
    for dim, blocks in cuts:
        heights = jax.random.uniform(jax.random.fold_in(jax.random.fold_in(own_key, 6), dim), (blocks,), jnp.float32, smallest / len(cuts), high / len(cuts))
        loudness = loudness * jnp.repeat(jnp.exp(heights), dims[dim] // blocks).reshape((-1,) + (1,) * (len(dims) - 1 - dim))
    return loudness


def scatter_about(rng, shape, width, most, pieces=(), kind=jnp.bfloat16):
    entries = jax.random.normal(rng, shape, jnp.float32) * width
    if len(pieces) > 0:
        entries = block_scale(rng, shape, pieces, -0.22, 0.18) * entries
    return jnp.clip(entries, min=-most, max=most).astype(kind)


def setup_inputs(seed: int = 0) -> dict:
    streams_of = jax.random.split(jax.random.key(seed), 17)
    tokens = scatter_about(streams_of[0], (TOKENS, D), 1.0, 6.0, ((0, 32),))
    offsets = draw_offsets(jax.random.fold_in(streams_of[16], 71), 0)
    qkv_weight = scatter_about(streams_of[2], (D, 3 * D), D ** -0.5, 0.15625, ((0, 8),))
    out_weight = scatter_about(streams_of[3], (D, D), (D // 16) ** -0.5, 0.625, ((0, 8),))
    fc_weight = scatter_about(streams_of[4], (D, FF), D ** -0.5, 0.15625, ((0, 8),))
    proj_weight = scatter_about(streams_of[5], (FF, D), FF ** -0.5, 0.078125, ((0, 8),))
    query_bias = scatter_about(streams_of[6], (D,), 0.5, 3.0, ((0, 8),))
    value_bias = scatter_about(streams_of[7], (D,), 0.5, 3.0, ((0, 8),))
    out_bias = scatter_about(streams_of[8], (D,), 0.5, 3.0, ((0, 8),))
    fc_bias = scatter_about(streams_of[9], (FF,), 0.5, 3.0, ((0, 8),))
    proj_bias = scatter_about(streams_of[10], (D,), 0.5, 3.0, ((0, 8),))
    gain_first = jnp.clip(1.0 + 0.15 * jax.random.normal(streams_of[11], (D,), jnp.float32), 0.25, 1.75).astype(jnp.bfloat16)
    shift_first = scatter_about(streams_of[12], (D,), 0.3, 2.0, ((0, 8),))
    gain_second = jnp.clip(1.0 + 0.15 * jax.random.normal(streams_of[13], (D,), jnp.float32), 0.25, 1.75).astype(jnp.bfloat16)
    shift_second = scatter_about(streams_of[14], (D,), 0.3, 2.0, ((0, 8),))
    cotangent = scatter_about(streams_of[15], (TOKENS, D), 1.0, 6.0, ((0, 32),))
    return {"tokens": tokens, "offsets": offsets, "qkv_weight": qkv_weight, "out_weight": out_weight, "fc_weight": fc_weight, "proj_weight": proj_weight, "query_bias": query_bias, "value_bias": value_bias, "out_bias": out_bias, "fc_bias": fc_bias, "proj_bias": proj_bias, "gain_first": gain_first, "shift_first": shift_first, "gain_second": gain_second, "shift_second": shift_second, "cotangent": cotangent}


@jax.custom_vjp
def low(v):
    return lax.optimization_barrier(v.astype(jnp.bfloat16)).astype(jnp.float32)

@jax.custom_vjp
def low_back(v):
    return v

def low_keep(v):
    return (low(v), None)

def low_pass(kept, grad):
    return (grad,)

def back_keep(v):
    return (v, None)

def back_low(kept, grad):
    return (low(grad),)
low.defvjp(low_keep, low_pass)
low_back.defvjp(back_keep, back_low)
norm_eps = 1e-05
masked_score = -1e+30
gelu_coeff = 0.7978845608028654

def layer_norm(values, gain_vec, shift_vec):
    average = lax.optimization_barrier(jnp.mean(values, axis=-1, keepdims=True))
    centred = values - average
    variance = lax.optimization_barrier(jnp.mean(centred * centred, axis=-1, keepdims=True))
    return centred * lax.rsqrt(variance + norm_eps) * gain_vec + shift_vec

def gelu_tanh(values):
    return 0.5 * values * (1.0 + jnp.tanh(gelu_coeff * (values + 0.044715 * values * values * values)))

def product(left_side, right_side):
    return jnp.dot(left_side, right_side, precision=lax.Precision.HIGHEST, preferred_element_type=jnp.float32)

def attend(inputs):
    queries, keys_all, values_all, places = inputs
    scores = jnp.einsum('qhd,khd->hqk', queries, keys_all, precision=lax.Precision.HIGHEST) * HD ** (-0.5)
    scores = low_back(scores)
    allowed = places[None, :] <= places[:, None]
    scores = jnp.where(allowed[None], scores, masked_score)
    highest = lax.optimization_barrier(jnp.max(scores, axis=-1, keepdims=True))
    weights = jnp.exp(scores - highest)
    probabilities = low(weights / lax.optimization_barrier(jnp.sum(weights, axis=-1, keepdims=True)))
    return jnp.einsum('hqk,khd->qhd', probabilities, values_all, precision=lax.Precision.HIGHEST)

def block_forward(params, inputs, block_offsets):
    qkv_weight, out_weight, fc_weight, proj_weight, query_bias, value_bias, out_bias, fc_bias, proj_bias, gain_first, shift_first, gain_second, shift_second = params
    normed = low(layer_norm(inputs, gain_first, shift_first))
    projected = product(normed, qkv_weight)
    queries = low_back(low(projected[:, :D] + query_bias))
    keys_all = low_back(low(projected[:, D:2 * D]))
    values_all = low_back(low(projected[:, 2 * D:] + value_bias))

    def by_sequence(stacked):
        return stacked.reshape(CP, SEQ_GRP, STRETCH, H, HD).transpose(1, 0, 2, 3, 4).reshape(SEQ_GRP, CP * STRETCH, H, HD)
    places = (block_offsets.T[:, :, None] + jnp.arange(STRETCH, dtype=jnp.int32)[None, None, :]).reshape(SEQ_GRP, CP * STRETCH)
    attended = lax.map(jax.checkpoint(attend), (by_sequence(queries), by_sequence(keys_all), by_sequence(values_all), places))
    attended = attended.reshape(SEQ_GRP, CP, STRETCH, D).transpose(1, 0, 2, 3).reshape(CP * SEQ_GRP * STRETCH, D)
    attended = low_back(low(attended))
    branch = low_back(product(attended, out_weight) + out_bias)
    middle = inputs + branch
    normed_two = low(layer_norm(middle, gain_second, shift_second))
    hidden = low_back(product(normed_two, fc_weight) + fc_bias)
    active = low(gelu_tanh(hidden))
    return middle + product(active, proj_weight) + proj_bias

def reference(tokens, offsets, qkv_weight, out_weight, fc_weight, proj_weight, query_bias, value_bias, out_bias, fc_bias, proj_bias, gain_first, shift_first, gain_second, shift_second, cotangent):
    params = tuple((argument.astype(jnp.float32) for argument in (qkv_weight, out_weight, fc_weight, proj_weight, query_bias, value_bias, out_bias, fc_bias, proj_bias, gain_first, shift_first, gain_second, shift_second)))
    group_rows = CP * SEQ_GRP * STRETCH
    inputs = tokens.astype(jnp.float32).reshape(GROUPS, group_rows, D)
    cotangents = cotangent.astype(jnp.float32).reshape(GROUPS, group_rows, D)

    def group_step(totals, argument):
        group_input, group_offsets, group_cot = argument
        result, pullback = jax.vjp(lambda weights, values: block_forward(weights, values, group_offsets), params, group_input)
        grad_params, grad_input = pullback(group_cot)
        totals = tuple((total_one + grad_one for total_one, grad_one in zip(totals, grad_params)))
        return (totals, (result, grad_input))
    zero_grads = tuple((jnp.zeros_like(argument) for argument in params))
    totals, (results, grad_inputs) = lax.scan(group_step, zero_grads, (inputs, offsets, cotangents))
    output = results.reshape(TOKENS, D).astype(jnp.bfloat16)
    tokens_grad = grad_inputs.reshape(TOKENS, D).astype(jnp.bfloat16)
    return (output, tokens_grad, totals[0], totals[1], totals[2], totals[3], totals[4], totals[5], totals[6], totals[7], totals[8], totals[9], totals[10], totals[11], totals[12])
```

```python
import functools

import jax
import jax.numpy as jnp
from jax import lax
from jax.experimental import pallas as pl
from jax.experimental.pallas import tpu as pltpu
from jax.experimental.layout import Layout, with_layout_constraint
from jax.sharding import PartitionSpec as P

D = 1600
H = 25
HD = 64
CP = 8
STRETCH = 128
SEQ = CP * STRETCH
TILE = 256

norm_eps = 1e-05
masked_score = -1e30
gelu_coeff = 0.7978845608028654
low = jnp.bfloat16
full = jnp.float32


def xor_send(block, axis, bits):
    count = lax.axis_size(axis)
    return lax.ppermute(block, axis, [(i, i ^ bits) for i in range(count)])


def normed(values):
    average = jnp.mean(values, axis=-1, keepdims=True)
    centred = values - average
    variance = jnp.mean(centred * centred, axis=-1, keepdims=True)
    return centred * lax.rsqrt(variance + norm_eps)


def layer_norm(values, gain_vec, shift_vec):
    return normed(values) * gain_vec + shift_vec


def gelu_tanh(values):
    return (
        0.5 * values * (1.0 + jnp.tanh(gelu_coeff * (values + 0.044715 * values * values * values)))
    )


def mm(left_side, right_side, left_dim, right_dim):
    return lax.dot_general(
        left_side,
        right_side,
        (((left_dim,), (right_dim,)), ((), ())),
        preferred_element_type=full,
    )


def sort_blocks(order_ref, seq, source, target):
    for place in range(CP):
        start = pl.multiple_of(order_ref[seq, place] * STRETCH, STRETCH)
        target[place * STRETCH : (place + 1) * STRETCH, :] = source[pl.ds(start, STRETCH), :]


def unsort_tile(order_ref, seq, tile, value, target):
    for part in range(TILE // STRETCH):
        place = tile * (TILE // STRETCH) + part
        start = pl.multiple_of(order_ref[seq, place] * STRETCH, STRETCH)
        target[pl.ds(start, STRETCH), :] = value[part * STRETCH : (part + 1) * STRETCH, :]


def causal(scores):
    key_row = lax.broadcasted_iota(jnp.int32, scores.shape, 0)
    query_col = lax.broadcasted_iota(jnp.int32, scores.shape, 1)
    return jnp.where(key_row <= query_col, scores, masked_score)


def forward_kernel(heads, seqs, order_ref, q_ref, k_ref, v_ref, a_ref, lse_ref, qs, ks, vs, qt, vt):
    width = heads * HD
    for seq in range(seqs):
        sort_blocks(order_ref, seq, q_ref, qs)
        sort_blocks(order_ref, seq, k_ref, ks)
        sort_blocks(order_ref, seq, v_ref, vs)
        qt[...] = (qs[...].astype(full).T * HD ** (-0.5)).astype(low)
        vt[...] = vs[...].astype(full).T.astype(low)
        for tile in range(SEQ // TILE):
            cols = slice(tile * TILE, (tile + 1) * TILE)
            before = tile * TILE
            pieces = []
            for head in range(heads):
                row = lax.broadcasted_iota(jnp.int32, (width, TILE), 0)
                mine = (row >= head * HD) & (row < (head + 1) * HD)
                query = jnp.where(mine, qt[:, cols], jnp.zeros((), low))
                diag = causal(mm(ks[cols, :], query, 1, 0))
                high = jnp.max(diag, axis=0, keepdims=True)
                if tile:
                    past = mm(ks[:before, :], query, 1, 0)
                    high = jnp.maximum(high, jnp.max(past, axis=0, keepdims=True))
                    past = jnp.exp(past - high)
                diag = jnp.exp(diag - high)
                total = jnp.sum(diag, axis=0, keepdims=True)
                if tile:
                    total = total + jnp.sum(past, axis=0, keepdims=True)
                share = 1.0 / total
                own = slice(head * HD, (head + 1) * HD)
                mixed = mm(vt[own, cols], (diag * share).astype(low), 1, 0)
                if tile:
                    mixed = mixed + mm(vt[own, :before], (past * share).astype(low), 1, 0)
                pieces.append(mixed)
                lse_ref[seq, head : head + 1, cols] = high + jnp.log(total)
            mixed = jnp.concatenate(pieces, 0).T.astype(low)
            unsort_tile(order_ref, seqs + seq, tile, mixed, a_ref)


def backward_kernel(
    heads, seqs, order_ref, q_ref, k_ref, v_ref, da_ref, lse_ref,
    dq_ref, dk_ref, dv_ref, qs, ks, vs, das, qt, kt, dat, dks, dvs,
):
    width = heads * HD
    scale = HD ** (-0.5)
    for seq in range(seqs):
        sort_blocks(order_ref, seq, q_ref, qs)
        sort_blocks(order_ref, seq, k_ref, ks)
        sort_blocks(order_ref, seq, v_ref, vs)
        sort_blocks(order_ref, 2 * seqs + seq, da_ref, das)
        qt[...] = (qs[...].astype(full).T * scale).astype(low)
        kt[...] = (ks[...].astype(full).T * scale).astype(low)
        dat[...] = das[...].astype(full).T.astype(low)
        dks[...] = jnp.zeros_like(dks)
        dvs[...] = jnp.zeros_like(dvs)
        for tile in range(SEQ // TILE):
            cols = slice(tile * TILE, (tile + 1) * TILE)
            before = tile * TILE
            pieces = []
            for head in range(heads):
                own = slice(head * HD, (head + 1) * HD)
                row = lax.broadcasted_iota(jnp.int32, (width, TILE), 0)
                mine = (row >= head * HD) & (row < (head + 1) * HD)
                lane = lax.broadcasted_iota(jnp.int32, (TILE, width), 1)
                mine_lane = (lane >= head * HD) & (lane < (head + 1) * HD)
                none = jnp.zeros((), low)
                query_t = jnp.where(mine, qt[:, cols], none)
                grad_t = jnp.where(mine, dat[:, cols], none)
                query = jnp.where(mine_lane, qs[cols, :], none)
                grad = jnp.where(mine_lane, das[cols, :], none)
                log_total = lse_ref[seq, head : head + 1, cols]

                spans = [(cols, True)] + ([(slice(0, before), False)] if tile else [])
                kept = []
                dot = None
                for span, edge in spans:
                    scores = mm(ks[span, :], query_t, 1, 0)
                    if edge:
                        scores = causal(scores)
                    weights = jnp.exp(scores - log_total)
                    weight_grads = mm(vs[span, :], grad_t, 1, 0)
                    part = jnp.sum(weights * weight_grads, axis=0, keepdims=True)
                    dot = part if dot is None else dot + part
                    dvs[span, :] += mm(weights.astype(low), grad, 1, 0)
                    kept.append((span, weights, weight_grads))
                total = None
                for span, weights, weight_grads in kept:
                    score_grads = (weights * (weight_grads - dot)).astype(low)
                    dks[span, :] += mm(score_grads, query, 1, 0)
                    part = mm(kt[own, span], score_grads, 1, 0)
                    total = part if total is None else total + part
                pieces.append(total)
            unsort_tile(order_ref, seq, tile, jnp.concatenate(pieces, 0).T.astype(low), dq_ref)
        for tile in range(SEQ // TILE):
            cols = slice(tile * TILE, (tile + 1) * TILE)
            unsort_tile(order_ref, seq, tile, (dks[cols, :] * scale).astype(low), dk_ref)
            unsort_tile(order_ref, seq, tile, dvs[cols, :].astype(low), dv_ref)


vmem = pl.BlockSpec(memory_space=pltpu.VMEM)
smem = pl.BlockSpec(memory_space=pltpu.SMEM)


def attend_forward(order, queries, keys, values, heads):
    rows, width = queries.shape
    seqs = rows // SEQ
    return pl.pallas_call(
        functools.partial(forward_kernel, heads, seqs),
        out_shape=(
            jax.ShapeDtypeStruct((rows, width), low),
            jax.ShapeDtypeStruct((seqs, heads, SEQ), full),
        ),
        in_specs=[smem, vmem, vmem, vmem],
        out_specs=(vmem, vmem),
        scratch_shapes=[pltpu.VMEM((SEQ, width), low)] * 3 + [pltpu.VMEM((width, SEQ), low)] * 2,
        compiler_params=pltpu.CompilerParams(vmem_limit_bytes=40 * 2**20),
        cost_estimate=pl.CostEstimate(
            flops=seqs * heads * 2 * 2 * SEQ * SEQ * 256,
            bytes_accessed=8 * rows * width,
            transcendentals=seqs * heads * SEQ * SEQ,
        ),
        name="attend_forward",
    )(order, queries, keys, values)


def attend_backward(order, queries, keys, values, grads, log_total, heads):
    rows, width = queries.shape
    seqs = rows // SEQ
    shape = jax.ShapeDtypeStruct((rows, width), low)
    return pl.pallas_call(
        functools.partial(backward_kernel, heads, seqs),
        out_shape=(shape, shape, shape),
        in_specs=[smem, vmem, vmem, vmem, vmem, vmem],
        out_specs=(vmem, vmem, vmem),
        scratch_shapes=[pltpu.VMEM((SEQ, width), low)] * 4
        + [pltpu.VMEM((width, SEQ), low)] * 3
        + [pltpu.VMEM((SEQ, width), full)] * 2,
        compiler_params=pltpu.CompilerParams(vmem_limit_bytes=48 * 2**20),
        cost_estimate=pl.CostEstimate(
            flops=seqs * heads * 2 * 5 * SEQ * SEQ * 256,
            bytes_accessed=14 * rows * width,
            transcendentals=seqs * heads * SEQ * SEQ,
        ),
        name="attend_backward",
    )(order, queries, keys, values, grads, log_total)


def ranks(count):
    return list(range(0, count, 2)) + list(range(1, count, 2))


def rank_of(bits, count):
    return (bits & 1) * (count // 2) + (bits >> 1)


def windows(rows, copies, unit):
    step = rows // copies // unit * unit
    return step, rows - step * (copies - 1)


def local_call(kernel, shapes, scratch, name, where, *operands, after=()):
    operands = operands + tuple(after)
    many = isinstance(shapes, (list, tuple))
    size = sum(x.size * x.dtype.itemsize for x in operands)
    free = pl.BlockSpec(memory_space=pl.ANY)
    used = len(operands) - len(after)
    return pl.pallas_call(
        kernel,
        out_shape=tuple(shapes) if many else shapes,
        in_specs=[smem] + [vmem] * used + [free] * len(after),
        out_specs=tuple(vmem for _ in shapes) if many else vmem,
        scratch_shapes=scratch,
        compiler_params=pltpu.CompilerParams(vmem_limit_bytes=56 * 2**20),
        cost_estimate=pl.CostEstimate(flops=0, bytes_accessed=3 * size, transcendentals=0),
        name=name,
    )(where, *operands)


def pack_heads(where, weight, copies, count, width):
    step, span = windows(weight.shape[0], copies, 16)

    def kernel(where_ref, weight_ref, *refs):
        outs, pieces = refs[: count // 2], refs[count // 2]
        start = pl.multiple_of(where_ref[1] * step, 16)
        for other in range(count):
            low_col, high_col = other * width, min(D, (other + 1) * width)
            for third in range(3):
                have = max(0, high_col - low_col)
                at = third * width
                if have:
                    pieces[other, :, at : at + have] = weight_ref[
                        pl.ds(start, span), third * D + low_col : third * D + high_col
                    ]
                if have < width:
                    pieces[other, :, at + have : at + width] = jnp.zeros((span, width - have), low)
        for bits in range(count):
            outs[bits // 2][bits % 2] = pieces[where_ref[0] ^ bits]

    shape = jax.ShapeDtypeStruct((2, span, 3 * width), low)
    scratch = [pltpu.VMEM((count, span, 3 * width), low)]
    return local_call(kernel, [shape] * (count // 2), scratch, "pack_heads", where, weight)


def slot_rows(span):
    return -(-span // 16) * 16


def pack_columns(where, weight, out_weight, vectors, copies, count):
    step, span = windows(weight.shape[0], copies, 16)
    cols = weight.shape[1] // count
    slot = slot_rows(span)

    def kernel(where_ref, weight_ref, out_ref, vectors_ref, *refs):
        outs, pieces = refs[: count // 2], refs[count // 2]
        start = pl.multiple_of(where_ref[1] * step, 16)
        for other in range(count):
            pieces[other] = weight_ref[pl.ds(start, span), other * cols : (other + 1) * cols]
        for pair, out in enumerate(outs):
            for side in range(2):
                out[:span, side * cols : (side + 1) * cols] = pieces[
                    where_ref[0] ^ (2 * pair + side)
                ]
            out[slot : slot + span, :] = out_ref[pl.ds(start, span), :]
            out[2 * slot :, :] = vectors_ref[...]

    shape = jax.ShapeDtypeStruct((2 * slot + 16, D), low)
    scratch = [pltpu.VMEM((count, span, cols), low)]
    return local_call(
        kernel, [shape] * (count // 2), scratch, "pack_columns", where, weight, out_weight, vectors
    )


def split_columns(where, got, span, cols):
    half = len(got)
    slot = slot_rows(span)

    def kernel(where_ref, *refs):
        odd, rows = refs[half:]
        for pair in range(half):
            odd[pair] = refs[pair][:span, cols : 2 * cols]
            rows[pair] = refs[pair][slot : slot + span, :]

    shapes = [
        jax.ShapeDtypeStruct((half, span, cols), low),
        jax.ShapeDtypeStruct((half, span, D), low),
    ]
    return local_call(kernel, shapes, [], "split_columns", where, *got)


def assemble_rows(where, stacks, own_rows):
    each = len(stacks[0])
    count = sum(array.shape[0] for array in stacks[0])
    span, cols = stacks[0][0].shape[1:]
    step, _ = windows(own_rows, len(stacks), 16)
    stacks = stacks if step else stacks[:1]
    copies = len(stacks)
    arrays = [array for stack in stacks for array in stack]

    def kernel(where_ref, *refs):
        out = refs[-1]
        for bits_copy in range(copies):
            start = pl.multiple_of((where_ref[1] ^ bits_copy) * step, 16)
            blocks = [
                ref.at[row]
                for ref in refs[bits_copy * each : (bits_copy + 1) * each]
                for row in range(ref.shape[0])
            ]
            for block, bits in zip(blocks, ranks(count)):
                out[where_ref[0] ^ bits, pl.ds(start, span), :] = block[...]

    shape = jax.ShapeDtypeStruct((count, own_rows, cols), low)
    return local_call(kernel, shape, [], "assemble_rows", where, *arrays)


def split_heads(where, block, count, width):
    rows, cols = block.shape

    def kernel(where_ref, block_ref, *refs):
        outs, pieces = refs[: count // 2], refs[count // 2]
        for other in range(count):
            start, stop = min(cols, other * width), min(cols, (other + 1) * width)
            if start < stop:
                pieces[other, :, : stop - start] = block_ref[:, start:stop]
            if stop - start < width:
                pieces[other, :, stop - start :] = jnp.zeros((rows, width - stop + start), low)
        for bits in range(count):
            outs[bits // 2][bits % 2] = pieces[where_ref[0] ^ bits]

    shape = jax.ShapeDtypeStruct((2, rows, width), low)
    scratch = [pltpu.VMEM((count, rows, width), low)]
    return local_call(kernel, [shape] * (count // 2), scratch, "split_heads", where, block)


def order_heads(where, pairs, far):
    half = len(pairs)
    count = 2 * half
    _, rows, width = far.shape

    def kernel(where_ref, *refs):
        out, pieces = refs[-2], refs[-1]
        for pair in range(half):
            pieces[2 * pair] = refs[pair][0]
            pieces[2 * pair + 1] = refs[half][pair]
        for other in range(count):
            out[:, other * width : (other + 1) * width] = pieces[where_ref[0] ^ other]

    shape = jax.ShapeDtypeStruct((rows, count * width), low)
    scratch = [pltpu.VMEM((count, rows, width), low)]
    return local_call(kernel, shape, scratch, "order_heads", where, *pairs, far)


SLOTS = 4


def lane_of(bits, cols):
    return bits // SLOTS * cols


def own_block(ref, bits, cols, groups):
    slot, group = lax.rem(bits, SLOTS), lax.div(bits, SLOTS)
    value = ref[slot, :, :cols].astype(full)
    for index in range(1, groups):
        other = ref[slot, :, index * cols : (index + 1) * cols].astype(full)
        value = jnp.where(group == index, other, value)
    return value


def pack_hidden(where, fc_full, proj_full, sums, copies):
    count, rows, cols = fc_full.shape
    step, span = windows(rows, copies, 16)
    proj_step, proj_span = windows(proj_full.shape[0], copies, 8)
    extra = -(-(proj_span + 16) // span)
    after = slot_rows(proj_span) - (extra - 1) * span

    def kernel(where_ref, fc_ref, proj_ref, sums_ref, *outs):
        for index, out in enumerate(outs):
            copy = where_ref[1] ^ index
            start = pl.multiple_of(copy * step, 16)
            for bits in range(count):
                lane = lane_of(bits, cols)
                out[bits % SLOTS, :, lane : lane + cols] = fc_ref[
                    where_ref[0] ^ bits, pl.ds(start, span), :
                ].astype(low)
            first = copy * proj_step
            for slot in range(extra):
                length = min(span, proj_span - slot * span)
                if length > 0:
                    at = pl.multiple_of(first + slot * span, 8) if span % 8 == 0 else first
                    out[SLOTS + slot, :length, :] = proj_ref[pl.ds(at, length), :].astype(low)
            out[SLOTS + extra - 1, after : after + 16, : sums.shape[2]] = sums_ref[copy].astype(low)

    shape = jax.ShapeDtypeStruct((SLOTS + extra, span, D), low)
    return local_call(
        kernel, [shape] * copies, [], "pack_hidden", where, fc_full, proj_full, sums
    )


def sum_hidden(where, pieces, count, cols):
    number = len(pieces)
    slots, span, _ = pieces[0].shape

    def kernel(where_ref, *refs):
        outs, rest = refs[number:-1], refs[-1]
        for slot in range(slots):
            total = refs[0][slot].astype(full)
            for piece in refs[1:number]:
                total = total + piece[slot].astype(full)
            total = total.astype(low)
            if slot >= SLOTS:
                rest[slot - SLOTS] = total
                continue
            for bits in range(slot, count, SLOTS):
                lane = lane_of(bits, cols)
                outs[bits // 2][bits % 2] = total[:, lane : lane + cols]

    shapes = [jax.ShapeDtypeStruct((2, span, cols), low)] * (count // 2)
    shapes.append(jax.ShapeDtypeStruct((slots - SLOTS, span, D), low))
    outs = local_call(kernel, shapes, [], "sum_hidden", where, *pieces)
    return outs[:-1], outs[-1]


def join_hidden(where, got, far, rest):
    half = len(got)
    _, span, cols = far.shape

    def kernel(where_ref, *refs):
        out = refs[-1]
        for bits in range(2 * half):
            block = refs[half][bits // 2] if bits % 2 else refs[bits // 2][0]
            lane = lane_of(bits, cols)
            out[bits % SLOTS, :, lane : lane + cols] = block
        for slot in range(rest.shape[0]):
            out[SLOTS + slot] = refs[half + 1][slot]

    shape = jax.ShapeDtypeStruct((SLOTS + rest.shape[0], span, D), low)
    return local_call(kernel, shape, [], "join_hidden", where, *got, far, rest)


def finish_hidden(where, stacks, count, rows, cols, proj_rows, lanes):
    copies = len(stacks)
    slots, span, _ = stacks[0].shape
    step, _ = windows(rows, copies, 16)
    proj_step, proj_span = windows(proj_rows, copies, 8)
    extra = slots - SLOTS
    after = slot_rows(proj_span) - (extra - 1) * span

    def kernel(where_ref, *refs):
        fc_out, proj_out, sums_out = refs[copies:]
        for index in range(copies):
            piece, copy = refs[index], where_ref[1] ^ index
            start = pl.multiple_of(copy * step, 16)
            if step or index == 0:
                for other in range(count):
                    fc_out[pl.ds(start, span), other * cols : (other + 1) * cols] = own_block(
                        piece, where_ref[0] ^ other, cols, count // SLOTS
                    )
            for slot in range(extra):
                length = min(span, proj_span - slot * span)
                if length > 0:
                    at = copy * proj_step
                    at = pl.multiple_of(at + slot * span, 8) if span % 8 == 0 else at
                    proj_out[pl.ds(at, length), :] = piece[SLOTS + slot, :length, :].astype(full)
            sums_out[copy] = piece[SLOTS + extra - 1, after : after + 16, :lanes].astype(full)

    shapes = [
        jax.ShapeDtypeStruct((rows, count * cols), full),
        jax.ShapeDtypeStruct((proj_rows, D), full),
        jax.ShapeDtypeStruct((copies, 16, lanes), full),
    ]
    return local_call(kernel, shapes, [], "finish_hidden", where, *stacks)


def split_outw(where, grad, copies):
    count, rows, cols = grad.shape
    half = count // 2
    step, span = windows(rows, copies, 16)
    parts = copies if step else 1

    def kernel(where_ref, grad_ref, *refs):
        far = refs[parts]
        for index in range(parts):
            start = pl.multiple_of((where_ref[1] ^ index) * step, 16)
            for pair in range(half):
                for side, out in enumerate((refs[index], far.at[index])):
                    out[pair] = grad_ref[
                        where_ref[0] ^ (2 * pair + side), pl.ds(start, span), :
                    ].astype(low)

    shapes = [jax.ShapeDtypeStruct((half, span, cols), low)] * parts
    shapes.append(jax.ShapeDtypeStruct((parts, half, span, cols), low))
    outs = local_call(kernel, shapes, [], "split_outw", where, grad)
    return outs[:-1], outs[-1]


def pack_last(where, qkv_full, near, far, sums):
    copies, parts = sums.shape[0], len(near)
    count, rows, cols = qkv_full.shape
    half = count // 2
    step, span = windows(rows, copies, 16)
    spare = count // SLOTS * cols

    def kernel(where_ref, qkv_ref, *refs):
        far_ref, sums_ref = refs[parts], refs[parts + 1]
        for index, out in enumerate(refs[parts + 2 :]):
            copy = where_ref[1] ^ index
            start = pl.multiple_of(copy * step, 16)
            for bits in range(count):
                lane = lane_of(bits, cols)
                out[bits % SLOTS, :, lane : lane + cols] = qkv_ref[
                    where_ref[0] ^ bits, pl.ds(start, span), :
                ].astype(low)
                row = bits // SLOTS * 16
                out[bits % SLOTS, row : row + 16, spare : spare + 64] = sums_ref[copy, bits].astype(
                    low
                )
            for pair in range(half):
                total = refs[index % parts][pair].astype(full)
                total = total + far_ref[index % parts, pair].astype(full)
                out[SLOTS + pair] = total.astype(low)

    shape = jax.ShapeDtypeStruct((SLOTS + half, span, D), low)
    return local_call(kernel, [shape] * copies, [], "pack_last", where, qkv_full, *near, far, sums)


def sum_last(where, pieces, count, cols):
    number = len(pieces)
    half = count // 2
    span = pieces[0].shape[1]
    spare = count // SLOTS * cols

    def kernel(where_ref, *refs):
        outs = refs[number:]
        for slot in range(SLOTS + half):
            total = refs[0][slot].astype(full)
            for piece in refs[1:number]:
                total = total + piece[slot].astype(full)
            total = total.astype(low)
            if slot >= SLOTS:
                outs[slot - SLOTS][1] = total
                continue
            for bits in range(slot, count, SLOTS):
                lane, row, side = lane_of(bits, cols), bits // SLOTS * 16, bits % 2
                out = outs[bits // 2]
                out[0, :, side * cols : (side + 1) * cols] = total[:, lane : lane + cols]
                out[0, side * 16 : side * 16 + 16, 2 * cols : 2 * cols + 64] = total[
                    row : row + 16, spare : spare + 64
                ]

    shape = jax.ShapeDtypeStruct((2, span, D), low)
    return local_call(kernel, [shape] * half, [], "sum_last", where, *pieces)


def odd_last(where, got, cols):
    half = len(got)
    span = got[0].shape[1]

    def kernel(where_ref, *refs):
        out = refs[half]
        for pair in range(half):
            out[pair, :, :cols] = refs[pair][0, :, cols : 2 * cols]
            out[pair, :16, cols : cols + 64] = refs[pair][0, 16:32, 2 * cols : 2 * cols + 64]

    shape = jax.ShapeDtypeStruct((half, span, cols + 64), low)
    return local_call(kernel, shape, [], "odd_last", where, *got)


def join_last(where, got, far):
    half = len(got)
    _, span, wide = far.shape
    cols = wide - 64
    spare = 2 * half // SLOTS * cols

    def kernel(where_ref, *refs):
        far_ref, out = refs[half], refs[half + 1]
        sums = jnp.zeros((16, 64), full)
        total = jnp.zeros((span, D), full)
        for pair in range(half):
            for side in range(2):
                lane = lane_of(2 * pair + side, cols)
                block = far_ref[pair, :, :cols] if side else refs[pair][0, :, :cols]
                out[(2 * pair + side) % SLOTS, :, lane : lane + cols] = block
            sums = sums + refs[pair][0, :16, 2 * cols : 2 * cols + 64].astype(full)
            sums = sums + far_ref[pair, :16, cols : cols + 64].astype(full)
            total = total + refs[pair][1].astype(full)
        out[SLOTS] = total.astype(low)
        out[0, :16, spare : spare + 64] = sums.astype(low)

    shape = jax.ShapeDtypeStruct((SLOTS + 1, span, D), low)
    return local_call(kernel, shape, [], "join_last", where, *got, far)


def finish_last(where, stacks, count, rows, width):
    copies = len(stacks)
    span = stacks[0].shape[1]
    step, _ = windows(rows, copies, 16)
    cols = 3 * width
    spare = count // SLOTS * cols

    def kernel(where_ref, *refs):
        qkv_out, outw_out, sums_out = refs[copies:]
        for index in range(copies):
            piece, copy = refs[index], where_ref[1] ^ index
            start = pl.multiple_of(copy * step, 16)
            sums_out[copy] = piece[0, :16, spare : spare + 64].astype(full)
            if index and not step:
                continue
            outw_out[pl.ds(start, span), :] = piece[SLOTS].astype(full)
            for other in range(count):
                have = min(width, D - other * width)
                if have <= 0:
                    continue
                block = own_block(piece, where_ref[0] ^ other, cols, count // SLOTS)
                for third in range(3):
                    target = third * D + other * width
                    qkv_out[pl.ds(start, span), target : target + have] = block[
                        :, third * width : third * width + have
                    ]

    shapes = [
        jax.ShapeDtypeStruct((rows, 3 * D), full),
        jax.ShapeDtypeStruct((rows, D), full),
        jax.ShapeDtypeStruct((copies, 16, 64), full),
    ]
    return local_call(kernel, shapes, [], "finish_last", where, *stacks)


def on_device(
    tokens,
    offsets,
    qkv_weight,
    out_weight,
    fc_weight,
    proj_weight,
    query_bias,
    value_bias,
    out_bias,
    fc_bias,
    proj_bias,
    gain_first,
    shift_first,
    gain_second,
    shift_second,
    cotangent,
):
    count = lax.axis_size("shard")
    copies = lax.axis_size("replica")
    place = lax.axis_index("shard")
    copy = lax.axis_index("replica")
    where = jnp.stack([place, copy]).astype(jnp.int32)
    evens = list(range(0, count, 2))
    bits_of = ranks(count)
    half = count // 2
    heads = -(-H // count)
    span = windows(D // count, copies, 16)[1]
    width = heads * HD
    own_rows = D // count
    ff_cols = fc_weight.shape[1] // count

    def gather_rows(block):
        return lax.all_gather(block, "shard", axis=0, tiled=True)

    def scatter_rows(blocks):
        blocks = with_layout_constraint(blocks, Layout((0, 1)))
        return lax.psum_scatter(blocks, "shard", scatter_dimension=0, tiled=True)

    def exchange(pairs):
        got = [pairs[0]] + [xor_send(pairs[j], "shard", evens[j]) for j in range(1, half)]
        return got, xor_send(jnp.concatenate([pair[1:] for pair in got], 0), "shard", 1)

    def by_rank(got, far):
        return jnp.concatenate([pair[:1] for pair in got] + [far], 0)

    def from_copies(block):
        return [block] + [xor_send(block, "replica", bits) for bits in range(1, copies)]

    def to_copies(pieces):
        return [pieces[0]] + [xor_send(pieces[bits], "replica", bits) for bits in range(1, copies)]

    def tie(value, *others):
        return lax.optimization_barrier((value,) + others)[0]

    vectors = (
        query_bias,
        value_bias,
        out_bias,
        proj_bias,
        gain_first,
        shift_first,
        gain_second,
        shift_second,
    )
    token_all = gather_rows(tokens)
    qkv_got, qkv_far = exchange(pack_heads(where, qkv_weight, copies, count, width))
    qkv_stack = by_rank(qkv_got, qkv_far)
    vectors = tie(jnp.concatenate(vectors), qkv_stack)
    vectors = jnp.pad(vectors[None], ((0, 15), (0, D - 8 * own_rows)))
    fc_pairs = pack_columns(where, fc_weight, out_weight, vectors, copies, count)
    fc_got = [fc_pairs[0]] + [xor_send(fc_pairs[j], "shard", evens[j]) for j in range(1, half)]
    fc_odd, out_near = split_columns(where, fc_got, span, ff_cols)
    fc_far = xor_send(fc_odd, "shard", 1)
    vectors = jnp.concatenate([got[2 * slot_rows(span) :][:1] for got in fc_got], 0)
    vectors = jnp.concatenate([vectors, xor_send(vectors, "shard", 1)], 0)
    vectors = vectors[:, : 8 * own_rows].astype(full)
    chosen = (jnp.arange(count)[:, None] ^ place == jnp.array(bits_of)[None, :]).astype(full)
    vectors = lax.dot(chosen, vectors, precision=lax.Precision.HIGHEST)
    vectors = vectors.reshape(count, 8, own_rows).transpose(1, 0, 2).reshape(8, D)
    b_query, b_value, b_out, b_proj, g_first, s_first, g_second, s_second = vectors
    qkv_stacks = from_copies(qkv_stack)
    w_qkv = assemble_rows(where, [[stack] for stack in qkv_stacks], own_rows)
    w_qkv = w_qkv.reshape(D, 3 * width)

    out_near = from_copies(tie(out_near, *qkv_stacks))
    out_far = [xor_send(block, "shard", 1) for block in out_near]
    w_out = assemble_rows(where, list(zip(out_near, out_far)), own_rows).reshape(D, D)
    fc_stack = jnp.concatenate(
        [got[:span, :ff_cols][None] for got in fc_got] + [fc_far], 0
    )
    fc_stacks = from_copies(fc_stack)
    w_fc = assemble_rows(where, [[stack] for stack in fc_stacks], own_rows).reshape(D, ff_cols)

    def own_heads(vector):
        vector = jnp.pad(vector, (0, count * width - D))
        return lax.dynamic_slice_in_dim(vector, place * width, width, 0)

    seqs = count // CP
    starts = lax.dynamic_slice_in_dim(offsets, copy * seqs, seqs, 0)[:, :, 0] // STRETCH
    is_at = starts[:, None, :] == jnp.arange(CP)[None, :, None]
    order = jnp.sum(jnp.where(is_at, jnp.arange(CP)[None, None, :], 0), axis=2)
    order = order + CP * jnp.arange(seqs)[:, None]
    bits = order ^ place
    order = jnp.concatenate([order, bits, rank_of(bits, count)], 0).astype(jnp.int32)

    normed_low = layer_norm(token_all.astype(full), g_first, s_first).astype(low)
    projected = mm(normed_low, w_qkv, 1, 0)
    queries = (projected[:, :width] + own_heads(b_query)).astype(low)
    keys = tie(projected, fc_stack)[:, width : 2 * width].astype(low)
    values = (projected[:, 2 * width :] + own_heads(b_value)).astype(low)
    cot_all = gather_rows(tie(cotangent, queries))
    attended, log_total = attend_forward(order, queries, keys, values, heads)

    attended_own = order_heads(where, *exchange(list(attended.reshape(half, 2, STRETCH, width))))
    attended_own = attended_own[:, :D]
    in_rows = tokens.astype(full)
    middle = in_rows + mm(attended_own, w_out, 1, 0) + b_out
    second_own = layer_norm(middle, g_second, s_second).astype(low)
    second_all = gather_rows(tie(second_own, cot_all, *fc_stacks))
    hidden = mm(second_all, w_fc, 1, 0) + fc_bias.astype(full)
    active, pull_gelu = jax.vjp(gelu_tanh, hidden)
    active_low = active.astype(low)

    (hidden_grad,) = pull_gelu(mm(cot_all, proj_weight, 1, 1))
    hidden_low = hidden_grad.astype(low)
    second_part = mm(hidden_low, w_fc, 1, 1).astype(low)
    second_grad = scatter_rows(second_part).astype(full)

    proj_full = mm(tie(active_low, second_part), cot_all, 0, 0)
    fc_full = mm(tie(second_all, second_part), hidden_low, 0, 0)
    hidden_sums = jnp.sum(hidden_low.astype(full), axis=0).reshape(copies, 1, ff_cols // copies)
    hidden_sums = jnp.pad(hidden_sums, ((0, 0), (0, 15), (0, -ff_cols // copies % 128)))
    hidden_pieces = pack_hidden(
        where, fc_full.reshape(count, own_rows, ff_cols), proj_full, hidden_sums, copies
    )
    second_grad = tie(second_grad, hidden_pieces[0])
    hidden_pieces = to_copies(hidden_pieces)
    grad_rows = cotangent.astype(full)
    _, pull_second = jax.vjp(layer_norm, middle, g_second, s_second)
    middle_part, gsecond_part, ssecond_part = pull_second(second_grad)
    middle_grad = grad_rows + middle_part
    branch_low = middle_grad.astype(low)
    attended_grad = mm(branch_low, w_out, 1, 1).astype(low)
    attended_pairs = split_heads(where, attended_grad, count, width)
    outw_full = mm(attended_own, tie(branch_low, attended_pairs[0]), 0, 0)
    outw_near, outw_far = split_outw(where, outw_full.reshape(count, own_rows, D), copies)
    attended_grad = by_rank(*exchange(attended_pairs)).reshape(count * STRETCH, width)
    outw_far = xor_send(outw_far, "shard", 1)
    output_low = tie(active_low, attended_grad)
    attended_grad = tie(attended_grad, *hidden_pieces)
    early = jnp.stack(
        [jnp.sum(branch_low.astype(full), axis=0), jnp.sum(grad_rows, axis=0), gsecond_part, ssecond_part]
    )

    query_grads, key_grads, value_grads = attend_backward(
        order, queries, keys, values, attended_grad, log_total, heads
    )
    projected_grad = jnp.concatenate([query_grads, key_grads, value_grads], 1)
    first_part = mm(projected_grad, w_qkv, 1, 1)

    def head_sums(block):
        sums = jnp.sum(block.astype(full), axis=0)
        placed = lax.dynamic_update_slice_in_dim(
            jnp.zeros((count * width,), full), sums, place * width, 0
        )
        return placed[:D]

    norms = normed(token_all.astype(full))
    sums = jnp.stack(
        [
            head_sums(query_grads),
            head_sums(value_grads),
            early[0],
            early[1],
            jnp.sum(first_part * norms, axis=0),
            jnp.sum(first_part, axis=0),
            early[2],
            early[3],
        ]
    )
    sums = sums.reshape(8, count, own_rows).transpose(1, 0, 2).reshape(count, 8 * own_rows)
    by_bits = (jnp.arange(count)[:, None] ^ place == jnp.arange(count)[None, :]).astype(full)
    sums = lax.dot(by_bits, sums, precision=lax.Precision.HIGHEST)
    share = 8 * own_rows // copies
    sums = sums.reshape(count, copies, share).transpose(1, 0, 2)
    sums = jnp.pad(sums, ((0, 0), (0, 0), (0, 16 * 64 - share))).reshape(copies, count, 16, 64)
    first_grad = scatter_rows(first_part.astype(low)).astype(full)
    qkv_full = mm(normed_low, projected_grad, 0, 0).reshape(count, own_rows, 3 * width)
    last = pack_last(where, qkv_full, outw_near, outw_far, sums)
    first_grad = tie(first_grad, last[0])
    hidden_pieces[0] = tie(hidden_pieces[0], last[0])
    last = to_copies(last)

    fc_sums, rest = sum_hidden(where, hidden_pieces, count, ff_cols)
    hidden_stacks = from_copies(join_hidden(where, *exchange(fc_sums), rest))
    fc_grad, proj_grad, fbias = finish_hidden(
        where, hidden_stacks, count, own_rows, ff_cols, ff_cols, hidden_sums.shape[2]
    )
    fbias = fbias[:, 0, : ff_cols // copies].reshape(ff_cols)

    last = sum_last(where, last, count, 3 * width)
    last = [last[0]] + [xor_send(last[j], "shard", evens[j]) for j in range(1, half)]
    far = xor_send(odd_last(where, last, 3 * width), "shard", 1)
    last = from_copies(join_last(where, last, tie(far, hidden_stacks[1])))
    qkv_grad, outw_grad, sums = finish_last(where, last, count, own_rows, width)
    sums = sums.reshape(copies, 16 * 64)[:, :share].reshape(8, own_rows)

    output_part = mm(output_low, proj_weight, 1, 0).astype(low)
    output = middle + b_proj + scatter_rows(output_part).astype(full)

    _, pull_first = jax.vjp(lambda rows: layer_norm(rows, g_first, s_first), in_rows)
    (input_part,) = pull_first(first_grad)
    tokens_grad = (middle_grad + input_part).astype(low)
    qbias, vbias, obias, pbias, gfirst, sfirst, gsecond, ssecond = sums
    return (
        output.astype(low),
        tokens_grad,
        qkv_grad,
        outw_grad,
        fc_grad,
        proj_grad,
        qbias,
        vbias,
        obias,
        fbias,
        pbias,
        gfirst,
        sfirst,
        gsecond,
        ssecond,
    )


def solution(mesh):
    rows = P(("replica", "shard"), None)
    matrix = P("shard", None)
    vector = P("shard")
    return jax.shard_map(
        on_device,
        mesh=mesh,
        in_specs=(rows, P()) + (matrix,) * 4 + (vector,) * 9 + (rows,),
        out_specs=(rows, rows) + (matrix,) * 4 + (vector,) * 9,
        check_vma=False,
    )
```

```python
import functools

import jax
import jax.numpy as jnp
from jax import lax
from jax.experimental import pallas as pl
from jax.experimental.pallas import tpu as pltpu
from jax.experimental.layout import Layout, with_layout_constraint
from jax.sharding import PartitionSpec as P

D = 1600
H = 25
HD = 64
CP = 8
STRETCH = 128
SEQ = CP * STRETCH
TILE = 256

norm_eps = 1e-05
masked_score = -1e30
gelu_coeff = 0.7978845608028654
low = jnp.bfloat16
full = jnp.float32


def xor_send(block, axis, bits):
    count = lax.axis_size(axis)
    return lax.ppermute(block, axis, [(i, i ^ bits) for i in range(count)])


def normed(values):
    average = jnp.mean(values, axis=-1, keepdims=True)
    centred = values - average
    variance = jnp.mean(centred * centred, axis=-1, keepdims=True)
    return centred * lax.rsqrt(variance + norm_eps)


def layer_norm(values, gain_vec, shift_vec):
    return normed(values) * gain_vec + shift_vec


def gelu_tanh(values):
    return (
        0.5 * values * (1.0 + jnp.tanh(gelu_coeff * (values + 0.044715 * values * values * values)))
    )


def mm(left_side, right_side, left_dim, right_dim):
    return lax.dot_general(
        left_side,
        right_side,
        (((left_dim,), (right_dim,)), ((), ())),
        preferred_element_type=full,
    )


def sort_blocks(order_ref, seq, source, target):
    for place in range(CP):
        start = pl.multiple_of(order_ref[seq, place] * STRETCH, STRETCH)
        target[place * STRETCH : (place + 1) * STRETCH, :] = source[pl.ds(start, STRETCH), :]


def unsort_tile(order_ref, seq, tile, value, target):
    for part in range(TILE // STRETCH):
        place = tile * (TILE // STRETCH) + part
        start = pl.multiple_of(order_ref[seq, place] * STRETCH, STRETCH)
        target[pl.ds(start, STRETCH), :] = value[part * STRETCH : (part + 1) * STRETCH, :]


def causal(scores):
    key_row = lax.broadcasted_iota(jnp.int32, scores.shape, 0)
    query_col = lax.broadcasted_iota(jnp.int32, scores.shape, 1)
    return jnp.where(key_row <= query_col, scores, masked_score)


def forward_kernel(heads, seqs, order_ref, q_ref, k_ref, v_ref, a_ref, lse_ref, qs, ks, vs, qt, vt):
    width = heads * HD
    for seq in range(seqs):
        sort_blocks(order_ref, seq, q_ref, qs)
        sort_blocks(order_ref, seq, k_ref, ks)
        sort_blocks(order_ref, seq, v_ref, vs)
        qt[...] = (qs[...].astype(full).T * HD ** (-0.5)).astype(low)
        vt[...] = vs[...].astype(full).T.astype(low)
        for tile in range(SEQ // TILE):
            cols = slice(tile * TILE, (tile + 1) * TILE)
            before = tile * TILE
            pieces = []
            for head in range(heads):
                row = lax.broadcasted_iota(jnp.int32, (width, TILE), 0)
                mine = (row >= head * HD) & (row < (head + 1) * HD)
                query = jnp.where(mine, qt[:, cols], jnp.zeros((), low))
                diag = causal(mm(ks[cols, :], query, 1, 0))
                high = jnp.max(diag, axis=0, keepdims=True)
                if tile:
                    past = mm(ks[:before, :], query, 1, 0)
                    high = jnp.maximum(high, jnp.max(past, axis=0, keepdims=True))
                    past = jnp.exp(past - high)
                diag = jnp.exp(diag - high)
                total = jnp.sum(diag, axis=0, keepdims=True)
                if tile:
                    total = total + jnp.sum(past, axis=0, keepdims=True)
                share = 1.0 / total
                own = slice(head * HD, (head + 1) * HD)
                mixed = mm(vt[own, cols], (diag * share).astype(low), 1, 0)
                if tile:
                    mixed = mixed + mm(vt[own, :before], (past * share).astype(low), 1, 0)
                pieces.append(mixed)
                lse_ref[seq, head : head + 1, cols] = high + jnp.log(total)
            mixed = jnp.concatenate(pieces, 0).T.astype(low)
            unsort_tile(order_ref, seqs + seq, tile, mixed, a_ref)


def backward_kernel(
    heads, seqs, order_ref, q_ref, k_ref, v_ref, da_ref, lse_ref,
    dq_ref, dk_ref, dv_ref, qs, ks, vs, das, qt, kt, dat, dks, dvs,
):
    width = heads * HD
    scale = HD ** (-0.5)
    for seq in range(seqs):
        sort_blocks(order_ref, seq, q_ref, qs)
        sort_blocks(order_ref, seq, k_ref, ks)
        sort_blocks(order_ref, seq, v_ref, vs)
        sort_blocks(order_ref, 2 * seqs + seq, da_ref, das)
        qt[...] = (qs[...].astype(full).T * scale).astype(low)
        kt[...] = (ks[...].astype(full).T * scale).astype(low)
        dat[...] = das[...].astype(full).T.astype(low)
        dks[...] = jnp.zeros_like(dks)
        dvs[...] = jnp.zeros_like(dvs)
        for tile in range(SEQ // TILE):
            cols = slice(tile * TILE, (tile + 1) * TILE)
            before = tile * TILE
            pieces = []
            for head in range(heads):
                own = slice(head * HD, (head + 1) * HD)
                row = lax.broadcasted_iota(jnp.int32, (width, TILE), 0)
                mine = (row >= head * HD) & (row < (head + 1) * HD)
                lane = lax.broadcasted_iota(jnp.int32, (TILE, width), 1)
                mine_lane = (lane >= head * HD) & (lane < (head + 1) * HD)
                none = jnp.zeros((), low)
                query_t = jnp.where(mine, qt[:, cols], none)
                grad_t = jnp.where(mine, dat[:, cols], none)
                query = jnp.where(mine_lane, qs[cols, :], none)
                grad = jnp.where(mine_lane, das[cols, :], none)
                log_total = lse_ref[seq, head : head + 1, cols]

                spans = [(cols, True)] + ([(slice(0, before), False)] if tile else [])
                kept = []
                dot = None
                for span, edge in spans:
                    scores = mm(ks[span, :], query_t, 1, 0)
                    if edge:
                        scores = causal(scores)
                    weights = jnp.exp(scores - log_total)
                    weight_grads = mm(vs[span, :], grad_t, 1, 0)
                    part = jnp.sum(weights * weight_grads, axis=0, keepdims=True)
                    dot = part if dot is None else dot + part
                    dvs[span, :] += mm(weights.astype(low), grad, 1, 0)
                    kept.append((span, weights, weight_grads))
                total = None
                for span, weights, weight_grads in kept:
                    score_grads = (weights * (weight_grads - dot)).astype(low)
                    dks[span, :] += mm(score_grads, query, 1, 0)
                    part = mm(kt[own, span], score_grads, 1, 0)
                    total = part if total is None else total + part
                pieces.append(total)
            unsort_tile(order_ref, seq, tile, jnp.concatenate(pieces, 0).T.astype(low), dq_ref)
        for tile in range(SEQ // TILE):
            cols = slice(tile * TILE, (tile + 1) * TILE)
            unsort_tile(order_ref, seq, tile, (dks[cols, :] * scale).astype(low), dk_ref)
            unsort_tile(order_ref, seq, tile, dvs[cols, :].astype(low), dv_ref)


vmem = pl.BlockSpec(memory_space=pltpu.VMEM)
smem = pl.BlockSpec(memory_space=pltpu.SMEM)


def attend_forward(order, queries, keys, values, heads):
    rows, width = queries.shape
    seqs = rows // SEQ
    return pl.pallas_call(
        functools.partial(forward_kernel, heads, seqs),
        out_shape=(
            jax.ShapeDtypeStruct((rows, width), low),
            jax.ShapeDtypeStruct((seqs, heads, SEQ), full),
        ),
        in_specs=[smem, vmem, vmem, vmem],
        out_specs=(vmem, vmem),
        scratch_shapes=[pltpu.VMEM((SEQ, width), low)] * 3 + [pltpu.VMEM((width, SEQ), low)] * 2,
        compiler_params=pltpu.CompilerParams(vmem_limit_bytes=40 * 2**20),
        cost_estimate=pl.CostEstimate(
            flops=seqs * heads * 2 * 2 * SEQ * SEQ * 256,
            bytes_accessed=8 * rows * width,
            transcendentals=seqs * heads * SEQ * SEQ,
        ),
        name="attend_forward",
    )(order, queries, keys, values)


def attend_backward(order, queries, keys, values, grads, log_total, heads):
    rows, width = queries.shape
    seqs = rows // SEQ
    shape = jax.ShapeDtypeStruct((rows, width), low)
    return pl.pallas_call(
        functools.partial(backward_kernel, heads, seqs),
        out_shape=(shape, shape, shape),
        in_specs=[smem, vmem, vmem, vmem, vmem, vmem],
        out_specs=(vmem, vmem, vmem),
        scratch_shapes=[pltpu.VMEM((SEQ, width), low)] * 4
        + [pltpu.VMEM((width, SEQ), low)] * 3
        + [pltpu.VMEM((SEQ, width), full)] * 2,
        compiler_params=pltpu.CompilerParams(vmem_limit_bytes=48 * 2**20),
        cost_estimate=pl.CostEstimate(
            flops=seqs * heads * 2 * 5 * SEQ * SEQ * 256,
            bytes_accessed=14 * rows * width,
            transcendentals=seqs * heads * SEQ * SEQ,
        ),
        name="attend_backward",
    )(order, queries, keys, values, grads, log_total)


def ranks(count):
    return list(range(0, count, 2)) + list(range(1, count, 2))


def rank_of(bits, count):
    return (bits & 1) * (count // 2) + (bits >> 1)


def windows(rows, copies, unit):
    step = rows // copies // unit * unit
    return step, rows - step * (copies - 1)


def local_call(kernel, shapes, scratch, name, where, *operands, after=()):
    operands = operands + tuple(after)
    many = isinstance(shapes, (list, tuple))
    size = sum(x.size * x.dtype.itemsize for x in operands)
    free = pl.BlockSpec(memory_space=pl.ANY)
    used = len(operands) - len(after)
    return pl.pallas_call(
        kernel,
        out_shape=tuple(shapes) if many else shapes,
        in_specs=[smem] + [vmem] * used + [free] * len(after),
        out_specs=tuple(vmem for _ in shapes) if many else vmem,
        scratch_shapes=scratch,
        compiler_params=pltpu.CompilerParams(vmem_limit_bytes=56 * 2**20),
        cost_estimate=pl.CostEstimate(flops=0, bytes_accessed=3 * size, transcendentals=0),
        name=name,
    )(where, *operands)


def pack_heads(where, weight, copies, count, width):
    step, span = windows(weight.shape[0], copies, 16)

    def kernel(where_ref, weight_ref, *refs):
        outs, pieces = refs[: count // 2], refs[count // 2]
        start = pl.multiple_of(where_ref[1] * step, 16)
        for other in range(count):
            low_col, high_col = other * width, min(D, (other + 1) * width)
            for third in range(3):
                have = max(0, high_col - low_col)
                at = third * width
                if have:
                    pieces[other, :, at : at + have] = weight_ref[
                        pl.ds(start, span), third * D + low_col : third * D + high_col
                    ]
                if have < width:
                    pieces[other, :, at + have : at + width] = jnp.zeros((span, width - have), low)
        for bits in range(count):
            outs[bits // 2][bits % 2] = pieces[where_ref[0] ^ bits]

    shape = jax.ShapeDtypeStruct((2, span, 3 * width), low)
    scratch = [pltpu.VMEM((count, span, 3 * width), low)]
    return local_call(kernel, [shape] * (count // 2), scratch, "pack_heads", where, weight)


def slot_rows(span):
    return -(-span // 16) * 16


def pack_columns(where, weight, out_weight, vectors, copies, count):
    step, span = windows(weight.shape[0], copies, 16)
    cols = weight.shape[1] // count
    slot = slot_rows(span)

    def kernel(where_ref, weight_ref, out_ref, vectors_ref, *refs):
        outs, pieces = refs[: count // 2], refs[count // 2]
        start = pl.multiple_of(where_ref[1] * step, 16)
        for other in range(count):
            pieces[other] = weight_ref[pl.ds(start, span), other * cols : (other + 1) * cols]
        for pair, out in enumerate(outs):
            for side in range(2):
                out[:span, side * cols : (side + 1) * cols] = pieces[
                    where_ref[0] ^ (2 * pair + side)
                ]
            out[slot : slot + span, :] = out_ref[pl.ds(start, span), :]
            out[2 * slot :, :] = vectors_ref[...]

    shape = jax.ShapeDtypeStruct((2 * slot + 16, D), low)
    scratch = [pltpu.VMEM((count, span, cols), low)]
    return local_call(
        kernel, [shape] * (count // 2), scratch, "pack_columns", where, weight, out_weight, vectors
    )


def split_columns(where, got, span, cols):
    half = len(got)
    slot = slot_rows(span)

    def kernel(where_ref, *refs):
        odd, rows = refs[half:]
        for pair in range(half):
            odd[pair] = refs[pair][:span, cols : 2 * cols]
            rows[pair] = refs[pair][slot : slot + span, :]

    shapes = [
        jax.ShapeDtypeStruct((half, span, cols), low),
        jax.ShapeDtypeStruct((half, span, D), low),
    ]
    return local_call(kernel, shapes, [], "split_columns", where, *got)


def assemble_rows(where, stacks, own_rows):
    each = len(stacks[0])
    count = sum(array.shape[0] for array in stacks[0])
    span, cols = stacks[0][0].shape[1:]
    step, _ = windows(own_rows, len(stacks), 16)
    stacks = stacks if step else stacks[:1]
    copies = len(stacks)
    arrays = [array for stack in stacks for array in stack]

    def kernel(where_ref, *refs):
        out = refs[-1]
        for bits_copy in range(copies):
            start = pl.multiple_of((where_ref[1] ^ bits_copy) * step, 16)
            blocks = [
                ref.at[row]
                for ref in refs[bits_copy * each : (bits_copy + 1) * each]
                for row in range(ref.shape[0])
            ]
            for block, bits in zip(blocks, ranks(count)):
                out[where_ref[0] ^ bits, pl.ds(start, span), :] = block[...]

    shape = jax.ShapeDtypeStruct((count, own_rows, cols), low)
    return local_call(kernel, shape, [], "assemble_rows", where, *arrays)


def assemble_copies(where, stacks, own_rows):
    copies, count, span, cols = stacks.shape
    step, _ = windows(own_rows, copies, 16)

    def kernel(where_ref, stacks_ref, out):
        for copy in range(copies if step else 1):
            for rank, bits in enumerate(ranks(count)):
                out[where_ref[0] ^ bits, copy * step : copy * step + span, :] = stacks_ref[
                    copy, rank
                ]

    shape = jax.ShapeDtypeStruct((count, own_rows, cols), low)
    return local_call(kernel, shape, [], "assemble_copies", where, stacks)


def split_heads(where, block, count, width):
    rows, cols = block.shape

    def kernel(where_ref, block_ref, *refs):
        outs, pieces = refs[: count // 2], refs[count // 2]
        for other in range(count):
            start, stop = min(cols, other * width), min(cols, (other + 1) * width)
            if start < stop:
                pieces[other, :, : stop - start] = block_ref[:, start:stop]
            if stop - start < width:
                pieces[other, :, stop - start :] = jnp.zeros((rows, width - stop + start), low)
        for bits in range(count):
            outs[bits // 2][bits % 2] = pieces[where_ref[0] ^ bits]

    shape = jax.ShapeDtypeStruct((2, rows, width), low)
    scratch = [pltpu.VMEM((count, rows, width), low)]
    return local_call(kernel, [shape] * (count // 2), scratch, "split_heads", where, block)


def order_heads(where, pairs, far):
    half = len(pairs)
    count = 2 * half
    _, rows, width = far.shape

    def kernel(where_ref, *refs):
        out, pieces = refs[-2], refs[-1]
        for pair in range(half):
            pieces[2 * pair] = refs[pair][0]
            pieces[2 * pair + 1] = refs[half][pair]
        for other in range(count):
            out[:, other * width : (other + 1) * width] = pieces[where_ref[0] ^ other]

    shape = jax.ShapeDtypeStruct((rows, count * width), low)
    scratch = [pltpu.VMEM((count, rows, width), low)]
    return local_call(kernel, shape, scratch, "order_heads", where, *pairs, far)


SLOTS = 4


def lane_of(bits, cols):
    return bits // SLOTS * cols


def own_block(ref, bits, cols, groups):
    slot, group = lax.rem(bits, SLOTS), lax.div(bits, SLOTS)
    value = ref[slot, :, :cols].astype(full)
    for index in range(1, groups):
        other = ref[slot, :, index * cols : (index + 1) * cols].astype(full)
        value = jnp.where(group == index, other, value)
    return value


def pack_hidden(where, fc_full, proj_full, sums, copies):
    count, rows, cols = fc_full.shape
    step, span = windows(rows, copies, 16)
    proj_step, proj_span = windows(proj_full.shape[0], copies, 8)
    extra = -(-(proj_span + 16) // span)
    after = slot_rows(proj_span) - (extra - 1) * span

    def kernel(where_ref, fc_ref, proj_ref, sums_ref, out_ref):
        for copy in range(copies):
            out = out_ref.at[copy]
            for bits in range(count):
                lane = lane_of(bits, cols)
                out[bits % SLOTS, :, lane : lane + cols] = fc_ref[
                    where_ref[0] ^ bits, copy * step : copy * step + span, :
                ].astype(low)
            for slot in range(extra):
                length = min(span, proj_span - slot * span)
                if length > 0:
                    at = copy * proj_step + slot * span
                    out[SLOTS + slot, :length, :] = proj_ref[at : at + length, :].astype(low)
            out[SLOTS + extra - 1, after : after + 16, : sums.shape[2]] = sums_ref[copy].astype(low)

    shape = jax.ShapeDtypeStruct((copies, SLOTS + extra, span, D), low)
    return local_call(kernel, shape, [], "pack_hidden", where, fc_full, proj_full, sums)


def sum_hidden(where, pieces, count, cols):
    number = len(pieces)
    slots, span, _ = pieces[0].shape

    def kernel(where_ref, *refs):
        outs, rest = refs[number:-1], refs[-1]
        for slot in range(slots):
            total = refs[0][slot].astype(full)
            for piece in refs[1:number]:
                total = total + piece[slot].astype(full)
            total = total.astype(low)
            if slot >= SLOTS:
                rest[slot - SLOTS] = total
                continue
            for bits in range(slot, count, SLOTS):
                lane = lane_of(bits, cols)
                outs[bits // 2][bits % 2] = total[:, lane : lane + cols]

    shapes = [jax.ShapeDtypeStruct((2, span, cols), low)] * (count // 2)
    shapes.append(jax.ShapeDtypeStruct((slots - SLOTS, span, D), low))
    outs = local_call(kernel, shapes, [], "sum_hidden", where, *pieces)
    return outs[:-1], outs[-1]


def join_hidden(where, got, far, rest):
    half = len(got)
    _, span, cols = far.shape

    def kernel(where_ref, *refs):
        out = refs[-1]
        for bits in range(2 * half):
            block = refs[half][bits // 2] if bits % 2 else refs[bits // 2][0]
            lane = lane_of(bits, cols)
            out[bits % SLOTS, :, lane : lane + cols] = block
        for slot in range(rest.shape[0]):
            out[SLOTS + slot] = refs[half + 1][slot]

    shape = jax.ShapeDtypeStruct((SLOTS + rest.shape[0], span, D), low)
    return local_call(kernel, shape, [], "join_hidden", where, *got, far, rest)


def finish_hidden(where, stacks, count, rows, cols, proj_rows, lanes):
    copies = len(stacks)
    slots, span, _ = stacks[0].shape
    step, _ = windows(rows, copies, 16)
    proj_step, proj_span = windows(proj_rows, copies, 8)
    extra = slots - SLOTS
    after = slot_rows(proj_span) - (extra - 1) * span

    def kernel(where_ref, *refs):
        fc_out, proj_out, sums_out = refs[copies:]
        for index in range(copies):
            piece, copy = refs[index], where_ref[1] ^ index
            start = pl.multiple_of(copy * step, 16)
            if step or index == 0:
                for other in range(count):
                    fc_out[pl.ds(start, span), other * cols : (other + 1) * cols] = own_block(
                        piece, where_ref[0] ^ other, cols, count // SLOTS
                    )
            for slot in range(extra):
                length = min(span, proj_span - slot * span)
                if length > 0:
                    at = copy * proj_step
                    at = pl.multiple_of(at + slot * span, 8) if span % 8 == 0 else at
                    proj_out[pl.ds(at, length), :] = piece[SLOTS + slot, :length, :].astype(full)
            sums_out[copy] = piece[SLOTS + extra - 1, after : after + 16, :lanes].astype(full)

    shapes = [
        jax.ShapeDtypeStruct((rows, count * cols), full),
        jax.ShapeDtypeStruct((proj_rows, D), full),
        jax.ShapeDtypeStruct((copies, 16, lanes), full),
    ]
    return local_call(kernel, shapes, [], "finish_hidden", where, *stacks)


def split_outw(where, grad, copies):
    count, rows, cols = grad.shape
    half = count // 2
    step, span = windows(rows, copies, 16)
    parts = copies if step else 1

    def kernel(where_ref, grad_ref, *refs):
        far = refs[parts]
        for index in range(parts):
            start = pl.multiple_of((where_ref[1] ^ index) * step, 16)
            for pair in range(half):
                for side, out in enumerate((refs[index], far.at[index])):
                    out[pair] = grad_ref[
                        where_ref[0] ^ (2 * pair + side), pl.ds(start, span), :
                    ].astype(low)

    shapes = [jax.ShapeDtypeStruct((half, span, cols), low)] * parts
    shapes.append(jax.ShapeDtypeStruct((parts, half, span, cols), low))
    outs = local_call(kernel, shapes, [], "split_outw", where, grad)
    return outs[:-1], outs[-1]


def pack_last(where, qkv_full, near, far, sums):
    copies, parts = sums.shape[0], len(near)
    count, rows, cols = qkv_full.shape
    half = count // 2
    step, span = windows(rows, copies, 16)
    spare = count // SLOTS * cols

    def kernel(where_ref, qkv_ref, *refs):
        far_ref, sums_ref = refs[parts], refs[parts + 1]
        for index, out in enumerate(refs[parts + 2 :]):
            copy = where_ref[1] ^ index
            start = pl.multiple_of(copy * step, 16)
            for bits in range(count):
                lane = lane_of(bits, cols)
                out[bits % SLOTS, :, lane : lane + cols] = qkv_ref[
                    where_ref[0] ^ bits, pl.ds(start, span), :
                ].astype(low)
                row = bits // SLOTS * 16
                out[bits % SLOTS, row : row + 16, spare : spare + 64] = sums_ref[copy, bits].astype(
                    low
                )
            for pair in range(half):
                total = refs[index % parts][pair].astype(full)
                total = total + far_ref[index % parts, pair].astype(full)
                out[SLOTS + pair] = total.astype(low)

    shape = jax.ShapeDtypeStruct((SLOTS + half, span, D), low)
    return local_call(kernel, [shape] * copies, [], "pack_last", where, qkv_full, *near, far, sums)


def sum_last(where, pieces, count, cols):
    number = len(pieces)
    half = count // 2
    span = pieces[0].shape[1]
    spare = count // SLOTS * cols

    def kernel(where_ref, *refs):
        outs = refs[number:]
        for slot in range(SLOTS + half):
            total = refs[0][slot].astype(full)
            for piece in refs[1:number]:
                total = total + piece[slot].astype(full)
            total = total.astype(low)
            if slot >= SLOTS:
                outs[slot - SLOTS][1] = total
                continue
            for bits in range(slot, count, SLOTS):
                lane, row, side = lane_of(bits, cols), bits // SLOTS * 16, bits % 2
                out = outs[bits // 2]
                out[0, :, side * cols : (side + 1) * cols] = total[:, lane : lane + cols]
                out[0, side * 16 : side * 16 + 16, 2 * cols : 2 * cols + 64] = total[
                    row : row + 16, spare : spare + 64
                ]

    shape = jax.ShapeDtypeStruct((2, span, D), low)
    return local_call(kernel, [shape] * half, [], "sum_last", where, *pieces)


def odd_last(where, got, cols):
    half = len(got)
    span = got[0].shape[1]

    def kernel(where_ref, *refs):
        out = refs[half]
        for pair in range(half):
            out[pair, :, :cols] = refs[pair][0, :, cols : 2 * cols]
            out[pair, :16, cols : cols + 64] = refs[pair][0, 16:32, 2 * cols : 2 * cols + 64]

    shape = jax.ShapeDtypeStruct((half, span, cols + 64), low)
    return local_call(kernel, shape, [], "odd_last", where, *got)


def join_last(where, got, far):
    half = len(got)
    _, span, wide = far.shape
    cols = wide - 64
    spare = 2 * half // SLOTS * cols

    def kernel(where_ref, *refs):
        far_ref, out = refs[half], refs[half + 1]
        sums = jnp.zeros((16, 64), full)
        total = jnp.zeros((span, D), full)
        for pair in range(half):
            for side in range(2):
                lane = lane_of(2 * pair + side, cols)
                block = far_ref[pair, :, :cols] if side else refs[pair][0, :, :cols]
                out[(2 * pair + side) % SLOTS, :, lane : lane + cols] = block
            sums = sums + refs[pair][0, :16, 2 * cols : 2 * cols + 64].astype(full)
            sums = sums + far_ref[pair, :16, cols : cols + 64].astype(full)
            total = total + refs[pair][1].astype(full)
        out[SLOTS] = total.astype(low)
        out[0, :16, spare : spare + 64] = sums.astype(low)

    shape = jax.ShapeDtypeStruct((SLOTS + 1, span, D), low)
    return local_call(kernel, shape, [], "join_last", where, *got, far)


def finish_last(where, stacks, count, rows, width):
    copies = len(stacks)
    span = stacks[0].shape[1]
    step, _ = windows(rows, copies, 16)
    cols = 3 * width
    spare = count // SLOTS * cols

    def kernel(where_ref, *refs):
        qkv_out, outw_out, sums_out = refs[copies:]
        for index in range(copies):
            piece, copy = refs[index], where_ref[1] ^ index
            start = pl.multiple_of(copy * step, 16)
            sums_out[copy] = piece[0, :16, spare : spare + 64].astype(full)
            if index and not step:
                continue
            outw_out[pl.ds(start, span), :] = piece[SLOTS].astype(full)
            for other in range(count):
                have = min(width, D - other * width)
                if have <= 0:
                    continue
                block = own_block(piece, where_ref[0] ^ other, cols, count // SLOTS)
                for third in range(3):
                    target = third * D + other * width
                    qkv_out[pl.ds(start, span), target : target + have] = block[
                        :, third * width : third * width + have
                    ]

    shapes = [
        jax.ShapeDtypeStruct((rows, 3 * D), full),
        jax.ShapeDtypeStruct((rows, D), full),
        jax.ShapeDtypeStruct((copies, 16, 64), full),
    ]
    return local_call(kernel, shapes, [], "finish_last", where, *stacks)


def on_device(
    tokens,
    offsets,
    qkv_weight,
    out_weight,
    fc_weight,
    proj_weight,
    query_bias,
    value_bias,
    out_bias,
    fc_bias,
    proj_bias,
    gain_first,
    shift_first,
    gain_second,
    shift_second,
    cotangent,
):
    count = lax.axis_size("shard")
    copies = lax.axis_size("replica")
    place = lax.axis_index("shard")
    copy = lax.axis_index("replica")
    where = jnp.stack([place, copy]).astype(jnp.int32)
    evens = list(range(0, count, 2))
    bits_of = ranks(count)
    half = count // 2
    heads = -(-H // count)
    span = windows(D // count, copies, 16)[1]
    width = heads * HD
    own_rows = D // count
    ff_cols = fc_weight.shape[1] // count

    def gather_rows(block):
        return lax.all_gather(block, "shard", axis=0, tiled=True)

    def scatter_rows(blocks):
        blocks = with_layout_constraint(blocks, Layout((0, 1)))
        return lax.psum_scatter(blocks, "shard", scatter_dimension=0, tiled=True)

    def exchange(pairs):
        got = [pairs[0]] + [xor_send(pairs[j], "shard", evens[j]) for j in range(1, half)]
        return got, xor_send(jnp.concatenate([pair[1:] for pair in got], 0), "shard", 1)

    def by_rank(got, far):
        return jnp.concatenate([pair[:1] for pair in got] + [far], 0)

    def from_copies(block):
        return [block] + [xor_send(block, "replica", bits) for bits in range(1, copies)]

    def to_copies(pieces):
        return [pieces[0]] + [xor_send(pieces[bits], "replica", bits) for bits in range(1, copies)]

    def tie(value, *others):
        return lax.optimization_barrier((value,) + others)[0]

    vectors = (
        query_bias,
        value_bias,
        out_bias,
        proj_bias,
        gain_first,
        shift_first,
        gain_second,
        shift_second,
    )
    token_all = gather_rows(tokens)
    qkv_got, qkv_far = exchange(pack_heads(where, qkv_weight, copies, count, width))
    qkv_stack = by_rank(qkv_got, qkv_far)
    vectors = tie(jnp.concatenate(vectors), qkv_stack)
    vectors = jnp.pad(vectors[None], ((0, 15), (0, D - 8 * own_rows)))
    fc_pairs = pack_columns(where, fc_weight, out_weight, vectors, copies, count)
    fc_got = [fc_pairs[0]] + [xor_send(fc_pairs[j], "shard", evens[j]) for j in range(1, half)]
    fc_odd, out_near = split_columns(where, fc_got, span, ff_cols)
    fc_far = xor_send(fc_odd, "shard", 1)
    vectors = jnp.concatenate([got[2 * slot_rows(span) :][:1] for got in fc_got], 0)
    vectors = jnp.concatenate([vectors, xor_send(vectors, "shard", 1)], 0)
    vectors = vectors[:, : 8 * own_rows].astype(full)
    chosen = (jnp.arange(count)[:, None] ^ place == jnp.array(bits_of)[None, :]).astype(full)
    vectors = lax.dot(chosen, vectors, precision=lax.Precision.HIGHEST)
    vectors = vectors.reshape(count, 8, own_rows).transpose(1, 0, 2).reshape(8, D)
    b_query, b_value, b_out, b_proj, g_first, s_first, g_second, s_second = vectors
    qkv_stacks = from_copies(qkv_stack)
    w_qkv = assemble_rows(where, [[stack] for stack in qkv_stacks], own_rows)
    w_qkv = w_qkv.reshape(D, 3 * width)

    out_near = from_copies(tie(out_near, *qkv_stacks))
    out_far = [xor_send(block, "shard", 1) for block in out_near]
    w_out = assemble_rows(where, list(zip(out_near, out_far)), own_rows).reshape(D, D)
    fc_stack = jnp.concatenate(
        [got[:span, :ff_cols][None] for got in fc_got] + [fc_far], 0
    )
    fc_stacks = lax.all_gather(fc_stack.reshape(count * span, ff_cols), "replica")
    fc_stacks = fc_stacks.reshape(copies, count, span, ff_cols)
    w_fc = assemble_copies(where, fc_stacks, own_rows).reshape(D, ff_cols)

    def own_heads(vector):
        vector = jnp.pad(vector, (0, count * width - D))
        return lax.dynamic_slice_in_dim(vector, place * width, width, 0)

    seqs = count // CP
    starts = lax.dynamic_slice_in_dim(offsets, copy * seqs, seqs, 0)[:, :, 0] // STRETCH
    is_at = starts[:, None, :] == jnp.arange(CP)[None, :, None]
    order = jnp.sum(jnp.where(is_at, jnp.arange(CP)[None, None, :], 0), axis=2)
    order = order + CP * jnp.arange(seqs)[:, None]
    bits = order ^ place
    order = jnp.concatenate([order, bits, rank_of(bits, count)], 0).astype(jnp.int32)

    normed_low = layer_norm(token_all.astype(full), g_first, s_first).astype(low)
    projected = mm(normed_low, w_qkv, 1, 0)
    queries = (projected[:, :width] + own_heads(b_query)).astype(low)
    keys = tie(projected, fc_stack)[:, width : 2 * width].astype(low)
    values = (projected[:, 2 * width :] + own_heads(b_value)).astype(low)
    attended, log_total = attend_forward(order, queries, keys, values, heads)

    attended_own = order_heads(where, *exchange(list(attended.reshape(half, 2, STRETCH, width))))
    cot_all = gather_rows(tie(cotangent, attended_own, fc_stacks))
    attended_own = attended_own[:, :D]
    in_rows = tokens.astype(full)
    middle = in_rows + mm(attended_own, w_out, 1, 0) + b_out
    second_own = layer_norm(middle, g_second, s_second).astype(low)
    second_all = gather_rows(tie(second_own, cot_all))
    hidden = mm(second_all, w_fc, 1, 0) + fc_bias.astype(full)
    active, pull_gelu = jax.vjp(gelu_tanh, hidden)
    active_low = active.astype(low)

    (hidden_grad,) = pull_gelu(mm(cot_all, proj_weight, 1, 1))
    hidden_low = hidden_grad.astype(low)
    second_part = mm(hidden_low, w_fc, 1, 1).astype(low)
    second_grad = scatter_rows(second_part).astype(full)

    proj_full = mm(tie(active_low, second_part), cot_all, 0, 0)
    fc_full = mm(tie(second_all, second_part), hidden_low, 0, 0)
    hidden_sums = jnp.sum(hidden_low.astype(full), axis=0).reshape(copies, 1, ff_cols // copies)
    hidden_sums = jnp.pad(hidden_sums, ((0, 0), (0, 15), (0, -ff_cols // copies % 128)))
    hidden_pieces = pack_hidden(
        where, fc_full.reshape(count, own_rows, ff_cols), proj_full, hidden_sums, copies
    )
    second_grad = tie(second_grad, hidden_pieces)
    hidden_shape = hidden_pieces.shape[1:]
    hidden_sum = lax.psum_scatter(
        hidden_pieces.reshape(-1, D), "replica", scatter_dimension=0, tiled=True
    ).reshape(hidden_shape)
    grad_rows = cotangent.astype(full)
    _, pull_second = jax.vjp(layer_norm, middle, g_second, s_second)
    middle_part, gsecond_part, ssecond_part = pull_second(second_grad)
    middle_grad = grad_rows + middle_part
    branch_low = middle_grad.astype(low)
    attended_grad = mm(branch_low, w_out, 1, 1).astype(low)
    attended_pairs = split_heads(where, attended_grad, count, width)
    outw_full = mm(attended_own, tie(branch_low, attended_pairs[0]), 0, 0)
    outw_near, outw_far = split_outw(where, outw_full.reshape(count, own_rows, D), copies)
    attended_grad = by_rank(*exchange(attended_pairs)).reshape(count * STRETCH, width)
    outw_far = xor_send(outw_far, "shard", 1)
    output_low = tie(active_low, attended_grad)
    early = jnp.stack(
        [jnp.sum(branch_low.astype(full), axis=0), jnp.sum(grad_rows, axis=0), gsecond_part, ssecond_part]
    )

    query_grads, key_grads, value_grads = attend_backward(
        order, queries, keys, values, attended_grad, log_total, heads
    )
    projected_grad = jnp.concatenate([query_grads, key_grads, value_grads], 1)
    first_part = mm(projected_grad, w_qkv, 1, 1)

    def head_sums(block):
        sums = jnp.sum(block.astype(full), axis=0)
        placed = lax.dynamic_update_slice_in_dim(
            jnp.zeros((count * width,), full), sums, place * width, 0
        )
        return placed[:D]

    norms = normed(token_all.astype(full))
    sums = jnp.stack(
        [
            head_sums(query_grads),
            head_sums(value_grads),
            early[0],
            early[1],
            jnp.sum(first_part * norms, axis=0),
            jnp.sum(first_part, axis=0),
            early[2],
            early[3],
        ]
    )
    sums = sums.reshape(8, count, own_rows).transpose(1, 0, 2).reshape(count, 8 * own_rows)
    by_bits = (jnp.arange(count)[:, None] ^ place == jnp.arange(count)[None, :]).astype(full)
    sums = lax.dot(by_bits, sums, precision=lax.Precision.HIGHEST)
    share = 8 * own_rows // copies
    sums = sums.reshape(count, copies, share).transpose(1, 0, 2)
    sums = jnp.pad(sums, ((0, 0), (0, 0), (0, 16 * 64 - share))).reshape(copies, count, 16, 64)
    first_grad = scatter_rows(first_part.astype(low)).astype(full)
    qkv_full = mm(normed_low, projected_grad, 0, 0).reshape(count, own_rows, 3 * width)
    last = pack_last(where, qkv_full, outw_near, outw_far, sums)
    first_grad = tie(first_grad, last[0])
    hidden_sum = tie(hidden_sum, last[0])
    last = to_copies(last)

    fc_sums, rest = sum_hidden(where, [hidden_sum], count, ff_cols)
    hidden_stacks = from_copies(join_hidden(where, *exchange(fc_sums), rest))
    fc_grad, proj_grad, fbias = finish_hidden(
        where, hidden_stacks, count, own_rows, ff_cols, ff_cols, hidden_sums.shape[2]
    )
    fbias = fbias[:, 0, : ff_cols // copies].reshape(ff_cols)

    last = sum_last(where, last, count, 3 * width)
    last = [last[0]] + [xor_send(last[j], "shard", evens[j]) for j in range(1, half)]
    far = xor_send(odd_last(where, last, 3 * width), "shard", 1)
    last = from_copies(join_last(where, last, tie(far, hidden_stacks[1])))
    output_part = mm(output_low, proj_weight, 1, 0).astype(low)
    output = middle + b_proj + scatter_rows(output_part).astype(full)

    _, pull_first = jax.vjp(lambda rows: layer_norm(rows, g_first, s_first), in_rows)
    (input_part,) = pull_first(first_grad)
    tokens_grad = (middle_grad + input_part).astype(low)
    output = output.astype(low)
    last[0] = tie(last[0], output, tokens_grad)

    qkv_grad, outw_grad, sums = finish_last(where, last, count, own_rows, width)
    sums = sums.reshape(copies, 16 * 64)[:, :share].reshape(8, own_rows)
    qbias, vbias, obias, pbias, gfirst, sfirst, gsecond, ssecond = sums
    return (
        output,
        tokens_grad,
        qkv_grad,
        outw_grad,
        fc_grad,
        proj_grad,
        qbias,
        vbias,
        obias,
        fbias,
        pbias,
        gfirst,
        sfirst,
        gsecond,
        ssecond,
    )


def solution(mesh):
    rows = P(("replica", "shard"), None)
    matrix = P("shard", None)
    vector = P("shard")
    return jax.shard_map(
        on_device,
        mesh=mesh,
        in_specs=(rows, P()) + (matrix,) * 4 + (vector,) * 9 + (rows,),
        out_specs=(rows, rows) + (matrix,) * 4 + (vector,) * 9,
        check_vma=False,
    )
```

```python
import functools

import jax
import jax.numpy as jnp
from jax import lax
from jax.experimental import pallas as pl
from jax.experimental.pallas import tpu as pltpu
from jax.experimental.layout import Layout, with_layout_constraint
from jax.sharding import PartitionSpec as P

D = 1600
H = 25
HD = 64
CP = 8
STRETCH = 128
SEQ = CP * STRETCH
TILE = 256

norm_eps = 1e-05
masked_score = -1e30
gelu_coeff = 0.7978845608028654
low = jnp.bfloat16
full = jnp.float32


def xor_send(block, axis, bits):
    count = lax.axis_size(axis)
    return lax.ppermute(block, axis, [(i, i ^ bits) for i in range(count)])


def normed(values):
    average = jnp.mean(values, axis=-1, keepdims=True)
    centred = values - average
    variance = jnp.mean(centred * centred, axis=-1, keepdims=True)
    return centred * lax.rsqrt(variance + norm_eps)


def layer_norm(values, gain_vec, shift_vec):
    return normed(values) * gain_vec + shift_vec


def gelu_tanh(values):
    return (
        0.5 * values * (1.0 + jnp.tanh(gelu_coeff * (values + 0.044715 * values * values * values)))
    )


def mm(left_side, right_side, left_dim, right_dim):
    return lax.dot_general(
        left_side,
        right_side,
        (((left_dim,), (right_dim,)), ((), ())),
        preferred_element_type=full,
    )


def sort_blocks(order_ref, seq, source, target):
    for place in range(CP):
        start = pl.multiple_of(order_ref[seq, place] * STRETCH, STRETCH)
        target[place * STRETCH : (place + 1) * STRETCH, :] = source[pl.ds(start, STRETCH), :]


def unsort_tile(order_ref, seq, tile, value, target):
    for part in range(TILE // STRETCH):
        place = tile * (TILE // STRETCH) + part
        start = pl.multiple_of(order_ref[seq, place] * STRETCH, STRETCH)
        target[pl.ds(start, STRETCH), :] = value[part * STRETCH : (part + 1) * STRETCH, :]


def causal(scores):
    key_row = lax.broadcasted_iota(jnp.int32, scores.shape, 0)
    query_col = lax.broadcasted_iota(jnp.int32, scores.shape, 1)
    return jnp.where(key_row <= query_col, scores, masked_score)


def forward_kernel(heads, seqs, order_ref, q_ref, k_ref, v_ref, a_ref, lse_ref, qs, ks, vs, qt, vt):
    width = heads * HD
    for seq in range(seqs):
        sort_blocks(order_ref, seq, q_ref, qs)
        sort_blocks(order_ref, seq, k_ref, ks)
        sort_blocks(order_ref, seq, v_ref, vs)
        qt[...] = (qs[...].astype(full).T * HD ** (-0.5)).astype(low)
        vt[...] = vs[...].astype(full).T.astype(low)
        for tile in range(SEQ // TILE):
            cols = slice(tile * TILE, (tile + 1) * TILE)
            before = tile * TILE
            pieces = []
            for head in range(heads):
                row = lax.broadcasted_iota(jnp.int32, (width, TILE), 0)
                mine = (row >= head * HD) & (row < (head + 1) * HD)
                query = jnp.where(mine, qt[:, cols], jnp.zeros((), low))
                diag = causal(mm(ks[cols, :], query, 1, 0))
                high = jnp.max(diag, axis=0, keepdims=True)
                if tile:
                    past = mm(ks[:before, :], query, 1, 0)
                    high = jnp.maximum(high, jnp.max(past, axis=0, keepdims=True))
                    past = jnp.exp(past - high)
                diag = jnp.exp(diag - high)
                total = jnp.sum(diag, axis=0, keepdims=True)
                if tile:
                    total = total + jnp.sum(past, axis=0, keepdims=True)
                share = 1.0 / total
                own = slice(head * HD, (head + 1) * HD)
                mixed = mm(vt[own, cols], (diag * share).astype(low), 1, 0)
                if tile:
                    mixed = mixed + mm(vt[own, :before], (past * share).astype(low), 1, 0)
                pieces.append(mixed)
                lse_ref[seq, head : head + 1, cols] = high + jnp.log(total)
            mixed = jnp.concatenate(pieces, 0).T.astype(low)
            unsort_tile(order_ref, seqs + seq, tile, mixed, a_ref)


def backward_kernel(
    heads, seqs, order_ref, q_ref, k_ref, v_ref, da_ref, lse_ref,
    dq_ref, dk_ref, dv_ref, qs, ks, vs, das, qt, kt, dat, dks, dvs,
):
    width = heads * HD
    scale = HD ** (-0.5)
    for seq in range(seqs):
        sort_blocks(order_ref, seq, q_ref, qs)
        sort_blocks(order_ref, seq, k_ref, ks)
        sort_blocks(order_ref, seq, v_ref, vs)
        sort_blocks(order_ref, 2 * seqs + seq, da_ref, das)
        qt[...] = (qs[...].astype(full).T * scale).astype(low)
        kt[...] = (ks[...].astype(full).T * scale).astype(low)
        dat[...] = das[...].astype(full).T.astype(low)
        dks[...] = jnp.zeros_like(dks)
        dvs[...] = jnp.zeros_like(dvs)
        for tile in range(SEQ // TILE):
            cols = slice(tile * TILE, (tile + 1) * TILE)
            before = tile * TILE
            pieces = []
            for head in range(heads):
                own = slice(head * HD, (head + 1) * HD)
                row = lax.broadcasted_iota(jnp.int32, (width, TILE), 0)
                mine = (row >= head * HD) & (row < (head + 1) * HD)
                lane = lax.broadcasted_iota(jnp.int32, (TILE, width), 1)
                mine_lane = (lane >= head * HD) & (lane < (head + 1) * HD)
                none = jnp.zeros((), low)
                query_t = jnp.where(mine, qt[:, cols], none)
                grad_t = jnp.where(mine, dat[:, cols], none)
                query = jnp.where(mine_lane, qs[cols, :], none)
                grad = jnp.where(mine_lane, das[cols, :], none)
                log_total = lse_ref[seq, head : head + 1, cols]

                spans = [(cols, True)] + ([(slice(0, before), False)] if tile else [])
                kept = []
                dot = None
                for span, edge in spans:
                    scores = mm(ks[span, :], query_t, 1, 0)
                    if edge:
                        scores = causal(scores)
                    weights = jnp.exp(scores - log_total)
                    weight_grads = mm(vs[span, :], grad_t, 1, 0)
                    part = jnp.sum(weights * weight_grads, axis=0, keepdims=True)
                    dot = part if dot is None else dot + part
                    dvs[span, :] += mm(weights.astype(low), grad, 1, 0)
                    kept.append((span, weights, weight_grads))
                total = None
                for span, weights, weight_grads in kept:
                    score_grads = (weights * (weight_grads - dot)).astype(low)
                    dks[span, :] += mm(score_grads, query, 1, 0)
                    part = mm(kt[own, span], score_grads, 1, 0)
                    total = part if total is None else total + part
                pieces.append(total)
            unsort_tile(order_ref, seq, tile, jnp.concatenate(pieces, 0).T.astype(low), dq_ref)
        for tile in range(SEQ // TILE):
            cols = slice(tile * TILE, (tile + 1) * TILE)
            unsort_tile(order_ref, seq, tile, (dks[cols, :] * scale).astype(low), dk_ref)
            unsort_tile(order_ref, seq, tile, dvs[cols, :].astype(low), dv_ref)


vmem = pl.BlockSpec(memory_space=pltpu.VMEM)
smem = pl.BlockSpec(memory_space=pltpu.SMEM)


def attend_forward(order, queries, keys, values, heads):
    rows, width = queries.shape
    seqs = rows // SEQ
    return pl.pallas_call(
        functools.partial(forward_kernel, heads, seqs),
        out_shape=(
            jax.ShapeDtypeStruct((rows, width), low),
            jax.ShapeDtypeStruct((seqs, heads, SEQ), full),
        ),
        in_specs=[smem, vmem, vmem, vmem],
        out_specs=(vmem, vmem),
        scratch_shapes=[pltpu.VMEM((SEQ, width), low)] * 3 + [pltpu.VMEM((width, SEQ), low)] * 2,
        compiler_params=pltpu.CompilerParams(vmem_limit_bytes=40 * 2**20),
        cost_estimate=pl.CostEstimate(
            flops=seqs * heads * 2 * 2 * SEQ * SEQ * 256,
            bytes_accessed=8 * rows * width,
            transcendentals=seqs * heads * SEQ * SEQ,
        ),
        name="attend_forward",
    )(order, queries, keys, values)


def attend_backward(order, queries, keys, values, grads, log_total, heads):
    rows, width = queries.shape
    seqs = rows // SEQ
    shape = jax.ShapeDtypeStruct((rows, width), low)
    return pl.pallas_call(
        functools.partial(backward_kernel, heads, seqs),
        out_shape=(shape, shape, shape),
        in_specs=[smem, vmem, vmem, vmem, vmem, vmem],
        out_specs=(vmem, vmem, vmem),
        scratch_shapes=[pltpu.VMEM((SEQ, width), low)] * 4
        + [pltpu.VMEM((width, SEQ), low)] * 3
        + [pltpu.VMEM((SEQ, width), full)] * 2,
        compiler_params=pltpu.CompilerParams(vmem_limit_bytes=48 * 2**20),
        cost_estimate=pl.CostEstimate(
            flops=seqs * heads * 2 * 5 * SEQ * SEQ * 256,
            bytes_accessed=14 * rows * width,
            transcendentals=seqs * heads * SEQ * SEQ,
        ),
        name="attend_backward",
    )(order, queries, keys, values, grads, log_total)


def ranks(count):
    return list(range(0, count, 2)) + list(range(1, count, 2))


def rank_of(bits, count):
    return (bits & 1) * (count // 2) + (bits >> 1)


def windows(rows, copies, unit):
    step = rows // copies // unit * unit
    return step, rows - step * (copies - 1)


def local_call(kernel, shapes, scratch, name, where, *operands, after=()):
    operands = operands + tuple(after)
    many = isinstance(shapes, (list, tuple))
    size = sum(x.size * x.dtype.itemsize for x in operands)
    free = pl.BlockSpec(memory_space=pl.ANY)
    used = len(operands) - len(after)
    return pl.pallas_call(
        kernel,
        out_shape=tuple(shapes) if many else shapes,
        in_specs=[smem] + [vmem] * used + [free] * len(after),
        out_specs=tuple(vmem for _ in shapes) if many else vmem,
        scratch_shapes=scratch,
        compiler_params=pltpu.CompilerParams(vmem_limit_bytes=56 * 2**20),
        cost_estimate=pl.CostEstimate(flops=0, bytes_accessed=3 * size, transcendentals=0),
        name=name,
    )(where, *operands)


def pack_heads(where, weight, copies, count, width):
    step, span = windows(weight.shape[0], copies, 16)

    def kernel(where_ref, weight_ref, *refs):
        outs, pieces = refs[: count // 2], refs[count // 2]
        start = pl.multiple_of(where_ref[1] * step, 16)
        for other in range(count):
            low_col, high_col = other * width, min(D, (other + 1) * width)
            for third in range(3):
                have = max(0, high_col - low_col)
                at = third * width
                if have:
                    pieces[other, :, at : at + have] = weight_ref[
                        pl.ds(start, span), third * D + low_col : third * D + high_col
                    ]
                if have < width:
                    pieces[other, :, at + have : at + width] = jnp.zeros((span, width - have), low)
        for bits in range(count):
            outs[bits // 2][bits % 2] = pieces[where_ref[0] ^ bits]

    shape = jax.ShapeDtypeStruct((2, span, 3 * width), low)
    scratch = [pltpu.VMEM((count, span, 3 * width), low)]
    return local_call(kernel, [shape] * (count // 2), scratch, "pack_heads", where, weight)


def slot_rows(span):
    return -(-span // 16) * 16


def pack_columns(where, weight, out_weight, vectors, copies, count):
    step, span = windows(weight.shape[0], copies, 16)
    cols = weight.shape[1] // count
    slot = slot_rows(span)

    def kernel(where_ref, weight_ref, out_ref, vectors_ref, *refs):
        outs, pieces = refs[: count // 2], refs[count // 2]
        start = pl.multiple_of(where_ref[1] * step, 16)
        for other in range(count):
            pieces[other] = weight_ref[pl.ds(start, span), other * cols : (other + 1) * cols]
        for pair, out in enumerate(outs):
            for side in range(2):
                out[:span, side * cols : (side + 1) * cols] = pieces[
                    where_ref[0] ^ (2 * pair + side)
                ]
            out[slot : slot + span, :] = out_ref[pl.ds(start, span), :]
            out[2 * slot :, :] = vectors_ref[...]

    shape = jax.ShapeDtypeStruct((2 * slot + 16, D), low)
    scratch = [pltpu.VMEM((count, span, cols), low)]
    return local_call(
        kernel, [shape] * (count // 2), scratch, "pack_columns", where, weight, out_weight, vectors
    )


def split_columns(where, got, span, cols):
    half = len(got)
    slot = slot_rows(span)

    def kernel(where_ref, *refs):
        odd, rows = refs[half:]
        for pair in range(half):
            odd[pair] = refs[pair][:span, cols : 2 * cols]
            rows[pair] = refs[pair][slot : slot + span, :]

    shapes = [
        jax.ShapeDtypeStruct((half, span, cols), low),
        jax.ShapeDtypeStruct((half, span, D), low),
    ]
    return local_call(kernel, shapes, [], "split_columns", where, *got)


def assemble_rows(where, stacks, own_rows):
    each = len(stacks[0])
    count = sum(array.shape[0] for array in stacks[0])
    span, cols = stacks[0][0].shape[1:]
    step, _ = windows(own_rows, len(stacks), 16)
    stacks = stacks if step else stacks[:1]
    copies = len(stacks)
    arrays = [array for stack in stacks for array in stack]

    def kernel(where_ref, *refs):
        out = refs[-1]
        for bits_copy in range(copies):
            start = pl.multiple_of((where_ref[1] ^ bits_copy) * step, 16)
            blocks = [
                ref.at[row]
                for ref in refs[bits_copy * each : (bits_copy + 1) * each]
                for row in range(ref.shape[0])
            ]
            for block, bits in zip(blocks, ranks(count)):
                out[where_ref[0] ^ bits, pl.ds(start, span), :] = block[...]

    shape = jax.ShapeDtypeStruct((count, own_rows, cols), low)
    return local_call(kernel, shape, [], "assemble_rows", where, *arrays)


def assemble_copies(where, stacks, own_rows):
    copies, count, span, cols = stacks.shape
    step, _ = windows(own_rows, copies, 16)

    def kernel(where_ref, stacks_ref, out):
        for copy in range(copies if step else 1):
            for rank, bits in enumerate(ranks(count)):
                out[where_ref[0] ^ bits, copy * step : copy * step + span, :] = stacks_ref[
                    copy, rank
                ]

    shape = jax.ShapeDtypeStruct((count, own_rows, cols), low)
    return local_call(kernel, shape, [], "assemble_copies", where, stacks)


def split_heads(where, block, count, width):
    rows, cols = block.shape

    def kernel(where_ref, block_ref, *refs):
        outs, pieces = refs[: count // 2], refs[count // 2]
        for other in range(count):
            start, stop = min(cols, other * width), min(cols, (other + 1) * width)
            if start < stop:
                pieces[other, :, : stop - start] = block_ref[:, start:stop]
            if stop - start < width:
                pieces[other, :, stop - start :] = jnp.zeros((rows, width - stop + start), low)
        for bits in range(count):
            outs[bits // 2][bits % 2] = pieces[where_ref[0] ^ bits]

    shape = jax.ShapeDtypeStruct((2, rows, width), low)
    scratch = [pltpu.VMEM((count, rows, width), low)]
    return local_call(kernel, [shape] * (count // 2), scratch, "split_heads", where, block)


def order_heads(where, pairs, far):
    half = len(pairs)
    count = 2 * half
    _, rows, width = far.shape

    def kernel(where_ref, *refs):
        out, pieces = refs[-2], refs[-1]
        for pair in range(half):
            pieces[2 * pair] = refs[pair][0]
            pieces[2 * pair + 1] = refs[half][pair]
        for other in range(count):
            out[:, other * width : (other + 1) * width] = pieces[where_ref[0] ^ other]

    shape = jax.ShapeDtypeStruct((rows, count * width), low)
    scratch = [pltpu.VMEM((count, rows, width), low)]
    return local_call(kernel, shape, scratch, "order_heads", where, *pairs, far)


SLOTS = 4


def lane_of(bits, cols):
    return bits // SLOTS * cols


def own_block(ref, bits, cols, groups):
    slot, group = lax.rem(bits, SLOTS), lax.div(bits, SLOTS)
    value = ref[slot, :, :cols].astype(full)
    for index in range(1, groups):
        other = ref[slot, :, index * cols : (index + 1) * cols].astype(full)
        value = jnp.where(group == index, other, value)
    return value


def pack_hidden(where, fc_full, proj_full, sums, copies):
    count, rows, cols = fc_full.shape
    step, span = windows(rows, copies, 16)
    proj_step, proj_span = windows(proj_full.shape[0], copies, 8)
    extra = -(-(proj_span + 16) // span)
    after = slot_rows(proj_span) - (extra - 1) * span

    def kernel(where_ref, fc_ref, proj_ref, sums_ref, out_ref):
        for copy in range(copies):
            out = out_ref.at[copy]
            for bits in range(count):
                lane = lane_of(bits, cols)
                out[bits % SLOTS, :, lane : lane + cols] = fc_ref[
                    where_ref[0] ^ bits, copy * step : copy * step + span, :
                ].astype(low)
            for slot in range(extra):
                length = min(span, proj_span - slot * span)
                if length > 0:
                    at = copy * proj_step + slot * span
                    out[SLOTS + slot, :length, :] = proj_ref[at : at + length, :].astype(low)
            out[SLOTS + extra - 1, after : after + 16, : sums.shape[2]] = sums_ref[copy].astype(low)

    shape = jax.ShapeDtypeStruct((copies, SLOTS + extra, span, D), low)
    return local_call(kernel, shape, [], "pack_hidden", where, fc_full, proj_full, sums)


def sum_hidden(where, pieces, count, cols):
    number = len(pieces)
    slots, span, _ = pieces[0].shape

    def kernel(where_ref, *refs):
        outs, rest = refs[number:-1], refs[-1]
        for slot in range(slots):
            total = refs[0][slot].astype(full)
            for piece in refs[1:number]:
                total = total + piece[slot].astype(full)
            total = total.astype(low)
            if slot >= SLOTS:
                rest[slot - SLOTS] = total
                continue
            for bits in range(slot, count, SLOTS):
                lane = lane_of(bits, cols)
                outs[bits // 2][bits % 2] = total[:, lane : lane + cols]

    shapes = [jax.ShapeDtypeStruct((2, span, cols), low)] * (count // 2)
    shapes.append(jax.ShapeDtypeStruct((slots - SLOTS, span, D), low))
    outs = local_call(kernel, shapes, [], "sum_hidden", where, *pieces)
    return outs[:-1], outs[-1]


def join_hidden(where, got, far, rest):
    half = len(got)
    _, span, cols = far.shape

    def kernel(where_ref, *refs):
        out = refs[-1]
        for bits in range(2 * half):
            block = refs[half][bits // 2] if bits % 2 else refs[bits // 2][0]
            lane = lane_of(bits, cols)
            out[bits % SLOTS, :, lane : lane + cols] = block
        for slot in range(rest.shape[0]):
            out[SLOTS + slot] = refs[half + 1][slot]

    shape = jax.ShapeDtypeStruct((SLOTS + rest.shape[0], span, D), low)
    return local_call(kernel, shape, [], "join_hidden", where, *got, far, rest)


def finish_hidden(where, stacks, count, rows, cols, proj_rows, lanes):
    copies = len(stacks)
    slots, span, _ = stacks[0].shape
    step, _ = windows(rows, copies, 16)
    proj_step, proj_span = windows(proj_rows, copies, 8)
    extra = slots - SLOTS
    after = slot_rows(proj_span) - (extra - 1) * span

    def kernel(where_ref, *refs):
        fc_out, proj_out, sums_out = refs[copies:]
        for index in range(copies):
            piece, copy = refs[index], where_ref[1] ^ index
            start = pl.multiple_of(copy * step, 16)
            if step or index == 0:
                for other in range(count):
                    fc_out[pl.ds(start, span), other * cols : (other + 1) * cols] = own_block(
                        piece, where_ref[0] ^ other, cols, count // SLOTS
                    )
            for slot in range(extra):
                length = min(span, proj_span - slot * span)
                if length > 0:
                    at = copy * proj_step
                    at = pl.multiple_of(at + slot * span, 8) if span % 8 == 0 else at
                    proj_out[pl.ds(at, length), :] = piece[SLOTS + slot, :length, :].astype(full)
            sums_out[copy] = piece[SLOTS + extra - 1, after : after + 16, :lanes].astype(full)

    shapes = [
        jax.ShapeDtypeStruct((rows, count * cols), full),
        jax.ShapeDtypeStruct((proj_rows, D), full),
        jax.ShapeDtypeStruct((copies, 16, lanes), full),
    ]
    return local_call(kernel, shapes, [], "finish_hidden", where, *stacks)


def split_outw(where, grad, copies):
    count, rows, cols = grad.shape
    half = count // 2
    step, span = windows(rows, copies, 16)
    parts = copies if step else 1

    def kernel(where_ref, grad_ref, *refs):
        far = refs[parts]
        for index in range(parts):
            start = pl.multiple_of((where_ref[1] ^ index) * step, 16)
            for pair in range(half):
                for side, out in enumerate((refs[index], far.at[index])):
                    out[pair] = grad_ref[
                        where_ref[0] ^ (2 * pair + side), pl.ds(start, span), :
                    ].astype(low)

    shapes = [jax.ShapeDtypeStruct((half, span, cols), low)] * parts
    shapes.append(jax.ShapeDtypeStruct((parts, half, span, cols), low))
    outs = local_call(kernel, shapes, [], "split_outw", where, grad)
    return outs[:-1], outs[-1]


def pack_last(where, qkv_full, near, far, sums):
    copies, parts = sums.shape[0], len(near)
    count, rows, cols = qkv_full.shape
    half = count // 2
    step, span = windows(rows, copies, 16)
    spare = count // SLOTS * cols

    def kernel(where_ref, qkv_ref, *refs):
        far_ref, sums_ref = refs[parts], refs[parts + 1]
        for index, out in enumerate(refs[parts + 2 :]):
            copy = where_ref[1] ^ index
            start = pl.multiple_of(copy * step, 16)
            for bits in range(count):
                lane = lane_of(bits, cols)
                out[bits % SLOTS, :, lane : lane + cols] = qkv_ref[
                    where_ref[0] ^ bits, pl.ds(start, span), :
                ].astype(low)
                row = bits // SLOTS * 16
                out[bits % SLOTS, row : row + 16, spare : spare + 64] = sums_ref[copy, bits].astype(
                    low
                )
            for pair in range(half):
                total = refs[index % parts][pair].astype(full)
                total = total + far_ref[index % parts, pair].astype(full)
                out[SLOTS + pair] = total.astype(low)

    shape = jax.ShapeDtypeStruct((SLOTS + half, span, D), low)
    return local_call(kernel, [shape] * copies, [], "pack_last", where, qkv_full, *near, far, sums)


def sum_last(where, pieces, count, cols):
    number = len(pieces)
    half = count // 2
    span = pieces[0].shape[1]
    spare = count // SLOTS * cols

    def kernel(where_ref, *refs):
        outs = refs[number:]
        for slot in range(SLOTS + half):
            total = refs[0][slot].astype(full)
            for piece in refs[1:number]:
                total = total + piece[slot].astype(full)
            total = total.astype(low)
            if slot >= SLOTS:
                outs[slot - SLOTS][1] = total
                continue
            for bits in range(slot, count, SLOTS):
                lane, row, side = lane_of(bits, cols), bits // SLOTS * 16, bits % 2
                out = outs[bits // 2]
                out[0, :, side * cols : (side + 1) * cols] = total[:, lane : lane + cols]
                out[0, side * 16 : side * 16 + 16, 2 * cols : 2 * cols + 64] = total[
                    row : row + 16, spare : spare + 64
                ]

    shape = jax.ShapeDtypeStruct((2, span, D), low)
    return local_call(kernel, [shape] * half, [], "sum_last", where, *pieces)


def odd_last(where, got, cols):
    half = len(got)
    span = got[0].shape[1]

    def kernel(where_ref, *refs):
        out = refs[half]
        for pair in range(half):
            out[pair, :, :cols] = refs[pair][0, :, cols : 2 * cols]
            out[pair, :16, cols : cols + 64] = refs[pair][0, 16:32, 2 * cols : 2 * cols + 64]

    shape = jax.ShapeDtypeStruct((half, span, cols + 64), low)
    return local_call(kernel, shape, [], "odd_last", where, *got)


def join_last(where, got, far):
    half = len(got)
    _, span, wide = far.shape
    cols = wide - 64
    spare = 2 * half // SLOTS * cols

    def kernel(where_ref, *refs):
        far_ref, out = refs[half], refs[half + 1]
        sums = jnp.zeros((16, 64), full)
        total = jnp.zeros((span, D), full)
        for pair in range(half):
            for side in range(2):
                lane = lane_of(2 * pair + side, cols)
                block = far_ref[pair, :, :cols] if side else refs[pair][0, :, :cols]
                out[(2 * pair + side) % SLOTS, :, lane : lane + cols] = block
            sums = sums + refs[pair][0, :16, 2 * cols : 2 * cols + 64].astype(full)
            sums = sums + far_ref[pair, :16, cols : cols + 64].astype(full)
            total = total + refs[pair][1].astype(full)
        out[SLOTS] = total.astype(low)
        out[0, :16, spare : spare + 64] = sums.astype(low)

    shape = jax.ShapeDtypeStruct((SLOTS + 1, span, D), low)
    return local_call(kernel, shape, [], "join_last", where, *got, far)


def finish_last(where, stacks, count, rows, width):
    copies = len(stacks)
    span = stacks[0].shape[1]
    step, _ = windows(rows, copies, 16)
    cols = 3 * width
    spare = count // SLOTS * cols

    def kernel(where_ref, *refs):
        qkv_out, outw_out, sums_out = refs[copies:]
        for index in range(copies):
            piece, copy = refs[index], where_ref[1] ^ index
            start = pl.multiple_of(copy * step, 16)
            sums_out[copy] = piece[0, :16, spare : spare + 64].astype(full)
            if index and not step:
                continue
            outw_out[pl.ds(start, span), :] = piece[SLOTS].astype(full)
            for other in range(count):
                have = min(width, D - other * width)
                if have <= 0:
                    continue
                block = own_block(piece, where_ref[0] ^ other, cols, count // SLOTS)
                for third in range(3):
                    target = third * D + other * width
                    qkv_out[pl.ds(start, span), target : target + have] = block[
                        :, third * width : third * width + have
                    ]

    shapes = [
        jax.ShapeDtypeStruct((rows, 3 * D), full),
        jax.ShapeDtypeStruct((rows, D), full),
        jax.ShapeDtypeStruct((copies, 16, 64), full),
    ]
    return local_call(kernel, shapes, [], "finish_last", where, *stacks)


def on_device(
    tokens,
    offsets,
    qkv_weight,
    out_weight,
    fc_weight,
    proj_weight,
    query_bias,
    value_bias,
    out_bias,
    fc_bias,
    proj_bias,
    gain_first,
    shift_first,
    gain_second,
    shift_second,
    cotangent,
):
    count = lax.axis_size("shard")
    copies = lax.axis_size("replica")
    place = lax.axis_index("shard")
    copy = lax.axis_index("replica")
    where = jnp.stack([place, copy]).astype(jnp.int32)
    evens = list(range(0, count, 2))
    bits_of = ranks(count)
    half = count // 2
    heads = -(-H // count)
    span = windows(D // count, copies, 16)[1]
    width = heads * HD
    own_rows = D // count
    ff_cols = fc_weight.shape[1] // count

    def gather_rows(block):
        return lax.all_gather(block, "shard", axis=0, tiled=True)

    def scatter_rows(blocks):
        blocks = with_layout_constraint(blocks, Layout((0, 1)))
        return lax.psum_scatter(blocks, "shard", scatter_dimension=0, tiled=True)

    def exchange(pairs):
        got = [pairs[0]] + [xor_send(pairs[j], "shard", evens[j]) for j in range(1, half)]
        return got, xor_send(jnp.concatenate([pair[1:] for pair in got], 0), "shard", 1)

    def by_rank(got, far):
        return jnp.concatenate([pair[:1] for pair in got] + [far], 0)

    def from_copies(block):
        return [block] + [xor_send(block, "replica", bits) for bits in range(1, copies)]

    def to_copies(pieces):
        return [pieces[0]] + [xor_send(pieces[bits], "replica", bits) for bits in range(1, copies)]

    def tie(value, *others):
        return lax.optimization_barrier((value,) + others)[0]

    vectors = (
        query_bias,
        value_bias,
        out_bias,
        proj_bias,
        gain_first,
        shift_first,
        gain_second,
        shift_second,
    )
    token_all = gather_rows(tokens)
    qkv_got, qkv_far = exchange(pack_heads(where, qkv_weight, copies, count, width))
    qkv_stack = by_rank(qkv_got, qkv_far)
    vectors = tie(jnp.concatenate(vectors), qkv_stack)
    vectors = jnp.pad(vectors[None], ((0, 15), (0, D - 8 * own_rows)))
    fc_pairs = pack_columns(where, fc_weight, out_weight, vectors, copies, count)
    fc_got = [fc_pairs[0]] + [xor_send(fc_pairs[j], "shard", evens[j]) for j in range(1, half)]
    fc_odd, out_near = split_columns(where, fc_got, span, ff_cols)
    fc_far = xor_send(fc_odd, "shard", 1)
    vectors = jnp.concatenate([got[2 * slot_rows(span) :][:1] for got in fc_got], 0)
    vectors = jnp.concatenate([vectors, xor_send(vectors, "shard", 1)], 0)
    vectors = vectors[:, : 8 * own_rows].astype(full)
    chosen = (jnp.arange(count)[:, None] ^ place == jnp.array(bits_of)[None, :]).astype(full)
    vectors = lax.dot(chosen, vectors, precision=lax.Precision.HIGHEST)
    vectors = vectors.reshape(count, 8, own_rows).transpose(1, 0, 2).reshape(8, D)
    b_query, b_value, b_out, b_proj, g_first, s_first, g_second, s_second = vectors
    qkv_stacks = lax.all_gather(qkv_stack.reshape(count * span, 3 * width), "replica")
    qkv_stacks = qkv_stacks.reshape(copies, count, span, 3 * width)
    w_qkv = assemble_copies(where, qkv_stacks, own_rows)
    w_qkv = w_qkv.reshape(D, 3 * width)

    out_near = from_copies(out_near)
    out_far = [xor_send(block, "shard", 1) for block in out_near]
    w_out = assemble_rows(where, list(zip(out_near, out_far)), own_rows).reshape(D, D)
    fc_stack = jnp.concatenate(
        [got[:span, :ff_cols][None] for got in fc_got] + [fc_far], 0
    )
    fc_stacks = lax.all_gather(fc_stack.reshape(count * span, ff_cols), "replica")
    fc_stacks = fc_stacks.reshape(copies, count, span, ff_cols)
    w_fc = assemble_copies(where, fc_stacks, own_rows).reshape(D, ff_cols)

    def own_heads(vector):
        vector = jnp.pad(vector, (0, count * width - D))
        return lax.dynamic_slice_in_dim(vector, place * width, width, 0)

    seqs = count // CP
    starts = lax.dynamic_slice_in_dim(offsets, copy * seqs, seqs, 0)[:, :, 0] // STRETCH
    is_at = starts[:, None, :] == jnp.arange(CP)[None, :, None]
    order = jnp.sum(jnp.where(is_at, jnp.arange(CP)[None, None, :], 0), axis=2)
    order = order + CP * jnp.arange(seqs)[:, None]
    bits = order ^ place
    order = jnp.concatenate([order, bits, rank_of(bits, count)], 0).astype(jnp.int32)

    normed_low = layer_norm(token_all.astype(full), g_first, s_first).astype(low)
    projected = mm(normed_low, w_qkv, 1, 0)
    queries = (projected[:, :width] + own_heads(b_query)).astype(low)
    keys = tie(projected, fc_stack)[:, width : 2 * width].astype(low)
    values = (projected[:, 2 * width :] + own_heads(b_value)).astype(low)
    attended, log_total = attend_forward(order, queries, keys, values, heads)

    attended = tie(attended, *out_near)
    attended_own = order_heads(where, *exchange(list(attended.reshape(half, 2, STRETCH, width))))
    cot_all = gather_rows(tie(cotangent, attended_own, fc_stacks))
    attended_own = attended_own[:, :D]
    in_rows = tokens.astype(full)
    middle = in_rows + mm(attended_own, w_out, 1, 0) + b_out
    second_own = layer_norm(middle, g_second, s_second).astype(low)
    second_all = gather_rows(tie(second_own, cot_all))
    hidden = mm(second_all, w_fc, 1, 0) + fc_bias.astype(full)
    active, pull_gelu = jax.vjp(gelu_tanh, hidden)
    active_low = active.astype(low)

    (hidden_grad,) = pull_gelu(mm(cot_all, proj_weight, 1, 1))
    hidden_low = hidden_grad.astype(low)
    second_part = mm(hidden_low, w_fc, 1, 1).astype(low)
    second_grad = scatter_rows(second_part).astype(full)

    proj_full = mm(tie(active_low, second_part), cot_all, 0, 0)
    fc_full = mm(tie(second_all, second_part), hidden_low, 0, 0)
    hidden_sums = jnp.sum(hidden_low.astype(full), axis=0).reshape(copies, 1, ff_cols // copies)
    hidden_sums = jnp.pad(hidden_sums, ((0, 0), (0, 15), (0, -ff_cols // copies % 128)))
    hidden_pieces = pack_hidden(
        where, fc_full.reshape(count, own_rows, ff_cols), proj_full, hidden_sums, copies
    )
    second_grad = tie(second_grad, hidden_pieces)
    hidden_shape = hidden_pieces.shape[1:]
    hidden_sum = lax.psum_scatter(
        hidden_pieces.reshape(-1, D), "replica", scatter_dimension=0, tiled=True
    ).reshape(hidden_shape)
    grad_rows = cotangent.astype(full)
    _, pull_second = jax.vjp(layer_norm, middle, g_second, s_second)
    middle_part, gsecond_part, ssecond_part = pull_second(second_grad)
    middle_grad = grad_rows + middle_part
    branch_low = middle_grad.astype(low)
    attended_grad = mm(branch_low, w_out, 1, 1).astype(low)
    attended_pairs = split_heads(where, attended_grad, count, width)
    outw_full = mm(attended_own, tie(branch_low, attended_pairs[0]), 0, 0)
    outw_near, outw_far = split_outw(where, outw_full.reshape(count, own_rows, D), copies)
    attended_grad = by_rank(*exchange(attended_pairs)).reshape(count * STRETCH, width)
    outw_far = xor_send(outw_far, "shard", 1)
    early = jnp.stack(
        [jnp.sum(branch_low.astype(full), axis=0), jnp.sum(grad_rows, axis=0), gsecond_part, ssecond_part]
    )

    query_grads, key_grads, value_grads = attend_backward(
        order, queries, keys, values, attended_grad, log_total, heads
    )
    projected_grad = jnp.concatenate([query_grads, key_grads, value_grads], 1)
    first_part = mm(projected_grad, w_qkv, 1, 1)

    def head_sums(block):
        sums = jnp.sum(block.astype(full), axis=0)
        placed = lax.dynamic_update_slice_in_dim(
            jnp.zeros((count * width,), full), sums, place * width, 0
        )
        return placed[:D]

    norms = normed(token_all.astype(full))
    sums = jnp.stack(
        [
            head_sums(query_grads),
            head_sums(value_grads),
            early[0],
            early[1],
            jnp.sum(first_part * norms, axis=0),
            jnp.sum(first_part, axis=0),
            early[2],
            early[3],
        ]
    )
    sums = sums.reshape(8, count, own_rows).transpose(1, 0, 2).reshape(count, 8 * own_rows)
    by_bits = (jnp.arange(count)[:, None] ^ place == jnp.arange(count)[None, :]).astype(full)
    sums = lax.dot(by_bits, sums, precision=lax.Precision.HIGHEST)
    share = 8 * own_rows // copies
    sums = sums.reshape(count, copies, share).transpose(1, 0, 2)
    sums = jnp.pad(sums, ((0, 0), (0, 0), (0, 16 * 64 - share))).reshape(copies, count, 16, 64)
    first_grad = scatter_rows(first_part.astype(low)).astype(full)
    qkv_full = mm(normed_low, projected_grad, 0, 0).reshape(count, own_rows, 3 * width)
    last = pack_last(where, qkv_full, outw_near, outw_far, sums)
    first_grad = tie(first_grad, last[0])
    hidden_sum = tie(hidden_sum, last[0])
    last = to_copies(last)

    fc_sums, rest = sum_hidden(where, [hidden_sum], count, ff_cols)
    hidden_stacks = from_copies(join_hidden(where, *exchange(fc_sums), rest))
    fc_grad, proj_grad, fbias = finish_hidden(
        where, hidden_stacks, count, own_rows, ff_cols, ff_cols, hidden_sums.shape[2]
    )
    fbias = fbias[:, 0, : ff_cols // copies].reshape(ff_cols)

    last = sum_last(where, last, count, 3 * width)
    last = [last[0]] + [xor_send(last[j], "shard", evens[j]) for j in range(1, half)]
    far = xor_send(odd_last(where, last, 3 * width), "shard", 1)
    last = from_copies(join_last(where, last, tie(far, hidden_stacks[1])))
    output_part = mm(tie(active_low, fc_sums[0]), proj_weight, 1, 0).astype(low)
    output = middle + b_proj + scatter_rows(output_part).astype(full)

    _, pull_first = jax.vjp(lambda rows: layer_norm(rows, g_first, s_first), in_rows)
    (input_part,) = pull_first(first_grad)
    tokens_grad = (middle_grad + input_part).astype(low)
    output = output.astype(low)
    last[0] = tie(last[0], output, tokens_grad)

    qkv_grad, outw_grad, sums = finish_last(where, last, count, own_rows, width)
    sums = sums.reshape(copies, 16 * 64)[:, :share].reshape(8, own_rows)
    qbias, vbias, obias, pbias, gfirst, sfirst, gsecond, ssecond = sums
    return (
        output,
        tokens_grad,
        qkv_grad,
        outw_grad,
        fc_grad,
        proj_grad,
        qbias,
        vbias,
        obias,
        fbias,
        pbias,
        gfirst,
        sfirst,
        gsecond,
        ssecond,
    )


def solution(mesh):
    rows = P(("replica", "shard"), None)
    matrix = P("shard", None)
    vector = P("shard")
    return jax.shard_map(
        on_device,
        mesh=mesh,
        in_specs=(rows, P()) + (matrix,) * 4 + (vector,) * 9 + (rows,),
        out_specs=(rows, rows) + (matrix,) * 4 + (vector,) * 9,
        check_vma=False,
    )
```

```python
import functools

import jax
import jax.numpy as jnp
from jax import lax
from jax.experimental import pallas as pl
from jax.experimental.pallas import tpu as pltpu
from jax.experimental.layout import Layout, with_layout_constraint
from jax.sharding import PartitionSpec as P

D = 1600
H = 25
HD = 64
CP = 8
STRETCH = 128
SEQ = CP * STRETCH
TILE = 256

norm_eps = 1e-05
masked_score = -1e30
gelu_coeff = 0.7978845608028654
low = jnp.bfloat16
full = jnp.float32


def xor_send(block, axis, bits):
    count = lax.axis_size(axis)
    return lax.ppermute(block, axis, [(i, i ^ bits) for i in range(count)])


def normed(values):
    average = jnp.mean(values, axis=-1, keepdims=True)
    centred = values - average
    variance = jnp.mean(centred * centred, axis=-1, keepdims=True)
    return centred * lax.rsqrt(variance + norm_eps)


def layer_norm(values, gain_vec, shift_vec):
    return normed(values) * gain_vec + shift_vec


def gelu_tanh(values):
    return (
        0.5 * values * (1.0 + jnp.tanh(gelu_coeff * (values + 0.044715 * values * values * values)))
    )


def mm(left_side, right_side, left_dim, right_dim):
    return lax.dot_general(
        left_side,
        right_side,
        (((left_dim,), (right_dim,)), ((), ())),
        preferred_element_type=full,
    )


def sort_blocks(order_ref, seq, source, target):
    for place in range(CP):
        start = pl.multiple_of(order_ref[seq, place] * STRETCH, STRETCH)
        target[place * STRETCH : (place + 1) * STRETCH, :] = source[pl.ds(start, STRETCH), :]


def unsort_tile(order_ref, seq, tile, value, target):
    for part in range(TILE // STRETCH):
        place = tile * (TILE // STRETCH) + part
        start = pl.multiple_of(order_ref[seq, place] * STRETCH, STRETCH)
        target[pl.ds(start, STRETCH), :] = value[part * STRETCH : (part + 1) * STRETCH, :]


def causal(scores):
    key_row = lax.broadcasted_iota(jnp.int32, scores.shape, 0)
    query_col = lax.broadcasted_iota(jnp.int32, scores.shape, 1)
    return jnp.where(key_row <= query_col, scores, masked_score)


def forward_kernel(heads, seqs, order_ref, q_ref, k_ref, v_ref, a_ref, lse_ref, qs, ks, vs, qt, vt):
    width = heads * HD
    for seq in range(seqs):
        sort_blocks(order_ref, seq, q_ref, qs)
        sort_blocks(order_ref, seq, k_ref, ks)
        sort_blocks(order_ref, seq, v_ref, vs)
        qt[...] = (qs[...].astype(full).T * HD ** (-0.5)).astype(low)
        vt[...] = vs[...].astype(full).T.astype(low)
        for tile in range(SEQ // TILE):
            cols = slice(tile * TILE, (tile + 1) * TILE)
            before = tile * TILE
            pieces = []
            for head in range(heads):
                row = lax.broadcasted_iota(jnp.int32, (width, TILE), 0)
                mine = (row >= head * HD) & (row < (head + 1) * HD)
                query = jnp.where(mine, qt[:, cols], jnp.zeros((), low))
                diag = causal(mm(ks[cols, :], query, 1, 0))
                high = jnp.max(diag, axis=0, keepdims=True)
                if tile:
                    past = mm(ks[:before, :], query, 1, 0)
                    high = jnp.maximum(high, jnp.max(past, axis=0, keepdims=True))
                    past = jnp.exp(past - high)
                diag = jnp.exp(diag - high)
                total = jnp.sum(diag, axis=0, keepdims=True)
                if tile:
                    total = total + jnp.sum(past, axis=0, keepdims=True)
                share = 1.0 / total
                own = slice(head * HD, (head + 1) * HD)
                mixed = mm(vt[own, cols], (diag * share).astype(low), 1, 0)
                if tile:
                    mixed = mixed + mm(vt[own, :before], (past * share).astype(low), 1, 0)
                pieces.append(mixed)
                lse_ref[seq, head : head + 1, cols] = high + jnp.log(total)
            mixed = jnp.concatenate(pieces, 0).T.astype(low)
            unsort_tile(order_ref, seqs + seq, tile, mixed, a_ref)


def backward_kernel(
    heads, seqs, order_ref, q_ref, k_ref, v_ref, da_ref, lse_ref,
    dq_ref, dk_ref, dv_ref, qs, ks, vs, das, qt, kt, dat, dks, dvs,
):
    width = heads * HD
    scale = HD ** (-0.5)
    for seq in range(seqs):
        sort_blocks(order_ref, seq, q_ref, qs)
        sort_blocks(order_ref, seq, k_ref, ks)
        sort_blocks(order_ref, seq, v_ref, vs)
        sort_blocks(order_ref, 2 * seqs + seq, da_ref, das)
        qt[...] = (qs[...].astype(full).T * scale).astype(low)
        kt[...] = (ks[...].astype(full).T * scale).astype(low)
        dat[...] = das[...].astype(full).T.astype(low)
        dks[...] = jnp.zeros_like(dks)
        dvs[...] = jnp.zeros_like(dvs)
        for tile in range(SEQ // TILE):
            cols = slice(tile * TILE, (tile + 1) * TILE)
            before = tile * TILE
            pieces = []
            for head in range(heads):
                own = slice(head * HD, (head + 1) * HD)
                row = lax.broadcasted_iota(jnp.int32, (width, TILE), 0)
                mine = (row >= head * HD) & (row < (head + 1) * HD)
                lane = lax.broadcasted_iota(jnp.int32, (TILE, width), 1)
                mine_lane = (lane >= head * HD) & (lane < (head + 1) * HD)
                none = jnp.zeros((), low)
                query_t = jnp.where(mine, qt[:, cols], none)
                grad_t = jnp.where(mine, dat[:, cols], none)
                query = jnp.where(mine_lane, qs[cols, :], none)
                grad = jnp.where(mine_lane, das[cols, :], none)
                log_total = lse_ref[seq, head : head + 1, cols]

                spans = [(cols, True)] + ([(slice(0, before), False)] if tile else [])
                kept = []
                dot = None
                for span, edge in spans:
                    scores = mm(ks[span, :], query_t, 1, 0)
                    if edge:
                        scores = causal(scores)
                    weights = jnp.exp(scores - log_total)
                    weight_grads = mm(vs[span, :], grad_t, 1, 0)
                    part = jnp.sum(weights * weight_grads, axis=0, keepdims=True)
                    dot = part if dot is None else dot + part
                    dvs[span, :] += mm(weights.astype(low), grad, 1, 0)
                    kept.append((span, weights, weight_grads))
                total = None
                for span, weights, weight_grads in kept:
                    score_grads = (weights * (weight_grads - dot)).astype(low)
                    dks[span, :] += mm(score_grads, query, 1, 0)
                    part = mm(kt[own, span], score_grads, 1, 0)
                    total = part if total is None else total + part
                pieces.append(total)
            unsort_tile(order_ref, seq, tile, jnp.concatenate(pieces, 0).T.astype(low), dq_ref)
        for tile in range(SEQ // TILE):
            cols = slice(tile * TILE, (tile + 1) * TILE)
            unsort_tile(order_ref, seq, tile, (dks[cols, :] * scale).astype(low), dk_ref)
            unsort_tile(order_ref, seq, tile, dvs[cols, :].astype(low), dv_ref)


vmem = pl.BlockSpec(memory_space=pltpu.VMEM)
smem = pl.BlockSpec(memory_space=pltpu.SMEM)


def attend_forward(order, queries, keys, values, heads):
    rows, width = queries.shape
    seqs = rows // SEQ
    return pl.pallas_call(
        functools.partial(forward_kernel, heads, seqs),
        out_shape=(
            jax.ShapeDtypeStruct((rows, width), low),
            jax.ShapeDtypeStruct((seqs, heads, SEQ), full),
        ),
        in_specs=[smem, vmem, vmem, vmem],
        out_specs=(vmem, vmem),
        scratch_shapes=[pltpu.VMEM((SEQ, width), low)] * 3 + [pltpu.VMEM((width, SEQ), low)] * 2,
        compiler_params=pltpu.CompilerParams(vmem_limit_bytes=40 * 2**20),
        cost_estimate=pl.CostEstimate(
            flops=seqs * heads * 2 * 2 * SEQ * SEQ * 256,
            bytes_accessed=8 * rows * width,
            transcendentals=seqs * heads * SEQ * SEQ,
        ),
        name="attend_forward",
    )(order, queries, keys, values)


def attend_backward(order, queries, keys, values, grads, log_total, heads):
    rows, width = queries.shape
    seqs = rows // SEQ
    shape = jax.ShapeDtypeStruct((rows, width), low)
    return pl.pallas_call(
        functools.partial(backward_kernel, heads, seqs),
        out_shape=(shape, shape, shape),
        in_specs=[smem, vmem, vmem, vmem, vmem, vmem],
        out_specs=(vmem, vmem, vmem),
        scratch_shapes=[pltpu.VMEM((SEQ, width), low)] * 4
        + [pltpu.VMEM((width, SEQ), low)] * 3
        + [pltpu.VMEM((SEQ, width), full)] * 2,
        compiler_params=pltpu.CompilerParams(vmem_limit_bytes=48 * 2**20),
        cost_estimate=pl.CostEstimate(
            flops=seqs * heads * 2 * 5 * SEQ * SEQ * 256,
            bytes_accessed=14 * rows * width,
            transcendentals=seqs * heads * SEQ * SEQ,
        ),
        name="attend_backward",
    )(order, queries, keys, values, grads, log_total)


def ranks(count):
    return list(range(0, count, 2)) + list(range(1, count, 2))


def rank_of(bits, count):
    return (bits & 1) * (count // 2) + (bits >> 1)


def windows(rows, copies, unit):
    step = rows // copies // unit * unit
    return step, rows - step * (copies - 1)


def local_call(kernel, shapes, scratch, name, where, *operands, after=()):
    operands = operands + tuple(after)
    many = isinstance(shapes, (list, tuple))
    size = sum(x.size * x.dtype.itemsize for x in operands)
    free = pl.BlockSpec(memory_space=pl.ANY)
    used = len(operands) - len(after)
    return pl.pallas_call(
        kernel,
        out_shape=tuple(shapes) if many else shapes,
        in_specs=[smem] + [vmem] * used + [free] * len(after),
        out_specs=tuple(vmem for _ in shapes) if many else vmem,
        scratch_shapes=scratch,
        compiler_params=pltpu.CompilerParams(vmem_limit_bytes=56 * 2**20),
        cost_estimate=pl.CostEstimate(flops=0, bytes_accessed=3 * size, transcendentals=0),
        name=name,
    )(where, *operands)


def pack_heads(where, weight, copies, count, width):
    step, span = windows(weight.shape[0], copies, 16)

    def kernel(where_ref, weight_ref, *refs):
        outs, pieces = refs[: count // 2], refs[count // 2]
        start = pl.multiple_of(where_ref[1] * step, 16)
        for other in range(count):
            low_col, high_col = other * width, min(D, (other + 1) * width)
            for third in range(3):
                have = max(0, high_col - low_col)
                at = third * width
                if have:
                    pieces[other, :, at : at + have] = weight_ref[
                        pl.ds(start, span), third * D + low_col : third * D + high_col
                    ]
                if have < width:
                    pieces[other, :, at + have : at + width] = jnp.zeros((span, width - have), low)
        for bits in range(count):
            outs[bits // 2][bits % 2] = pieces[where_ref[0] ^ bits]

    shape = jax.ShapeDtypeStruct((2, span, 3 * width), low)
    scratch = [pltpu.VMEM((count, span, 3 * width), low)]
    return local_call(kernel, [shape] * (count // 2), scratch, "pack_heads", where, weight)


def slot_rows(span):
    return -(-span // 8) * 8


def pack_columns(where, weight, out_weight, vectors, copies, count):
    step, span = windows(weight.shape[0], copies, 16)
    cols = weight.shape[1] // count
    slot = slot_rows(span)

    def kernel(where_ref, weight_ref, out_ref, vectors_ref, *refs):
        outs, pieces = refs[: count // 2], refs[count // 2]
        start = pl.multiple_of(where_ref[1] * step, 16)
        for other in range(count):
            pieces[other] = weight_ref[pl.ds(start, span), other * cols : (other + 1) * cols]
        for pair, out in enumerate(outs):
            for side in range(2):
                out[:span, side * cols : (side + 1) * cols] = pieces[
                    where_ref[0] ^ (2 * pair + side)
                ]
            out[slot : slot + span, :] = out_ref[pl.ds(start, span), :]
            out[2 * slot :, :] = vectors_ref[...]

    shape = jax.ShapeDtypeStruct((2 * slot + 8, D), low)
    scratch = [pltpu.VMEM((count, span, cols), low)]
    return local_call(
        kernel, [shape] * (count // 2), scratch, "pack_columns", where, weight, out_weight, vectors
    )


def split_columns(where, got, span, cols):
    half = len(got)
    slot = slot_rows(span)

    def kernel(where_ref, *refs):
        odd, rows = refs[half:]
        for pair in range(half):
            odd[pair] = refs[pair][:span, cols : 2 * cols]
            rows[pair] = refs[pair][slot : slot + span, :]

    shapes = [
        jax.ShapeDtypeStruct((half, span, cols), low),
        jax.ShapeDtypeStruct((half, span, D), low),
    ]
    return local_call(kernel, shapes, [], "split_columns", where, *got)


def assemble_rows(where, stacks, own_rows):
    each = len(stacks[0])
    count = sum(array.shape[0] for array in stacks[0])
    span, cols = stacks[0][0].shape[1:]
    step, _ = windows(own_rows, len(stacks), 16)
    stacks = stacks if step else stacks[:1]
    copies = len(stacks)
    arrays = [array for stack in stacks for array in stack]

    def kernel(where_ref, *refs):
        out = refs[-1]
        for bits_copy in range(copies):
            start = pl.multiple_of((where_ref[1] ^ bits_copy) * step, 16)
            blocks = [
                ref.at[row]
                for ref in refs[bits_copy * each : (bits_copy + 1) * each]
                for row in range(ref.shape[0])
            ]
            for block, bits in zip(blocks, ranks(count)):
                out[where_ref[0] ^ bits, pl.ds(start, span), :] = block[...]

    shape = jax.ShapeDtypeStruct((count, own_rows, cols), low)
    return local_call(kernel, shape, [], "assemble_rows", where, *arrays)


def assemble_copies(where, stacks, own_rows):
    copies, count, span, cols = stacks.shape
    step, _ = windows(own_rows, copies, 16)

    def kernel(where_ref, stacks_ref, out):
        for copy in range(copies if step else 1):
            for rank, bits in enumerate(ranks(count)):
                out[where_ref[0] ^ bits, copy * step : copy * step + span, :] = stacks_ref[
                    copy, rank
                ]

    shape = jax.ShapeDtypeStruct((count, own_rows, cols), low)
    return local_call(kernel, shape, [], "assemble_copies", where, stacks)


def split_heads(where, block, count, width):
    rows, cols = block.shape

    def kernel(where_ref, block_ref, *refs):
        outs, pieces = refs[: count // 2], refs[count // 2]
        for other in range(count):
            start, stop = min(cols, other * width), min(cols, (other + 1) * width)
            if start < stop:
                pieces[other, :, : stop - start] = block_ref[:, start:stop]
            if stop - start < width:
                pieces[other, :, stop - start :] = jnp.zeros((rows, width - stop + start), low)
        for bits in range(count):
            outs[bits // 2][bits % 2] = pieces[where_ref[0] ^ bits]

    shape = jax.ShapeDtypeStruct((2, rows, width), low)
    scratch = [pltpu.VMEM((count, rows, width), low)]
    return local_call(kernel, [shape] * (count // 2), scratch, "split_heads", where, block)


def order_heads(where, pairs, far):
    half = len(pairs)
    count = 2 * half
    _, rows, width = far.shape

    def kernel(where_ref, *refs):
        out, pieces = refs[-2], refs[-1]
        for pair in range(half):
            pieces[2 * pair] = refs[pair][0]
            pieces[2 * pair + 1] = refs[half][pair]
        for other in range(count):
            out[:, other * width : (other + 1) * width] = pieces[where_ref[0] ^ other]

    shape = jax.ShapeDtypeStruct((rows, count * width), low)
    scratch = [pltpu.VMEM((count, rows, width), low)]
    return local_call(kernel, shape, scratch, "order_heads", where, *pairs, far)


SLOTS = 4


def lane_of(bits, cols):
    return bits // SLOTS * cols


def own_block(ref, bits, cols, groups):
    slot, group = lax.rem(bits, SLOTS), lax.div(bits, SLOTS)
    value = ref[slot, :, :cols].astype(full)
    for index in range(1, groups):
        other = ref[slot, :, index * cols : (index + 1) * cols].astype(full)
        value = jnp.where(group == index, other, value)
    return value


def pack_hidden(where, fc_full, proj_full, sums, copies):
    count, rows, cols = fc_full.shape
    step, span = windows(rows, copies, 16)
    proj_step, proj_span = windows(proj_full.shape[0], copies, 8)
    extra = -(-(proj_span + 16) // span)
    after = slot_rows(proj_span) - (extra - 1) * span

    def kernel(where_ref, fc_ref, proj_ref, sums_ref, out_ref):
        for copy in range(copies):
            out = out_ref.at[copy]
            for bits in range(count):
                lane = lane_of(bits, cols)
                out[bits % SLOTS, :, lane : lane + cols] = fc_ref[
                    where_ref[0] ^ bits, copy * step : copy * step + span, :
                ].astype(low)
            for slot in range(extra):
                length = min(span, proj_span - slot * span)
                if length > 0:
                    at = copy * proj_step + slot * span
                    out[SLOTS + slot, :length, :] = proj_ref[at : at + length, :].astype(low)
            out[SLOTS + extra - 1, after : after + 16, : sums.shape[2]] = sums_ref[copy].astype(low)

    shape = jax.ShapeDtypeStruct((copies, SLOTS + extra, span, D), low)
    return local_call(kernel, shape, [], "pack_hidden", where, fc_full, proj_full, sums)


def sum_hidden(where, pieces, count, cols):
    number = len(pieces)
    slots, span, _ = pieces[0].shape

    def kernel(where_ref, *refs):
        outs, rest = refs[number:-1], refs[-1]
        for slot in range(slots):
            total = refs[0][slot].astype(full)
            for piece in refs[1:number]:
                total = total + piece[slot].astype(full)
            total = total.astype(low)
            if slot >= SLOTS:
                rest[slot - SLOTS] = total
                continue
            for bits in range(slot, count, SLOTS):
                lane = lane_of(bits, cols)
                outs[bits // 2][bits % 2] = total[:, lane : lane + cols]

    shapes = [jax.ShapeDtypeStruct((2, span, cols), low)] * (count // 2)
    shapes.append(jax.ShapeDtypeStruct((slots - SLOTS, span, D), low))
    outs = local_call(kernel, shapes, [], "sum_hidden", where, *pieces)
    return outs[:-1], outs[-1]


def join_hidden(where, got, far, rest):
    half = len(got)
    _, span, cols = far.shape

    def kernel(where_ref, *refs):
        out = refs[-1]
        for bits in range(2 * half):
            block = refs[half][bits // 2] if bits % 2 else refs[bits // 2][0]
            lane = lane_of(bits, cols)
            out[bits % SLOTS, :, lane : lane + cols] = block
        for slot in range(rest.shape[0]):
            out[SLOTS + slot] = refs[half + 1][slot]

    shape = jax.ShapeDtypeStruct((SLOTS + rest.shape[0], span, D), low)
    return local_call(kernel, shape, [], "join_hidden", where, *got, far, rest)


def finish_hidden(where, stacks, count, rows, cols, proj_rows, lanes):
    copies = len(stacks)
    slots, span, _ = stacks[0].shape
    step, _ = windows(rows, copies, 16)
    proj_step, proj_span = windows(proj_rows, copies, 8)
    extra = slots - SLOTS
    after = slot_rows(proj_span) - (extra - 1) * span

    def kernel(where_ref, *refs):
        fc_out, proj_out, sums_out = refs[copies:]
        for index in range(copies):
            piece, copy = refs[index], where_ref[1] ^ index
            start = pl.multiple_of(copy * step, 16)
            if step or index == 0:
                for other in range(count):
                    fc_out[pl.ds(start, span), other * cols : (other + 1) * cols] = own_block(
                        piece, where_ref[0] ^ other, cols, count // SLOTS
                    )
            for slot in range(extra):
                length = min(span, proj_span - slot * span)
                if length > 0:
                    at = copy * proj_step
                    at = pl.multiple_of(at + slot * span, 8) if span % 8 == 0 else at
                    proj_out[pl.ds(at, length), :] = piece[SLOTS + slot, :length, :].astype(full)
            sums_out[copy] = piece[SLOTS + extra - 1, after : after + 16, :lanes].astype(full)

    shapes = [
        jax.ShapeDtypeStruct((rows, count * cols), full),
        jax.ShapeDtypeStruct((proj_rows, D), full),
        jax.ShapeDtypeStruct((copies, 16, lanes), full),
    ]
    return local_call(kernel, shapes, [], "finish_hidden", where, *stacks)


def split_outw(where, grad, copies):
    count, rows, cols = grad.shape
    half = count // 2
    step, span = windows(rows, copies, 16)
    parts = copies if step else 1

    def kernel(where_ref, grad_ref, *refs):
        far = refs[parts]
        for index in range(parts):
            start = pl.multiple_of((where_ref[1] ^ index) * step, 16)
            for pair in range(half):
                for side, out in enumerate((refs[index], far.at[index])):
                    out[pair] = grad_ref[
                        where_ref[0] ^ (2 * pair + side), pl.ds(start, span), :
                    ].astype(low)

    shapes = [jax.ShapeDtypeStruct((half, span, cols), low)] * parts
    shapes.append(jax.ShapeDtypeStruct((parts, half, span, cols), low))
    outs = local_call(kernel, shapes, [], "split_outw", where, grad)
    return outs[:-1], outs[-1]


def pack_last(where, qkv_full, near, far, sums):
    copies, parts = sums.shape[0], len(near)
    count, rows, cols = qkv_full.shape
    half = count // 2
    step, span = windows(rows, copies, 16)
    spare = count // SLOTS * cols

    def kernel(where_ref, qkv_ref, *refs):
        far_ref, sums_ref = refs[parts], refs[parts + 1]
        for index, out in enumerate(refs[parts + 2 :]):
            copy = where_ref[1] ^ index
            start = pl.multiple_of(copy * step, 16)
            for bits in range(count):
                lane = lane_of(bits, cols)
                out[bits % SLOTS, :, lane : lane + cols] = qkv_ref[
                    where_ref[0] ^ bits, pl.ds(start, span), :
                ].astype(low)
                row = bits // SLOTS * 16
                out[bits % SLOTS, row : row + 16, spare : spare + 64] = sums_ref[copy, bits].astype(
                    low
                )
            for pair in range(half):
                total = refs[index % parts][pair].astype(full)
                total = total + far_ref[index % parts, pair].astype(full)
                out[SLOTS + pair] = total.astype(low)

    shape = jax.ShapeDtypeStruct((SLOTS + half, span, D), low)
    return local_call(kernel, [shape] * copies, [], "pack_last", where, qkv_full, *near, far, sums)


def sum_last(where, pieces, count, cols):
    number = len(pieces)
    half = count // 2
    span = pieces[0].shape[1]
    spare = count // SLOTS * cols

    def kernel(where_ref, *refs):
        outs = refs[number:]
        for slot in range(SLOTS + half):
            total = refs[0][slot].astype(full)
            for piece in refs[1:number]:
                total = total + piece[slot].astype(full)
            total = total.astype(low)
            if slot >= SLOTS:
                outs[slot - SLOTS][1] = total
                continue
            for bits in range(slot, count, SLOTS):
                lane, row, side = lane_of(bits, cols), bits // SLOTS * 16, bits % 2
                out = outs[bits // 2]
                out[0, :, side * cols : (side + 1) * cols] = total[:, lane : lane + cols]
                out[0, side * 16 : side * 16 + 16, 2 * cols : 2 * cols + 64] = total[
                    row : row + 16, spare : spare + 64
                ]

    shape = jax.ShapeDtypeStruct((2, span, D), low)
    return local_call(kernel, [shape] * half, [], "sum_last", where, *pieces)


def odd_last(where, got, cols):
    half = len(got)
    span = got[0].shape[1]

    def kernel(where_ref, *refs):
        out = refs[half]
        for pair in range(half):
            out[pair, :, :cols] = refs[pair][0, :, cols : 2 * cols]
            out[pair, :16, cols : cols + 64] = refs[pair][0, 16:32, 2 * cols : 2 * cols + 64]

    shape = jax.ShapeDtypeStruct((half, span, cols + 64), low)
    return local_call(kernel, shape, [], "odd_last", where, *got)


def join_last(where, got, far):
    half = len(got)
    _, span, wide = far.shape
    cols = wide - 64
    spare = 2 * half // SLOTS * cols

    def kernel(where_ref, *refs):
        far_ref, out = refs[half], refs[half + 1]
        sums = jnp.zeros((16, 64), full)
        total = jnp.zeros((span, D), full)
        for pair in range(half):
            for side in range(2):
                lane = lane_of(2 * pair + side, cols)
                block = far_ref[pair, :, :cols] if side else refs[pair][0, :, :cols]
                out[(2 * pair + side) % SLOTS, :, lane : lane + cols] = block
            sums = sums + refs[pair][0, :16, 2 * cols : 2 * cols + 64].astype(full)
            sums = sums + far_ref[pair, :16, cols : cols + 64].astype(full)
            total = total + refs[pair][1].astype(full)
        out[SLOTS] = total.astype(low)
        out[0, :16, spare : spare + 64] = sums.astype(low)

    shape = jax.ShapeDtypeStruct((SLOTS + 1, span, D), low)
    return local_call(kernel, shape, [], "join_last", where, *got, far)


def finish_last(where, stacks, count, rows, width):
    copies = len(stacks)
    span = stacks[0].shape[1]
    step, _ = windows(rows, copies, 16)
    cols = 3 * width
    spare = count // SLOTS * cols

    def kernel(where_ref, *refs):
        qkv_out, outw_out, sums_out = refs[copies:]
        for index in range(copies):
            piece, copy = refs[index], where_ref[1] ^ index
            start = pl.multiple_of(copy * step, 16)
            sums_out[copy] = piece[0, :16, spare : spare + 64].astype(full)
            if index and not step:
                continue
            outw_out[pl.ds(start, span), :] = piece[SLOTS].astype(full)
            for other in range(count):
                have = min(width, D - other * width)
                if have <= 0:
                    continue
                block = own_block(piece, where_ref[0] ^ other, cols, count // SLOTS)
                for third in range(3):
                    target = third * D + other * width
                    qkv_out[pl.ds(start, span), target : target + have] = block[
                        :, third * width : third * width + have
                    ]

    shapes = [
        jax.ShapeDtypeStruct((rows, 3 * D), full),
        jax.ShapeDtypeStruct((rows, D), full),
        jax.ShapeDtypeStruct((copies, 16, 64), full),
    ]
    return local_call(kernel, shapes, [], "finish_last", where, *stacks)


def on_device(
    tokens,
    offsets,
    qkv_weight,
    out_weight,
    fc_weight,
    proj_weight,
    query_bias,
    value_bias,
    out_bias,
    fc_bias,
    proj_bias,
    gain_first,
    shift_first,
    gain_second,
    shift_second,
    cotangent,
):
    count = lax.axis_size("shard")
    copies = lax.axis_size("replica")
    place = lax.axis_index("shard")
    copy = lax.axis_index("replica")
    where = jnp.stack([place, copy]).astype(jnp.int32)
    evens = list(range(0, count, 2))
    bits_of = ranks(count)
    half = count // 2
    heads = -(-H // count)
    span = windows(D // count, copies, 16)[1]
    width = heads * HD
    own_rows = D // count
    ff_cols = fc_weight.shape[1] // count

    def gather_rows(block):
        return lax.all_gather(block, "shard", axis=0, tiled=True)

    def scatter_rows(blocks):
        blocks = with_layout_constraint(blocks, Layout((0, 1)))
        return lax.psum_scatter(blocks, "shard", scatter_dimension=0, tiled=True)

    def exchange(pairs):
        got = [pairs[0]] + [xor_send(pairs[j], "shard", evens[j]) for j in range(1, half)]
        return got, xor_send(jnp.concatenate([pair[1:] for pair in got], 0), "shard", 1)

    def by_rank(got, far):
        return jnp.concatenate([pair[:1] for pair in got] + [far], 0)

    def from_copies(block):
        return [block] + [xor_send(block, "replica", bits) for bits in range(1, copies)]

    def to_copies(pieces):
        return [pieces[0]] + [xor_send(pieces[bits], "replica", bits) for bits in range(1, copies)]

    def tie(value, *others):
        return lax.optimization_barrier((value,) + others)[0]

    vectors = (
        query_bias,
        value_bias,
        out_bias,
        proj_bias,
        gain_first,
        shift_first,
        gain_second,
        shift_second,
    )
    token_all = gather_rows(tokens)
    qkv_got, qkv_far = exchange(pack_heads(where, qkv_weight, copies, count, width))
    qkv_stack = by_rank(qkv_got, qkv_far)
    vectors = tie(jnp.concatenate(vectors), qkv_stack, token_all)
    vectors = jnp.pad(vectors[None], ((0, 7), (0, D - 8 * own_rows)))
    fc_pairs = pack_columns(where, fc_weight, out_weight, vectors, copies, count)
    fc_got = [fc_pairs[0]] + [xor_send(fc_pairs[j], "shard", evens[j]) for j in range(1, half)]
    fc_odd, out_near = split_columns(where, fc_got, span, ff_cols)
    fc_far = xor_send(fc_odd, "shard", 1)
    vectors = jnp.concatenate([got[2 * slot_rows(span) :][:1] for got in fc_got], 0)
    vectors = jnp.concatenate([vectors, xor_send(vectors, "shard", 1)], 0)
    vectors = vectors[:, : 8 * own_rows].astype(full)
    chosen = (jnp.arange(count)[:, None] ^ place == jnp.array(bits_of)[None, :]).astype(full)
    vectors = lax.dot(chosen, vectors, precision=lax.Precision.HIGHEST)
    vectors = vectors.reshape(count, 8, own_rows).transpose(1, 0, 2).reshape(8, D)
    b_query, b_value, b_out, b_proj, g_first, s_first, g_second, s_second = vectors
    qkv_stacks = lax.all_gather(qkv_stack.reshape(count * span, 3 * width), "replica")
    qkv_stacks = qkv_stacks.reshape(copies, count, span, 3 * width)
    w_qkv = assemble_copies(where, tie(qkv_stacks, *fc_got), own_rows)
    w_qkv = w_qkv.reshape(D, 3 * width)

    out_near = from_copies(out_near)
    out_far = [xor_send(block, "shard", 1) for block in out_near]
    w_out = assemble_rows(where, list(zip(out_near, out_far)), own_rows).reshape(D, D)
    fc_stack = jnp.concatenate(
        [got[:span, :ff_cols][None] for got in fc_got] + [fc_far], 0
    )
    fc_stacks = from_copies(fc_stack)
    w_fc = assemble_rows(where, [[stack] for stack in fc_stacks], own_rows).reshape(D, ff_cols)

    def own_heads(vector):
        vector = jnp.pad(vector, (0, count * width - D))
        return lax.dynamic_slice_in_dim(vector, place * width, width, 0)

    seqs = count // CP
    starts = lax.dynamic_slice_in_dim(offsets, copy * seqs, seqs, 0)[:, :, 0] // STRETCH
    is_at = starts[:, None, :] == jnp.arange(CP)[None, :, None]
    order = jnp.sum(jnp.where(is_at, jnp.arange(CP)[None, None, :], 0), axis=2)
    order = order + CP * jnp.arange(seqs)[:, None]
    bits = order ^ place
    order = jnp.concatenate([order, bits, rank_of(bits, count)], 0).astype(jnp.int32)

    normed_low = layer_norm(token_all.astype(full), g_first, s_first).astype(low)
    projected = mm(normed_low, w_qkv, 1, 0)
    queries = (projected[:, :width] + own_heads(b_query)).astype(low)
    keys = tie(projected, fc_stack)[:, width : 2 * width].astype(low)
    values = (projected[:, 2 * width :] + own_heads(b_value)).astype(low)
    cot_all = gather_rows(tie(cotangent, w_qkv))
    attended, log_total = attend_forward(order, queries, keys, values, heads)

    attended = tie(attended, *out_near)
    attended_own = order_heads(where, *exchange(list(attended.reshape(half, 2, STRETCH, width))))
    attended_own = attended_own[:, :D]
    in_rows = tokens.astype(full)
    middle = in_rows + mm(attended_own, w_out, 1, 0) + b_out
    second_own = layer_norm(middle, g_second, s_second).astype(low)
    second_all = gather_rows(tie(second_own, cot_all, fc_stacks[1]))
    hidden = mm(second_all, w_fc, 1, 0) + fc_bias.astype(full)
    active, pull_gelu = jax.vjp(gelu_tanh, hidden)
    active_low = active.astype(low)

    (hidden_grad,) = pull_gelu(mm(cot_all, proj_weight, 1, 1))
    hidden_low = hidden_grad.astype(low)
    second_part = mm(hidden_low, w_fc, 1, 1).astype(low)
    second_grad = scatter_rows(second_part).astype(full)

    proj_full = mm(tie(active_low, second_part), cot_all, 0, 0)
    fc_full = mm(tie(second_all, second_part), hidden_low, 0, 0)
    hidden_sums = jnp.sum(hidden_low.astype(full), axis=0).reshape(copies, 1, ff_cols // copies)
    hidden_sums = jnp.pad(hidden_sums, ((0, 0), (0, 15), (0, -ff_cols // copies % 128)))
    hidden_pieces = pack_hidden(
        where, fc_full.reshape(count, own_rows, ff_cols), proj_full, hidden_sums, copies
    )
    second_grad = tie(second_grad, hidden_pieces)
    hidden_shape = hidden_pieces.shape[1:]
    hidden_sum = lax.psum_scatter(
        hidden_pieces.reshape(-1, D), "replica", scatter_dimension=0, tiled=True
    ).reshape(hidden_shape)
    grad_rows = cotangent.astype(full)
    _, pull_second = jax.vjp(layer_norm, middle, g_second, s_second)
    middle_part, gsecond_part, ssecond_part = pull_second(second_grad)
    middle_grad = grad_rows + middle_part
    branch_low = middle_grad.astype(low)
    attended_grad = mm(branch_low, w_out, 1, 1).astype(low)
    attended_pairs = split_heads(where, attended_grad, count, width)
    outw_full = mm(attended_own, tie(branch_low, attended_pairs[0]), 0, 0)
    outw_near, outw_far = split_outw(where, outw_full.reshape(count, own_rows, D), copies)
    attended_grad = by_rank(*exchange(attended_pairs)).reshape(count * STRETCH, width)
    outw_far = xor_send(outw_far, "shard", 1)
    early = jnp.stack(
        [jnp.sum(branch_low.astype(full), axis=0), jnp.sum(grad_rows, axis=0), gsecond_part, ssecond_part]
    )

    query_grads, key_grads, value_grads = attend_backward(
        order, queries, keys, values, attended_grad, log_total, heads
    )
    projected_grad = jnp.concatenate([query_grads, key_grads, value_grads], 1)
    first_part = mm(projected_grad, w_qkv, 1, 1)

    def head_sums(block):
        sums = jnp.sum(block.astype(full), axis=0)
        placed = lax.dynamic_update_slice_in_dim(
            jnp.zeros((count * width,), full), sums, place * width, 0
        )
        return placed[:D]

    norms = normed(token_all.astype(full))
    sums = jnp.stack(
        [
            head_sums(query_grads),
            head_sums(value_grads),
            early[0],
            early[1],
            jnp.sum(first_part * norms, axis=0),
            jnp.sum(first_part, axis=0),
            early[2],
            early[3],
        ]
    )
    sums = sums.reshape(8, count, own_rows).transpose(1, 0, 2).reshape(count, 8 * own_rows)
    by_bits = (jnp.arange(count)[:, None] ^ place == jnp.arange(count)[None, :]).astype(full)
    sums = lax.dot(by_bits, sums, precision=lax.Precision.HIGHEST)
    share = 8 * own_rows // copies
    sums = sums.reshape(count, copies, share).transpose(1, 0, 2)
    sums = jnp.pad(sums, ((0, 0), (0, 0), (0, 16 * 64 - share))).reshape(copies, count, 16, 64)
    first_grad = scatter_rows(first_part.astype(low)).astype(full)
    qkv_full = mm(normed_low, projected_grad, 0, 0).reshape(count, own_rows, 3 * width)
    last = pack_last(where, qkv_full, outw_near, outw_far, sums)
    first_grad = tie(first_grad, last[0])
    hidden_sum = tie(hidden_sum, last[0])
    last = to_copies(last)

    fc_sums, rest = sum_hidden(where, [hidden_sum], count, ff_cols)
    hidden_joined = join_hidden(where, *exchange(fc_sums), rest)
    hidden_stacks = from_copies(hidden_joined)
    fc_grad, proj_grad, fbias = finish_hidden(
        where, hidden_stacks, count, own_rows, ff_cols, ff_cols, hidden_sums.shape[2]
    )
    fbias = fbias[:, 0, : ff_cols // copies].reshape(ff_cols)

    last[0] = tie(last[0], hidden_joined)
    last = sum_last(where, last, count, 3 * width)
    output_low = tie(active_low, last[0])
    last = [last[0]] + [xor_send(last[j], "shard", evens[j]) for j in range(1, half)]
    far = xor_send(odd_last(where, last, 3 * width), "shard", 1)
    last = from_copies(join_last(where, last, tie(far, hidden_stacks[1])))
    output_part = mm(output_low, proj_weight, 1, 0).astype(low)
    output = middle + b_proj + scatter_rows(output_part).astype(full)

    _, pull_first = jax.vjp(lambda rows: layer_norm(rows, g_first, s_first), in_rows)
    (input_part,) = pull_first(first_grad)
    tokens_grad = (middle_grad + input_part).astype(low)
    output = output.astype(low)
    last[0] = tie(last[0], output, tokens_grad)

    qkv_grad, outw_grad, sums = finish_last(where, last, count, own_rows, width)
    sums = sums.reshape(copies, 16 * 64)[:, :share].reshape(8, own_rows)
    qbias, vbias, obias, pbias, gfirst, sfirst, gsecond, ssecond = sums
    return (
        output,
        tokens_grad,
        qkv_grad,
        outw_grad,
        fc_grad,
        proj_grad,
        qbias,
        vbias,
        obias,
        fbias,
        pbias,
        gfirst,
        sfirst,
        gsecond,
        ssecond,
    )


def solution(mesh):
    rows = P(("replica", "shard"), None)
    matrix = P("shard", None)
    vector = P("shard")
    return jax.shard_map(
        on_device,
        mesh=mesh,
        in_specs=(rows, P()) + (matrix,) * 4 + (vector,) * 9 + (rows,),
        out_specs=(rows, rows) + (matrix,) * 4 + (vector,) * 9,
        check_vma=False,
    )
```

```python
import functools

import jax
import jax.numpy as jnp
from jax import lax
from jax.experimental import pallas as pl
from jax.experimental.pallas import tpu as pltpu
from jax.experimental.layout import Layout, with_layout_constraint
from jax.sharding import PartitionSpec as P

D = 1600
H = 25
HD = 64
CP = 8
STRETCH = 128
SEQ = CP * STRETCH
TILE = 256

norm_eps = 1e-05
masked_score = -1e30
gelu_coeff = 0.7978845608028654
low = jnp.bfloat16
full = jnp.float32


def xor_send(block, axis, bits):
    count = lax.axis_size(axis)
    return lax.ppermute(block, axis, [(i, i ^ bits) for i in range(count)])


def normed(values):
    average = jnp.mean(values, axis=-1, keepdims=True)
    centred = values - average
    variance = jnp.mean(centred * centred, axis=-1, keepdims=True)
    return centred * lax.rsqrt(variance + norm_eps)


def layer_norm(values, gain_vec, shift_vec):
    return normed(values) * gain_vec + shift_vec


def gelu_tanh(values):
    return (
        0.5 * values * (1.0 + jnp.tanh(gelu_coeff * (values + 0.044715 * values * values * values)))
    )


def mm(left_side, right_side, left_dim, right_dim):
    return lax.dot_general(
        left_side,
        right_side,
        (((left_dim,), (right_dim,)), ((), ())),
        preferred_element_type=full,
    )


def sort_blocks(order_ref, seq, source, target):
    for place in range(CP):
        start = pl.multiple_of(order_ref[seq, place] * STRETCH, STRETCH)
        target[place * STRETCH : (place + 1) * STRETCH, :] = source[pl.ds(start, STRETCH), :]


def unsort_tile(order_ref, seq, tile, value, target):
    for part in range(TILE // STRETCH):
        place = tile * (TILE // STRETCH) + part
        start = pl.multiple_of(order_ref[seq, place] * STRETCH, STRETCH)
        target[pl.ds(start, STRETCH), :] = value[part * STRETCH : (part + 1) * STRETCH, :]


def causal(scores):
    key_row = lax.broadcasted_iota(jnp.int32, scores.shape, 0)
    query_col = lax.broadcasted_iota(jnp.int32, scores.shape, 1)
    return jnp.where(key_row <= query_col, scores, masked_score)


def forward_kernel(heads, seqs, order_ref, q_ref, k_ref, v_ref, a_ref, lse_ref, qs, ks, vs, qt, vt):
    width = heads * HD
    for seq in range(seqs):
        sort_blocks(order_ref, seq, q_ref, qs)
        sort_blocks(order_ref, seq, k_ref, ks)
        sort_blocks(order_ref, seq, v_ref, vs)
        qt[...] = (qs[...].astype(full).T * HD ** (-0.5)).astype(low)
        vt[...] = vs[...].astype(full).T.astype(low)
        for tile in range(SEQ // TILE):
            cols = slice(tile * TILE, (tile + 1) * TILE)
            before = tile * TILE
            pieces = []
            for head in range(heads):
                row = lax.broadcasted_iota(jnp.int32, (width, TILE), 0)
                mine = (row >= head * HD) & (row < (head + 1) * HD)
                query = jnp.where(mine, qt[:, cols], jnp.zeros((), low))
                diag = causal(mm(ks[cols, :], query, 1, 0))
                high = jnp.max(diag, axis=0, keepdims=True)
                if tile:
                    past = mm(ks[:before, :], query, 1, 0)
                    high = jnp.maximum(high, jnp.max(past, axis=0, keepdims=True))
                    past = jnp.exp(past - high)
                diag = jnp.exp(diag - high)
                total = jnp.sum(diag, axis=0, keepdims=True)
                if tile:
                    total = total + jnp.sum(past, axis=0, keepdims=True)
                share = 1.0 / total
                own = slice(head * HD, (head + 1) * HD)
                mixed = mm(vt[own, cols], (diag * share).astype(low), 1, 0)
                if tile:
                    mixed = mixed + mm(vt[own, :before], (past * share).astype(low), 1, 0)
                pieces.append(mixed)
                lse_ref[seq, head : head + 1, cols] = high + jnp.log(total)
            mixed = jnp.concatenate(pieces, 0).T.astype(low)
            unsort_tile(order_ref, seqs + seq, tile, mixed, a_ref)


def backward_kernel(
    heads, seqs, order_ref, q_ref, k_ref, v_ref, da_ref, lse_ref,
    dq_ref, dk_ref, dv_ref, qs, ks, vs, das, qt, kt, dat, dks, dvs,
):
    width = heads * HD
    scale = HD ** (-0.5)
    for seq in range(seqs):
        sort_blocks(order_ref, seq, q_ref, qs)
        sort_blocks(order_ref, seq, k_ref, ks)
        sort_blocks(order_ref, seq, v_ref, vs)
        sort_blocks(order_ref, 2 * seqs + seq, da_ref, das)
        qt[...] = (qs[...].astype(full).T * scale).astype(low)
        kt[...] = (ks[...].astype(full).T * scale).astype(low)
        dat[...] = das[...].astype(full).T.astype(low)
        dks[...] = jnp.zeros_like(dks)
        dvs[...] = jnp.zeros_like(dvs)
        for tile in range(SEQ // TILE):
            cols = slice(tile * TILE, (tile + 1) * TILE)
            before = tile * TILE
            pieces = []
            for head in range(heads):
                own = slice(head * HD, (head + 1) * HD)
                row = lax.broadcasted_iota(jnp.int32, (width, TILE), 0)
                mine = (row >= head * HD) & (row < (head + 1) * HD)
                lane = lax.broadcasted_iota(jnp.int32, (TILE, width), 1)
                mine_lane = (lane >= head * HD) & (lane < (head + 1) * HD)
                none = jnp.zeros((), low)
                query_t = jnp.where(mine, qt[:, cols], none)
                grad_t = jnp.where(mine, dat[:, cols], none)
                query = jnp.where(mine_lane, qs[cols, :], none)
                grad = jnp.where(mine_lane, das[cols, :], none)
                log_total = lse_ref[seq, head : head + 1, cols]

                spans = [(cols, True)] + ([(slice(0, before), False)] if tile else [])
                kept = []
                dot = None
                for span, edge in spans:
                    scores = mm(ks[span, :], query_t, 1, 0)
                    if edge:
                        scores = causal(scores)
                    weights = jnp.exp(scores - log_total)
                    weight_grads = mm(vs[span, :], grad_t, 1, 0)
                    part = jnp.sum(weights * weight_grads, axis=0, keepdims=True)
                    dot = part if dot is None else dot + part
                    dvs[span, :] += mm(weights.astype(low), grad, 1, 0)
                    kept.append((span, weights, weight_grads))
                total = None
                for span, weights, weight_grads in kept:
                    score_grads = (weights * (weight_grads - dot)).astype(low)
                    dks[span, :] += mm(score_grads, query, 1, 0)
                    part = mm(kt[own, span], score_grads, 1, 0)
                    total = part if total is None else total + part
                pieces.append(total)
            unsort_tile(order_ref, seq, tile, jnp.concatenate(pieces, 0).T.astype(low), dq_ref)
        for tile in range(SEQ // TILE):
            cols = slice(tile * TILE, (tile + 1) * TILE)
            unsort_tile(order_ref, seq, tile, (dks[cols, :] * scale).astype(low), dk_ref)
            unsort_tile(order_ref, seq, tile, dvs[cols, :].astype(low), dv_ref)


vmem = pl.BlockSpec(memory_space=pltpu.VMEM)
smem = pl.BlockSpec(memory_space=pltpu.SMEM)


def attend_forward(order, queries, keys, values, heads):
    rows, width = queries.shape
    seqs = rows // SEQ
    return pl.pallas_call(
        functools.partial(forward_kernel, heads, seqs),
        out_shape=(
            jax.ShapeDtypeStruct((rows, width), low),
            jax.ShapeDtypeStruct((seqs, heads, SEQ), full),
        ),
        in_specs=[smem, vmem, vmem, vmem],
        out_specs=(vmem, vmem),
        scratch_shapes=[pltpu.VMEM((SEQ, width), low)] * 3 + [pltpu.VMEM((width, SEQ), low)] * 2,
        compiler_params=pltpu.CompilerParams(vmem_limit_bytes=40 * 2**20),
        cost_estimate=pl.CostEstimate(
            flops=seqs * heads * 2 * 2 * SEQ * SEQ * 256,
            bytes_accessed=8 * rows * width,
            transcendentals=seqs * heads * SEQ * SEQ,
        ),
        name="attend_forward",
    )(order, queries, keys, values)


def attend_backward(order, queries, keys, values, grads, log_total, heads):
    rows, width = queries.shape
    seqs = rows // SEQ
    shape = jax.ShapeDtypeStruct((rows, width), low)
    return pl.pallas_call(
        functools.partial(backward_kernel, heads, seqs),
        out_shape=(shape, shape, shape),
        in_specs=[smem, vmem, vmem, vmem, vmem, vmem],
        out_specs=(vmem, vmem, vmem),
        scratch_shapes=[pltpu.VMEM((SEQ, width), low)] * 4
        + [pltpu.VMEM((width, SEQ), low)] * 3
        + [pltpu.VMEM((SEQ, width), full)] * 2,
        compiler_params=pltpu.CompilerParams(vmem_limit_bytes=48 * 2**20),
        cost_estimate=pl.CostEstimate(
            flops=seqs * heads * 2 * 5 * SEQ * SEQ * 256,
            bytes_accessed=14 * rows * width,
            transcendentals=seqs * heads * SEQ * SEQ,
        ),
        name="attend_backward",
    )(order, queries, keys, values, grads, log_total)


def ranks(count):
    return list(range(0, count, 2)) + list(range(1, count, 2))


def rank_of(bits, count):
    return (bits & 1) * (count // 2) + (bits >> 1)


def windows(rows, copies, unit):
    step = rows // copies // unit * unit
    return step, rows - step * (copies - 1)


def local_call(kernel, shapes, scratch, name, where, *operands, after=()):
    operands = operands + tuple(after)
    many = isinstance(shapes, (list, tuple))
    size = sum(x.size * x.dtype.itemsize for x in operands)
    free = pl.BlockSpec(memory_space=pl.ANY)
    used = len(operands) - len(after)
    return pl.pallas_call(
        kernel,
        out_shape=tuple(shapes) if many else shapes,
        in_specs=[smem] + [vmem] * used + [free] * len(after),
        out_specs=tuple(vmem for _ in shapes) if many else vmem,
        scratch_shapes=scratch,
        compiler_params=pltpu.CompilerParams(vmem_limit_bytes=56 * 2**20),
        cost_estimate=pl.CostEstimate(flops=0, bytes_accessed=3 * size, transcendentals=0),
        name=name,
    )(where, *operands)


def pack_heads(where, weight, copies, count, width):
    step, span = windows(weight.shape[0], copies, 16)

    def kernel(where_ref, weight_ref, *refs):
        outs, pieces = refs[: count // 2], refs[count // 2]
        start = pl.multiple_of(where_ref[1] * step, 16)
        for other in range(count):
            low_col, high_col = other * width, min(D, (other + 1) * width)
            for third in range(3):
                have = max(0, high_col - low_col)
                at = third * width
                if have:
                    pieces[other, :, at : at + have] = weight_ref[
                        pl.ds(start, span), third * D + low_col : third * D + high_col
                    ]
                if have < width:
                    pieces[other, :, at + have : at + width] = jnp.zeros((span, width - have), low)
        for bits in range(count):
            outs[bits // 2][bits % 2] = pieces[where_ref[0] ^ bits]

    shape = jax.ShapeDtypeStruct((2, span, 3 * width), low)
    scratch = [pltpu.VMEM((count, span, 3 * width), low)]
    return local_call(kernel, [shape] * (count // 2), scratch, "pack_heads", where, weight)


def slot_rows(span):
    return -(-span // 8) * 8


def pack_columns(where, weight, out_weight, vectors, copies, count):
    step, span = windows(weight.shape[0], copies, 16)
    cols = weight.shape[1] // count
    slot = slot_rows(span)

    def kernel(where_ref, weight_ref, out_ref, vectors_ref, *refs):
        outs, pieces = refs[: count // 2], refs[count // 2]
        start = pl.multiple_of(where_ref[1] * step, 16)
        for other in range(count):
            pieces[other] = weight_ref[pl.ds(start, span), other * cols : (other + 1) * cols]
        for pair, out in enumerate(outs):
            for side in range(2):
                out[:span, side * cols : (side + 1) * cols] = pieces[
                    where_ref[0] ^ (2 * pair + side)
                ]
            out[slot : slot + span, :] = out_ref[pl.ds(start, span), :]
            out[2 * slot :, :] = vectors_ref[...]

    shape = jax.ShapeDtypeStruct((2 * slot + 8, D), low)
    scratch = [pltpu.VMEM((count, span, cols), low)]
    return local_call(
        kernel, [shape] * (count // 2), scratch, "pack_columns", where, weight, out_weight, vectors
    )


def split_columns(where, got, span, cols):
    half = len(got)
    slot = slot_rows(span)

    def kernel(where_ref, *refs):
        odd, rows = refs[half:]
        for pair in range(half):
            odd[pair] = refs[pair][:span, cols : 2 * cols]
            rows[pair] = refs[pair][slot : slot + span, :]

    shapes = [
        jax.ShapeDtypeStruct((half, span, cols), low),
        jax.ShapeDtypeStruct((half, span, D), low),
    ]
    return local_call(kernel, shapes, [], "split_columns", where, *got)


def assemble_rows(where, stacks, own_rows):
    each = len(stacks[0])
    count = sum(array.shape[0] for array in stacks[0])
    span, cols = stacks[0][0].shape[1:]
    step, _ = windows(own_rows, len(stacks), 16)
    stacks = stacks if step else stacks[:1]
    copies = len(stacks)
    arrays = [array for stack in stacks for array in stack]

    def kernel(where_ref, *refs):
        out = refs[-1]
        for bits_copy in range(copies):
            start = pl.multiple_of((where_ref[1] ^ bits_copy) * step, 16)
            blocks = [
                ref.at[row]
                for ref in refs[bits_copy * each : (bits_copy + 1) * each]
                for row in range(ref.shape[0])
            ]
            for block, bits in zip(blocks, ranks(count)):
                out[where_ref[0] ^ bits, pl.ds(start, span), :] = block[...]

    shape = jax.ShapeDtypeStruct((count, own_rows, cols), low)
    return local_call(kernel, shape, [], "assemble_rows", where, *arrays)


def assemble_copies(where, stacks, own_rows):
    copies, count, span, cols = stacks.shape
    step, _ = windows(own_rows, copies, 16)

    def kernel(where_ref, stacks_ref, out):
        for copy in range(copies if step else 1):
            for rank, bits in enumerate(ranks(count)):
                out[where_ref[0] ^ bits, copy * step : copy * step + span, :] = stacks_ref[
                    copy, rank
                ]

    shape = jax.ShapeDtypeStruct((count, own_rows, cols), low)
    return local_call(kernel, shape, [], "assemble_copies", where, stacks)


def split_heads(where, block, count, width):
    rows, cols = block.shape

    def kernel(where_ref, block_ref, *refs):
        outs, pieces = refs[: count // 2], refs[count // 2]
        for other in range(count):
            start, stop = min(cols, other * width), min(cols, (other + 1) * width)
            if start < stop:
                pieces[other, :, : stop - start] = block_ref[:, start:stop]
            if stop - start < width:
                pieces[other, :, stop - start :] = jnp.zeros((rows, width - stop + start), low)
        for bits in range(count):
            outs[bits // 2][bits % 2] = pieces[where_ref[0] ^ bits]

    shape = jax.ShapeDtypeStruct((2, rows, width), low)
    scratch = [pltpu.VMEM((count, rows, width), low)]
    return local_call(kernel, [shape] * (count // 2), scratch, "split_heads", where, block)


def order_heads(where, pairs, far):
    half = len(pairs)
    count = 2 * half
    _, rows, width = far.shape

    def kernel(where_ref, *refs):
        out, pieces = refs[-2], refs[-1]
        for pair in range(half):
            pieces[2 * pair] = refs[pair][0]
            pieces[2 * pair + 1] = refs[half][pair]
        for other in range(count):
            out[:, other * width : (other + 1) * width] = pieces[where_ref[0] ^ other]

    shape = jax.ShapeDtypeStruct((rows, count * width), low)
    scratch = [pltpu.VMEM((count, rows, width), low)]
    return local_call(kernel, shape, scratch, "order_heads", where, *pairs, far)


SLOTS = 4


def lane_of(bits, cols):
    return bits // SLOTS * cols


def own_block(ref, bits, cols, groups):
    slot, group = lax.rem(bits, SLOTS), lax.div(bits, SLOTS)
    value = ref[slot, :, :cols].astype(full)
    for index in range(1, groups):
        other = ref[slot, :, index * cols : (index + 1) * cols].astype(full)
        value = jnp.where(group == index, other, value)
    return value


def pack_hidden(where, fc_full, proj_full, sums, copies):
    count, rows, cols = fc_full.shape
    step, span = windows(rows, copies, 16)
    proj_step, proj_span = windows(proj_full.shape[0], copies, 8)
    extra = -(-(proj_span + 16) // span)
    after = slot_rows(proj_span) - (extra - 1) * span

    def kernel(where_ref, fc_ref, proj_ref, sums_ref, out_ref):
        for copy in range(copies):
            out = out_ref.at[copy]
            for bits in range(count):
                lane = lane_of(bits, cols)
                out[bits % SLOTS, :, lane : lane + cols] = fc_ref[
                    where_ref[0] ^ bits, copy * step : copy * step + span, :
                ].astype(low)
            for slot in range(extra):
                length = min(span, proj_span - slot * span)
                if length > 0:
                    at = copy * proj_step + slot * span
                    out[SLOTS + slot, :length, :] = proj_ref[at : at + length, :].astype(low)
            out[SLOTS + extra - 1, after : after + 16, : sums.shape[2]] = sums_ref[copy].astype(low)

    shape = jax.ShapeDtypeStruct((copies, SLOTS + extra, span, D), low)
    return local_call(kernel, shape, [], "pack_hidden", where, fc_full, proj_full, sums)


def sum_hidden(where, pieces, count, cols):
    number = len(pieces)
    slots, span, _ = pieces[0].shape

    def kernel(where_ref, *refs):
        outs, rest = refs[number:-1], refs[-1]
        for slot in range(slots):
            total = refs[0][slot].astype(full)
            for piece in refs[1:number]:
                total = total + piece[slot].astype(full)
            total = total.astype(low)
            if slot >= SLOTS:
                rest[slot - SLOTS] = total
                continue
            for bits in range(slot, count, SLOTS):
                lane = lane_of(bits, cols)
                outs[bits // 2][bits % 2] = total[:, lane : lane + cols]

    shapes = [jax.ShapeDtypeStruct((2, span, cols), low)] * (count // 2)
    shapes.append(jax.ShapeDtypeStruct((slots - SLOTS, span, D), low))
    outs = local_call(kernel, shapes, [], "sum_hidden", where, *pieces)
    return outs[:-1], outs[-1]


def join_hidden(where, got, far, rest):
    half = len(got)
    _, span, cols = far.shape

    def kernel(where_ref, *refs):
        out = refs[-1]
        for bits in range(2 * half):
            block = refs[half][bits // 2] if bits % 2 else refs[bits // 2][0]
            lane = lane_of(bits, cols)
            out[bits % SLOTS, :, lane : lane + cols] = block
        for slot in range(rest.shape[0]):
            out[SLOTS + slot] = refs[half + 1][slot]

    shape = jax.ShapeDtypeStruct((SLOTS + rest.shape[0], span, D), low)
    return local_call(kernel, shape, [], "join_hidden", where, *got, far, rest)


def finish_hidden(where, stacks, count, rows, cols, proj_rows, lanes):
    copies = len(stacks)
    slots, span, _ = stacks[0].shape
    step, _ = windows(rows, copies, 16)
    proj_step, proj_span = windows(proj_rows, copies, 8)
    extra = slots - SLOTS
    after = slot_rows(proj_span) - (extra - 1) * span

    def kernel(where_ref, *refs):
        fc_out, proj_out, sums_out = refs[copies:]
        for index in range(copies):
            piece, copy = refs[index], where_ref[1] ^ index
            start = pl.multiple_of(copy * step, 16)
            if step or index == 0:
                for other in range(count):
                    fc_out[pl.ds(start, span), other * cols : (other + 1) * cols] = own_block(
                        piece, where_ref[0] ^ other, cols, count // SLOTS
                    )
            for slot in range(extra):
                length = min(span, proj_span - slot * span)
                if length > 0:
                    at = copy * proj_step
                    at = pl.multiple_of(at + slot * span, 8) if span % 8 == 0 else at
                    proj_out[pl.ds(at, length), :] = piece[SLOTS + slot, :length, :].astype(full)
            sums_out[copy] = piece[SLOTS + extra - 1, after : after + 16, :lanes].astype(full)

    shapes = [
        jax.ShapeDtypeStruct((rows, count * cols), full),
        jax.ShapeDtypeStruct((proj_rows, D), full),
        jax.ShapeDtypeStruct((copies, 16, lanes), full),
    ]
    return local_call(kernel, shapes, [], "finish_hidden", where, *stacks)


def split_outw(where, grad, copies):
    count, rows, cols = grad.shape
    half = count // 2
    step, span = windows(rows, copies, 16)
    parts = copies if step else 1

    def kernel(where_ref, grad_ref, *refs):
        far = refs[parts]
        for index in range(parts):
            start = pl.multiple_of((where_ref[1] ^ index) * step, 16)
            for pair in range(half):
                for side, out in enumerate((refs[index], far.at[index])):
                    out[pair] = grad_ref[
                        where_ref[0] ^ (2 * pair + side), pl.ds(start, span), :
                    ].astype(low)

    shapes = [jax.ShapeDtypeStruct((half, span, cols), low)] * parts
    shapes.append(jax.ShapeDtypeStruct((parts, half, span, cols), low))
    outs = local_call(kernel, shapes, [], "split_outw", where, grad)
    return outs[:-1], outs[-1]


def pack_last(where, qkv_full, near, far, sums):
    copies, parts = sums.shape[0], len(near)
    count, rows, cols = qkv_full.shape
    half = count // 2
    step, span = windows(rows, copies, 16)
    spare = count // SLOTS * cols

    def kernel(where_ref, qkv_ref, *refs):
        far_ref, sums_ref = refs[parts], refs[parts + 1]
        for index, out in enumerate(refs[parts + 2 :]):
            copy = where_ref[1] ^ index
            start = pl.multiple_of(copy * step, 16)
            for bits in range(count):
                lane = lane_of(bits, cols)
                out[bits % SLOTS, :, lane : lane + cols] = qkv_ref[
                    where_ref[0] ^ bits, pl.ds(start, span), :
                ].astype(low)
                row = bits // SLOTS * 16
                out[bits % SLOTS, row : row + 16, spare : spare + 64] = sums_ref[copy, bits].astype(
                    low
                )
            for pair in range(half):
                total = refs[index % parts][pair].astype(full)
                total = total + far_ref[index % parts, pair].astype(full)
                out[SLOTS + pair] = total.astype(low)

    shape = jax.ShapeDtypeStruct((SLOTS + half, span, D), low)
    return local_call(kernel, [shape] * copies, [], "pack_last", where, qkv_full, *near, far, sums)


def sum_last(where, pieces, count, cols):
    number = len(pieces)
    half = count // 2
    span = pieces[0].shape[1]
    spare = count // SLOTS * cols

    def kernel(where_ref, *refs):
        outs = refs[number:]
        for slot in range(SLOTS + half):
            total = refs[0][slot].astype(full)
            for piece in refs[1:number]:
                total = total + piece[slot].astype(full)
            total = total.astype(low)
            if slot >= SLOTS:
                outs[slot - SLOTS][1] = total
                continue
            for bits in range(slot, count, SLOTS):
                lane, row, side = lane_of(bits, cols), bits // SLOTS * 16, bits % 2
                out = outs[bits // 2]
                out[0, :, side * cols : (side + 1) * cols] = total[:, lane : lane + cols]
                out[0, side * 16 : side * 16 + 16, 2 * cols : 2 * cols + 64] = total[
                    row : row + 16, spare : spare + 64
                ]

    shape = jax.ShapeDtypeStruct((2, span, D), low)
    return local_call(kernel, [shape] * half, [], "sum_last", where, *pieces)


def odd_last(where, got, cols):
    half = len(got)
    span = got[0].shape[1]

    def kernel(where_ref, *refs):
        out = refs[half]
        for pair in range(half):
            out[pair, :, :cols] = refs[pair][0, :, cols : 2 * cols]
            out[pair, :16, cols : cols + 64] = refs[pair][0, 16:32, 2 * cols : 2 * cols + 64]

    shape = jax.ShapeDtypeStruct((half, span, cols + 64), low)
    return local_call(kernel, shape, [], "odd_last", where, *got)


def join_last(where, got, far):
    half = len(got)
    _, span, wide = far.shape
    cols = wide - 64
    spare = 2 * half // SLOTS * cols

    def kernel(where_ref, *refs):
        far_ref, out = refs[half], refs[half + 1]
        sums = jnp.zeros((16, 64), full)
        total = jnp.zeros((span, D), full)
        for pair in range(half):
            for side in range(2):
                lane = lane_of(2 * pair + side, cols)
                block = far_ref[pair, :, :cols] if side else refs[pair][0, :, :cols]
                out[(2 * pair + side) % SLOTS, :, lane : lane + cols] = block
            sums = sums + refs[pair][0, :16, 2 * cols : 2 * cols + 64].astype(full)
            sums = sums + far_ref[pair, :16, cols : cols + 64].astype(full)
            total = total + refs[pair][1].astype(full)
        out[SLOTS] = total.astype(low)
        out[0, :16, spare : spare + 64] = sums.astype(low)

    shape = jax.ShapeDtypeStruct((SLOTS + 1, span, D), low)
    return local_call(kernel, shape, [], "join_last", where, *got, far)


def finish_last(where, stacks, count, rows, width):
    copies = len(stacks)
    span = stacks[0].shape[1]
    step, _ = windows(rows, copies, 16)
    cols = 3 * width
    spare = count // SLOTS * cols

    def kernel(where_ref, *refs):
        qkv_out, outw_out, sums_out = refs[copies:]
        for index in range(copies):
            piece, copy = refs[index], where_ref[1] ^ index
            start = pl.multiple_of(copy * step, 16)
            sums_out[copy] = piece[0, :16, spare : spare + 64].astype(full)
            if index and not step:
                continue
            outw_out[pl.ds(start, span), :] = piece[SLOTS].astype(full)
            for other in range(count):
                have = min(width, D - other * width)
                if have <= 0:
                    continue
                block = own_block(piece, where_ref[0] ^ other, cols, count // SLOTS)
                for third in range(3):
                    target = third * D + other * width
                    qkv_out[pl.ds(start, span), target : target + have] = block[
                        :, third * width : third * width + have
                    ]

    shapes = [
        jax.ShapeDtypeStruct((rows, 3 * D), full),
        jax.ShapeDtypeStruct((rows, D), full),
        jax.ShapeDtypeStruct((copies, 16, 64), full),
    ]
    return local_call(kernel, shapes, [], "finish_last", where, *stacks)


def on_device(
    tokens,
    offsets,
    qkv_weight,
    out_weight,
    fc_weight,
    proj_weight,
    query_bias,
    value_bias,
    out_bias,
    fc_bias,
    proj_bias,
    gain_first,
    shift_first,
    gain_second,
    shift_second,
    cotangent,
):
    count = lax.axis_size("shard")
    copies = lax.axis_size("replica")
    place = lax.axis_index("shard")
    copy = lax.axis_index("replica")
    where = jnp.stack([place, copy]).astype(jnp.int32)
    evens = list(range(0, count, 2))
    bits_of = ranks(count)
    half = count // 2
    heads = -(-H // count)
    span = windows(D // count, copies, 16)[1]
    width = heads * HD
    own_rows = D // count
    ff_cols = fc_weight.shape[1] // count

    def gather_rows(block):
        return lax.all_gather(block, "shard", axis=0, tiled=True)

    def scatter_rows(blocks):
        blocks = with_layout_constraint(blocks, Layout((0, 1)))
        return lax.psum_scatter(blocks, "shard", scatter_dimension=0, tiled=True)

    def exchange(pairs):
        got = [pairs[0]] + [xor_send(pairs[j], "shard", evens[j]) for j in range(1, half)]
        return got, xor_send(jnp.concatenate([pair[1:] for pair in got], 0), "shard", 1)

    def by_rank(got, far):
        return jnp.concatenate([pair[:1] for pair in got] + [far], 0)

    def from_copies(block):
        return [block] + [xor_send(block, "replica", bits) for bits in range(1, copies)]

    def to_copies(pieces):
        return [pieces[0]] + [xor_send(pieces[bits], "replica", bits) for bits in range(1, copies)]

    def tie(value, *others):
        return lax.optimization_barrier((value,) + others)[0]

    vectors = (
        query_bias,
        value_bias,
        out_bias,
        proj_bias,
        gain_first,
        shift_first,
        gain_second,
        shift_second,
    )
    token_all = gather_rows(tokens)
    qkv_got, qkv_far = exchange(pack_heads(where, qkv_weight, copies, count, width))
    qkv_stack = by_rank(qkv_got, qkv_far)
    vectors = tie(jnp.concatenate(vectors), qkv_stack, token_all)
    vectors = jnp.pad(vectors[None], ((0, 7), (0, D - 8 * own_rows)))
    fc_pairs = pack_columns(where, fc_weight, out_weight, vectors, copies, count)
    fc_got = [fc_pairs[0]] + [xor_send(fc_pairs[j], "shard", evens[j]) for j in range(1, half)]
    fc_odd, out_near = split_columns(where, fc_got, span, ff_cols)
    fc_far = xor_send(fc_odd, "shard", 1)
    vectors = jnp.concatenate([got[2 * slot_rows(span) :][:1] for got in fc_got], 0)
    vectors = jnp.concatenate([vectors, xor_send(vectors, "shard", 1)], 0)
    vectors = vectors[:, : 8 * own_rows].astype(full)
    chosen = (jnp.arange(count)[:, None] ^ place == jnp.array(bits_of)[None, :]).astype(full)
    vectors = lax.dot(chosen, vectors, precision=lax.Precision.HIGHEST)
    vectors = vectors.reshape(count, 8, own_rows).transpose(1, 0, 2).reshape(8, D)
    b_query, b_value, b_out, b_proj, g_first, s_first, g_second, s_second = vectors
    qkv_stacks = lax.all_gather(qkv_stack.reshape(count * span, 3 * width), "replica")
    qkv_stacks = qkv_stacks.reshape(copies, count, span, 3 * width)
    w_qkv = assemble_copies(where, tie(qkv_stacks, *fc_got), own_rows)
    w_qkv = w_qkv.reshape(D, 3 * width)

    out_near = from_copies(out_near)
    out_far = [xor_send(block, "shard", 1) for block in out_near]
    w_out = assemble_rows(where, list(zip(out_near, out_far)), own_rows).reshape(D, D)
    fc_stack = jnp.concatenate(
        [got[:span, :ff_cols][None] for got in fc_got] + [fc_far], 0
    )
    fc_stacks = from_copies(fc_stack)
    w_fc = assemble_rows(where, [[stack] for stack in fc_stacks], own_rows).reshape(D, ff_cols)

    def own_heads(vector):
        vector = jnp.pad(vector, (0, count * width - D))
        return lax.dynamic_slice_in_dim(vector, place * width, width, 0)

    seqs = count // CP
    starts = lax.dynamic_slice_in_dim(offsets, copy * seqs, seqs, 0)[:, :, 0] // STRETCH
    is_at = starts[:, None, :] == jnp.arange(CP)[None, :, None]
    order = jnp.sum(jnp.where(is_at, jnp.arange(CP)[None, None, :], 0), axis=2)
    order = order + CP * jnp.arange(seqs)[:, None]
    bits = order ^ place
    order = jnp.concatenate([order, bits, rank_of(bits, count)], 0).astype(jnp.int32)

    normed_low = layer_norm(token_all.astype(full), g_first, s_first).astype(low)
    projected = mm(normed_low, w_qkv, 1, 0)
    queries = (projected[:, :width] + own_heads(b_query)).astype(low)
    keys = tie(projected, fc_stack)[:, width : 2 * width].astype(low)
    values = (projected[:, 2 * width :] + own_heads(b_value)).astype(low)
    cot_all = gather_rows(tie(cotangent, w_qkv))
    attended, log_total = attend_forward(order, queries, keys, values, heads)

    attended = tie(attended, *out_near)
    attended_own = order_heads(where, *exchange(list(attended.reshape(half, 2, STRETCH, width))))
    attended_own = attended_own[:, :D]
    in_rows = tokens.astype(full)
    middle = in_rows + mm(attended_own, w_out, 1, 0) + b_out
    second_own = layer_norm(middle, g_second, s_second).astype(low)
    second_all = gather_rows(tie(second_own, cot_all, fc_stacks[1]))
    hidden = mm(second_all, w_fc, 1, 0) + fc_bias.astype(full)
    active, pull_gelu = jax.vjp(gelu_tanh, hidden)
    active_low = active.astype(low)

    (hidden_grad,) = pull_gelu(mm(cot_all, proj_weight, 1, 1))
    hidden_low = hidden_grad.astype(low)
    second_part = mm(hidden_low, w_fc, 1, 1).astype(low)
    second_grad = scatter_rows(second_part).astype(full)

    proj_full = mm(tie(active_low, second_part), cot_all, 0, 0)
    fc_full = mm(tie(second_all, second_part), hidden_low, 0, 0)
    hidden_sums = jnp.sum(hidden_low.astype(full), axis=0).reshape(copies, 1, ff_cols // copies)
    hidden_sums = jnp.pad(hidden_sums, ((0, 0), (0, 15), (0, -ff_cols // copies % 128)))
    hidden_pieces = pack_hidden(
        where, fc_full.reshape(count, own_rows, ff_cols), proj_full, hidden_sums, copies
    )
    second_grad = tie(second_grad, hidden_pieces)
    hidden_shape = hidden_pieces.shape[1:]
    hidden_sum = lax.psum_scatter(
        hidden_pieces.reshape(-1, D), "replica", scatter_dimension=0, tiled=True
    ).reshape(hidden_shape)
    grad_rows = cotangent.astype(full)
    _, pull_second = jax.vjp(layer_norm, middle, g_second, s_second)
    middle_part, gsecond_part, ssecond_part = pull_second(second_grad)
    middle_grad = grad_rows + middle_part
    branch_low = middle_grad.astype(low)
    attended_grad = mm(branch_low, w_out, 1, 1).astype(low)
    attended_pairs = split_heads(where, attended_grad, count, width)
    outw_full = mm(attended_own, tie(branch_low, attended_pairs[0]), 0, 0)
    outw_near, outw_far = split_outw(where, outw_full.reshape(count, own_rows, D), copies)
    attended_grad = by_rank(*exchange(attended_pairs)).reshape(count * STRETCH, width)
    outw_far = xor_send(outw_far, "shard", 1)
    early = jnp.stack(
        [jnp.sum(branch_low.astype(full), axis=0), jnp.sum(grad_rows, axis=0), gsecond_part, ssecond_part]
    )

    query_grads, key_grads, value_grads = attend_backward(
        order, queries, keys, values, attended_grad, log_total, heads
    )
    projected_grad = jnp.concatenate([query_grads, key_grads, value_grads], 1)
    first_part = mm(projected_grad, w_qkv, 1, 1)
    first_part = with_layout_constraint(first_part, Layout((0, 1)))

    def head_sums(block):
        sums = jnp.sum(block.astype(full), axis=0)
        placed = lax.dynamic_update_slice_in_dim(
            jnp.zeros((count * width,), full), sums, place * width, 0
        )
        return placed[:D]

    norms = normed(token_all.astype(full))
    sums = jnp.stack(
        [
            head_sums(query_grads),
            head_sums(value_grads),
            early[0],
            early[1],
            jnp.sum(first_part * norms, axis=0),
            jnp.sum(first_part, axis=0),
            early[2],
            early[3],
        ]
    )
    sums = sums.reshape(8, count, own_rows).transpose(1, 0, 2).reshape(count, 8 * own_rows)
    by_bits = (jnp.arange(count)[:, None] ^ place == jnp.arange(count)[None, :]).astype(full)
    sums = lax.dot(by_bits, sums, precision=lax.Precision.HIGHEST)
    share = 8 * own_rows // copies
    sums = sums.reshape(count, copies, share).transpose(1, 0, 2)
    sums = jnp.pad(sums, ((0, 0), (0, 0), (0, 16 * 64 - share))).reshape(copies, count, 16, 64)
    first_grad = scatter_rows(first_part.astype(low)).astype(full)
    qkv_full = mm(normed_low, projected_grad, 0, 0).reshape(count, own_rows, 3 * width)
    last = pack_last(where, qkv_full, outw_near, outw_far, sums)
    first_grad = tie(first_grad, last[0])
    hidden_sum = tie(hidden_sum, last[0])
    last = to_copies(last)

    fc_sums, rest = sum_hidden(where, [hidden_sum], count, ff_cols)
    fc_sums, fc_sums_far = exchange(fc_sums)
    output_low = tie(active_low, fc_sums[1])
    hidden_joined = join_hidden(where, fc_sums, fc_sums_far, tie(rest, *last[1:]))
    hidden_stacks = from_copies(hidden_joined)
    fc_grad, proj_grad, fbias = finish_hidden(
        where, hidden_stacks, count, own_rows, ff_cols, ff_cols, hidden_sums.shape[2]
    )
    fbias = fbias[:, 0, : ff_cols // copies].reshape(ff_cols)

    last[0] = tie(last[0], hidden_joined)
    last = sum_last(where, last, count, 3 * width)
    last = [last[0]] + [xor_send(last[j], "shard", evens[j]) for j in range(1, half)]
    _, pull_first = jax.vjp(lambda rows: layer_norm(rows, g_first, s_first), in_rows)
    (input_part,) = pull_first(first_grad)
    tokens_grad = (middle_grad + input_part).astype(low)
    last[1] = tie(last[1], tokens_grad)
    far = xor_send(odd_last(where, last, 3 * width), "shard", 1)
    last = from_copies(join_last(where, last, tie(far, hidden_stacks[1])))
    output_part = mm(output_low, proj_weight, 1, 0).astype(low)
    output = middle + b_proj + scatter_rows(output_part).astype(full)

    output = output.astype(low)
    last[0] = tie(last[0], output)

    qkv_grad, outw_grad, sums = finish_last(where, last, count, own_rows, width)
    sums = sums.reshape(copies, 16 * 64)[:, :share].reshape(8, own_rows)
    qbias, vbias, obias, pbias, gfirst, sfirst, gsecond, ssecond = sums
    return (
        output,
        tokens_grad,
        qkv_grad,
        outw_grad,
        fc_grad,
        proj_grad,
        qbias,
        vbias,
        obias,
        fbias,
        pbias,
        gfirst,
        sfirst,
        gsecond,
        ssecond,
    )


def solution(mesh):
    rows = P(("replica", "shard"), None)
    matrix = P("shard", None)
    vector = P("shard")
    return jax.shard_map(
        on_device,
        mesh=mesh,
        in_specs=(rows, P()) + (matrix,) * 4 + (vector,) * 9 + (rows,),
        out_specs=(rows, rows) + (matrix,) * 4 + (vector,) * 9,
        check_vma=False,
    )
```

```python
import functools

import jax
import jax.numpy as jnp
from jax import lax
from jax.experimental import pallas as pl
from jax.experimental.pallas import tpu as pltpu
from jax.experimental.layout import Layout, with_layout_constraint
from jax.sharding import PartitionSpec as P

D = 1600
H = 25
HD = 64
CP = 8
STRETCH = 128
SEQ = CP * STRETCH
TILE = 256

norm_eps = 1e-05
masked_score = -1e30
gelu_coeff = 0.7978845608028654
low = jnp.bfloat16
full = jnp.float32


def xor_send(block, axis, bits):
    count = lax.axis_size(axis)
    return lax.ppermute(block, axis, [(i, i ^ bits) for i in range(count)])


def normed(values):
    average = jnp.mean(values, axis=-1, keepdims=True)
    centred = values - average
    variance = jnp.mean(centred * centred, axis=-1, keepdims=True)
    return centred * lax.rsqrt(variance + norm_eps)


def layer_norm(values, gain_vec, shift_vec):
    return normed(values) * gain_vec + shift_vec


def gelu_tanh(values):
    return (
        0.5 * values * (1.0 + jnp.tanh(gelu_coeff * (values + 0.044715 * values * values * values)))
    )


def mm(left_side, right_side, left_dim, right_dim):
    return lax.dot_general(
        left_side,
        right_side,
        (((left_dim,), (right_dim,)), ((), ())),
        preferred_element_type=full,
    )


def sort_blocks(order_ref, seq, source, target):
    for place in range(CP):
        start = pl.multiple_of(order_ref[seq, place] * STRETCH, STRETCH)
        target[place * STRETCH : (place + 1) * STRETCH, :] = source[pl.ds(start, STRETCH), :]


def unsort_tile(order_ref, seq, tile, value, target):
    for part in range(TILE // STRETCH):
        place = tile * (TILE // STRETCH) + part
        start = pl.multiple_of(order_ref[seq, place] * STRETCH, STRETCH)
        target[pl.ds(start, STRETCH), :] = value[part * STRETCH : (part + 1) * STRETCH, :]


def causal(scores):
    key_row = lax.broadcasted_iota(jnp.int32, scores.shape, 0)
    query_col = lax.broadcasted_iota(jnp.int32, scores.shape, 1)
    return jnp.where(key_row <= query_col, scores, masked_score)


def forward_kernel(heads, seqs, order_ref, q_ref, k_ref, v_ref, a_ref, lse_ref, qs, ks, vs, qt, vt):
    width = heads * HD
    for seq in range(seqs):
        sort_blocks(order_ref, seq, q_ref, qs)
        sort_blocks(order_ref, seq, k_ref, ks)
        sort_blocks(order_ref, seq, v_ref, vs)
        qt[...] = (qs[...].astype(full).T * HD ** (-0.5)).astype(low)
        vt[...] = vs[...].astype(full).T.astype(low)
        for tile in range(SEQ // TILE):
            cols = slice(tile * TILE, (tile + 1) * TILE)
            before = tile * TILE
            pieces = []
            for head in range(heads):
                row = lax.broadcasted_iota(jnp.int32, (width, TILE), 0)
                mine = (row >= head * HD) & (row < (head + 1) * HD)
                query = jnp.where(mine, qt[:, cols], jnp.zeros((), low))
                diag = causal(mm(ks[cols, :], query, 1, 0))
                high = jnp.max(diag, axis=0, keepdims=True)
                if tile:
                    past = mm(ks[:before, :], query, 1, 0)
                    high = jnp.maximum(high, jnp.max(past, axis=0, keepdims=True))
                    past = jnp.exp(past - high)
                diag = jnp.exp(diag - high)
                total = jnp.sum(diag, axis=0, keepdims=True)
                if tile:
                    total = total + jnp.sum(past, axis=0, keepdims=True)
                share = 1.0 / total
                own = slice(head * HD, (head + 1) * HD)
                mixed = mm(vt[own, cols], (diag * share).astype(low), 1, 0)
                if tile:
                    mixed = mixed + mm(vt[own, :before], (past * share).astype(low), 1, 0)
                pieces.append(mixed)
                lse_ref[seq, head : head + 1, cols] = high + jnp.log(total)
            mixed = jnp.concatenate(pieces, 0).T.astype(low)
            unsort_tile(order_ref, seqs + seq, tile, mixed, a_ref)


def backward_kernel(
    heads, seqs, order_ref, q_ref, k_ref, v_ref, da_ref, lse_ref,
    dq_ref, dk_ref, dv_ref, qs, ks, vs, das, qt, kt, dat, dks, dvs,
):
    width = heads * HD
    scale = HD ** (-0.5)
    for seq in range(seqs):
        sort_blocks(order_ref, seq, q_ref, qs)
        sort_blocks(order_ref, seq, k_ref, ks)
        sort_blocks(order_ref, seq, v_ref, vs)
        sort_blocks(order_ref, 2 * seqs + seq, da_ref, das)
        qt[...] = (qs[...].astype(full).T * scale).astype(low)
        kt[...] = (ks[...].astype(full).T * scale).astype(low)
        dat[...] = das[...].astype(full).T.astype(low)
        dks[...] = jnp.zeros_like(dks)
        dvs[...] = jnp.zeros_like(dvs)
        for tile in range(SEQ // TILE):
            cols = slice(tile * TILE, (tile + 1) * TILE)
            before = tile * TILE
            pieces = []
            for head in range(heads):
                own = slice(head * HD, (head + 1) * HD)
                row = lax.broadcasted_iota(jnp.int32, (width, TILE), 0)
                mine = (row >= head * HD) & (row < (head + 1) * HD)
                lane = lax.broadcasted_iota(jnp.int32, (TILE, width), 1)
                mine_lane = (lane >= head * HD) & (lane < (head + 1) * HD)
                none = jnp.zeros((), low)
                query_t = jnp.where(mine, qt[:, cols], none)
                grad_t = jnp.where(mine, dat[:, cols], none)
                query = jnp.where(mine_lane, qs[cols, :], none)
                grad = jnp.where(mine_lane, das[cols, :], none)
                log_total = lse_ref[seq, head : head + 1, cols]

                spans = [(cols, True)] + ([(slice(0, before), False)] if tile else [])
                kept = []
                dot = None
                for span, edge in spans:
                    scores = mm(ks[span, :], query_t, 1, 0)
                    if edge:
                        scores = causal(scores)
                    weights = jnp.exp(scores - log_total)
                    weight_grads = mm(vs[span, :], grad_t, 1, 0)
                    part = jnp.sum(weights * weight_grads, axis=0, keepdims=True)
                    dot = part if dot is None else dot + part
                    dvs[span, :] += mm(weights.astype(low), grad, 1, 0)
                    kept.append((span, weights, weight_grads))
                total = None
                for span, weights, weight_grads in kept:
                    score_grads = (weights * (weight_grads - dot)).astype(low)
                    dks[span, :] += mm(score_grads, query, 1, 0)
                    part = mm(kt[own, span], score_grads, 1, 0)
                    total = part if total is None else total + part
                pieces.append(total)
            unsort_tile(order_ref, seq, tile, jnp.concatenate(pieces, 0).T.astype(low), dq_ref)
        for tile in range(SEQ // TILE):
            cols = slice(tile * TILE, (tile + 1) * TILE)
            unsort_tile(order_ref, seq, tile, (dks[cols, :] * scale).astype(low), dk_ref)
            unsort_tile(order_ref, seq, tile, dvs[cols, :].astype(low), dv_ref)


vmem = pl.BlockSpec(memory_space=pltpu.VMEM)
smem = pl.BlockSpec(memory_space=pltpu.SMEM)


def attend_forward(order, queries, keys, values, heads):
    rows, width = queries.shape
    seqs = rows // SEQ
    return pl.pallas_call(
        functools.partial(forward_kernel, heads, seqs),
        out_shape=(
            jax.ShapeDtypeStruct((rows, width), low),
            jax.ShapeDtypeStruct((seqs, heads, SEQ), full),
        ),
        in_specs=[smem, vmem, vmem, vmem],
        out_specs=(vmem, vmem),
        scratch_shapes=[pltpu.VMEM((SEQ, width), low)] * 3 + [pltpu.VMEM((width, SEQ), low)] * 2,
        compiler_params=pltpu.CompilerParams(vmem_limit_bytes=40 * 2**20),
        cost_estimate=pl.CostEstimate(
            flops=seqs * heads * 2 * 2 * SEQ * SEQ * 256,
            bytes_accessed=8 * rows * width,
            transcendentals=seqs * heads * SEQ * SEQ,
        ),
        name="attend_forward",
    )(order, queries, keys, values)


def attend_backward(order, queries, keys, values, grads, log_total, heads):
    rows, width = queries.shape
    seqs = rows // SEQ
    shape = jax.ShapeDtypeStruct((rows, width), low)
    return pl.pallas_call(
        functools.partial(backward_kernel, heads, seqs),
        out_shape=(shape, shape, shape),
        in_specs=[smem, vmem, vmem, vmem, vmem, vmem],
        out_specs=(vmem, vmem, vmem),
        scratch_shapes=[pltpu.VMEM((SEQ, width), low)] * 4
        + [pltpu.VMEM((width, SEQ), low)] * 3
        + [pltpu.VMEM((SEQ, width), full)] * 2,
        compiler_params=pltpu.CompilerParams(vmem_limit_bytes=48 * 2**20),
        cost_estimate=pl.CostEstimate(
            flops=seqs * heads * 2 * 5 * SEQ * SEQ * 256,
            bytes_accessed=14 * rows * width,
            transcendentals=seqs * heads * SEQ * SEQ,
        ),
        name="attend_backward",
    )(order, queries, keys, values, grads, log_total)


def ranks(count):
    return list(range(0, count, 2)) + list(range(1, count, 2))


def rank_of(bits, count):
    return (bits & 1) * (count // 2) + (bits >> 1)


def windows(rows, copies, unit):
    step = rows // copies // unit * unit
    return step, rows - step * (copies - 1)


def local_call(kernel, shapes, scratch, name, where, *operands, after=()):
    operands = operands + tuple(after)
    many = isinstance(shapes, (list, tuple))
    size = sum(x.size * x.dtype.itemsize for x in operands)
    free = pl.BlockSpec(memory_space=pl.ANY)
    used = len(operands) - len(after)
    return pl.pallas_call(
        kernel,
        out_shape=tuple(shapes) if many else shapes,
        in_specs=[smem] + [vmem] * used + [free] * len(after),
        out_specs=tuple(vmem for _ in shapes) if many else vmem,
        scratch_shapes=scratch,
        compiler_params=pltpu.CompilerParams(vmem_limit_bytes=56 * 2**20),
        cost_estimate=pl.CostEstimate(flops=0, bytes_accessed=3 * size, transcendentals=0),
        name=name,
    )(where, *operands)


def pack_heads(where, weight, copies, count, width):
    step, span = windows(weight.shape[0], copies, 16)

    def kernel(where_ref, weight_ref, *refs):
        outs, pieces = refs[: count // 2], refs[count // 2]
        start = pl.multiple_of(where_ref[1] * step, 16)
        for other in range(count):
            low_col, high_col = other * width, min(D, (other + 1) * width)
            for third in range(3):
                have = max(0, high_col - low_col)
                at = third * width
                if have:
                    pieces[other, :, at : at + have] = weight_ref[
                        pl.ds(start, span), third * D + low_col : third * D + high_col
                    ]
                if have < width:
                    pieces[other, :, at + have : at + width] = jnp.zeros((span, width - have), low)
        for bits in range(count):
            outs[bits // 2][bits % 2] = pieces[where_ref[0] ^ bits]

    shape = jax.ShapeDtypeStruct((2, span, 3 * width), low)
    scratch = [pltpu.VMEM((count, span, 3 * width), low)]
    return local_call(kernel, [shape] * (count // 2), scratch, "pack_heads", where, weight)


def slot_rows(span):
    return -(-span // 8) * 8


def pack_columns(where, weight, out_weight, vectors, copies, count):
    step, span = windows(weight.shape[0], copies, 16)
    cols = weight.shape[1] // count
    slot = slot_rows(span)

    def kernel(where_ref, weight_ref, out_ref, vectors_ref, *refs):
        outs, pieces = refs[: count // 2], refs[count // 2]
        start = pl.multiple_of(where_ref[1] * step, 16)
        for other in range(count):
            pieces[other] = weight_ref[pl.ds(start, span), other * cols : (other + 1) * cols]
        for pair, out in enumerate(outs):
            for side in range(2):
                out[:span, side * cols : (side + 1) * cols] = pieces[
                    where_ref[0] ^ (2 * pair + side)
                ]
            out[slot : slot + span, :] = out_ref[pl.ds(start, span), :]
            out[2 * slot :, :] = vectors_ref[...]

    shape = jax.ShapeDtypeStruct((2 * slot + 8, D), low)
    scratch = [pltpu.VMEM((count, span, cols), low)]
    return local_call(
        kernel, [shape] * (count // 2), scratch, "pack_columns", where, weight, out_weight, vectors
    )


def split_columns(where, got, span, cols):
    half = len(got)
    slot = slot_rows(span)

    def kernel(where_ref, *refs):
        odd, rows = refs[half:]
        for pair in range(half):
            odd[pair] = refs[pair][:span, cols : 2 * cols]
            rows[pair] = refs[pair][slot : slot + span, :]

    shapes = [
        jax.ShapeDtypeStruct((half, span, cols), low),
        jax.ShapeDtypeStruct((half, span, D), low),
    ]
    return local_call(kernel, shapes, [], "split_columns", where, *got)


def assemble_rows(where, stacks, own_rows):
    each = len(stacks[0])
    count = sum(array.shape[0] for array in stacks[0])
    span, cols = stacks[0][0].shape[1:]
    step, _ = windows(own_rows, len(stacks), 16)
    stacks = stacks if step else stacks[:1]
    copies = len(stacks)
    arrays = [array for stack in stacks for array in stack]

    def kernel(where_ref, *refs):
        out = refs[-1]
        for bits_copy in range(copies):
            start = pl.multiple_of((where_ref[1] ^ bits_copy) * step, 16)
            blocks = [
                ref.at[row]
                for ref in refs[bits_copy * each : (bits_copy + 1) * each]
                for row in range(ref.shape[0])
            ]
            for block, bits in zip(blocks, ranks(count)):
                out[where_ref[0] ^ bits, pl.ds(start, span), :] = block[...]

    shape = jax.ShapeDtypeStruct((count, own_rows, cols), low)
    return local_call(kernel, shape, [], "assemble_rows", where, *arrays)


def assemble_copies(where, stacks, own_rows):
    copies, count, span, cols = stacks.shape
    step, _ = windows(own_rows, copies, 16)

    def kernel(where_ref, stacks_ref, out):
        for copy in range(copies if step else 1):
            for rank, bits in enumerate(ranks(count)):
                out[where_ref[0] ^ bits, copy * step : copy * step + span, :] = stacks_ref[
                    copy, rank
                ]

    shape = jax.ShapeDtypeStruct((count, own_rows, cols), low)
    return local_call(kernel, shape, [], "assemble_copies", where, stacks)


def split_heads(where, block, count, width):
    rows, cols = block.shape

    def kernel(where_ref, block_ref, *refs):
        outs, pieces = refs[: count // 2], refs[count // 2]
        for other in range(count):
            start, stop = min(cols, other * width), min(cols, (other + 1) * width)
            if start < stop:
                pieces[other, :, : stop - start] = block_ref[:, start:stop]
            if stop - start < width:
                pieces[other, :, stop - start :] = jnp.zeros((rows, width - stop + start), low)
        for bits in range(count):
            outs[bits // 2][bits % 2] = pieces[where_ref[0] ^ bits]

    shape = jax.ShapeDtypeStruct((2, rows, width), low)
    scratch = [pltpu.VMEM((count, rows, width), low)]
    return local_call(kernel, [shape] * (count // 2), scratch, "split_heads", where, block)


def order_heads(where, pairs, far):
    half = len(pairs)
    count = 2 * half
    _, rows, width = far.shape

    def kernel(where_ref, *refs):
        out, pieces = refs[-2], refs[-1]
        for pair in range(half):
            pieces[2 * pair] = refs[pair][0]
            pieces[2 * pair + 1] = refs[half][pair]
        for other in range(count):
            out[:, other * width : (other + 1) * width] = pieces[where_ref[0] ^ other]

    shape = jax.ShapeDtypeStruct((rows, count * width), low)
    scratch = [pltpu.VMEM((count, rows, width), low)]
    return local_call(kernel, shape, scratch, "order_heads", where, *pairs, far)


SLOTS = 4


def lane_of(bits, cols):
    return bits // SLOTS * cols


def own_block(ref, bits, cols, groups):
    slot, group = lax.rem(bits, SLOTS), lax.div(bits, SLOTS)
    value = ref[slot, :, :cols].astype(full)
    for index in range(1, groups):
        other = ref[slot, :, index * cols : (index + 1) * cols].astype(full)
        value = jnp.where(group == index, other, value)
    return value


def pack_hidden(where, fc_full, proj_full, sums, copies):
    count, rows, cols = fc_full.shape
    step, span = windows(rows, copies, 16)
    proj_step, proj_span = windows(proj_full.shape[0], copies, 8)
    extra = -(-(proj_span + 16) // span)
    after = slot_rows(proj_span) - (extra - 1) * span

    def kernel(where_ref, fc_ref, proj_ref, sums_ref, out_ref):
        for copy in range(copies):
            out = out_ref.at[copy]
            for bits in range(count):
                lane = lane_of(bits, cols)
                out[bits % SLOTS, :, lane : lane + cols] = fc_ref[
                    where_ref[0] ^ bits, copy * step : copy * step + span, :
                ].astype(low)
            for slot in range(extra):
                length = min(span, proj_span - slot * span)
                if length > 0:
                    at = copy * proj_step + slot * span
                    out[SLOTS + slot, :length, :] = proj_ref[at : at + length, :].astype(low)
            out[SLOTS + extra - 1, after : after + 16, : sums.shape[2]] = sums_ref[copy].astype(low)

    shape = jax.ShapeDtypeStruct((copies, SLOTS + extra, span, D), low)
    return local_call(kernel, shape, [], "pack_hidden", where, fc_full, proj_full, sums)


def sum_hidden(where, pieces, count, cols):
    number = len(pieces)
    slots, span, _ = pieces[0].shape

    def kernel(where_ref, *refs):
        outs, rest = refs[number:-1], refs[-1]
        for slot in range(slots):
            total = refs[0][slot].astype(full)
            for piece in refs[1:number]:
                total = total + piece[slot].astype(full)
            total = total.astype(low)
            if slot >= SLOTS:
                rest[slot - SLOTS] = total
                continue
            for bits in range(slot, count, SLOTS):
                lane = lane_of(bits, cols)
                outs[bits // 2][bits % 2] = total[:, lane : lane + cols]

    shapes = [jax.ShapeDtypeStruct((2, span, cols), low)] * (count // 2)
    shapes.append(jax.ShapeDtypeStruct((slots - SLOTS, span, D), low))
    outs = local_call(kernel, shapes, [], "sum_hidden", where, *pieces)
    return outs[:-1], outs[-1]


def join_hidden(where, got, far, rest):
    half = len(got)
    _, span, cols = far.shape

    def kernel(where_ref, *refs):
        out = refs[-1]
        for bits in range(2 * half):
            block = refs[half][bits // 2] if bits % 2 else refs[bits // 2][0]
            lane = lane_of(bits, cols)
            out[bits % SLOTS, :, lane : lane + cols] = block
        for slot in range(rest.shape[0]):
            out[SLOTS + slot] = refs[half + 1][slot]

    shape = jax.ShapeDtypeStruct((SLOTS + rest.shape[0], span, D), low)
    return local_call(kernel, shape, [], "join_hidden", where, *got, far, rest)


def finish_hidden(where, stacks, count, rows, cols, proj_rows, lanes):
    copies = len(stacks)
    slots, span, _ = stacks[0].shape
    step, _ = windows(rows, copies, 16)
    proj_step, proj_span = windows(proj_rows, copies, 8)
    extra = slots - SLOTS
    after = slot_rows(proj_span) - (extra - 1) * span

    def kernel(where_ref, *refs):
        fc_out, proj_out, sums_out = refs[copies:]
        for index in range(copies):
            piece, copy = refs[index], where_ref[1] ^ index
            start = pl.multiple_of(copy * step, 16)
            if step or index == 0:
                for other in range(count):
                    fc_out[pl.ds(start, span), other * cols : (other + 1) * cols] = own_block(
                        piece, where_ref[0] ^ other, cols, count // SLOTS
                    )
            for slot in range(extra):
                length = min(span, proj_span - slot * span)
                if length > 0:
                    at = copy * proj_step
                    at = pl.multiple_of(at + slot * span, 8) if span % 8 == 0 else at
                    proj_out[pl.ds(at, length), :] = piece[SLOTS + slot, :length, :].astype(full)
            sums_out[copy] = piece[SLOTS + extra - 1, after : after + 16, :lanes].astype(full)

    shapes = [
        jax.ShapeDtypeStruct((rows, count * cols), full),
        jax.ShapeDtypeStruct((proj_rows, D), full),
        jax.ShapeDtypeStruct((copies, 16, lanes), full),
    ]
    return local_call(kernel, shapes, [], "finish_hidden", where, *stacks)


def split_outw(where, grad, copies):
    count, rows, cols = grad.shape
    half = count // 2
    step, span = windows(rows, copies, 16)
    parts = copies if step else 1

    def kernel(where_ref, grad_ref, *refs):
        far = refs[parts]
        for index in range(parts):
            start = pl.multiple_of((where_ref[1] ^ index) * step, 16)
            for pair in range(half):
                for side, out in enumerate((refs[index], far.at[index])):
                    out[pair] = grad_ref[
                        where_ref[0] ^ (2 * pair + side), pl.ds(start, span), :
                    ].astype(low)

    shapes = [jax.ShapeDtypeStruct((half, span, cols), low)] * parts
    shapes.append(jax.ShapeDtypeStruct((parts, half, span, cols), low))
    outs = local_call(kernel, shapes, [], "split_outw", where, grad)
    return outs[:-1], outs[-1]


def pack_last(where, qkv_full, near, far, sums):
    copies, parts = sums.shape[0], len(near)
    count, rows, cols = qkv_full.shape
    half = count // 2
    step, span = windows(rows, copies, 16)
    spare = count // SLOTS * cols

    def kernel(where_ref, qkv_ref, *refs):
        far_ref, sums_ref = refs[parts], refs[parts + 1]
        for index, out in enumerate(refs[parts + 2 :]):
            copy = where_ref[1] ^ index
            start = pl.multiple_of(copy * step, 16)
            for bits in range(count):
                lane = lane_of(bits, cols)
                out[bits % SLOTS, :, lane : lane + cols] = qkv_ref[
                    where_ref[0] ^ bits, pl.ds(start, span), :
                ].astype(low)
                row = bits // SLOTS * 16
                out[bits % SLOTS, row : row + 16, spare : spare + 64] = sums_ref[copy, bits].astype(
                    low
                )
            for pair in range(half):
                total = refs[index % parts][pair].astype(full)
                total = total + far_ref[index % parts, pair].astype(full)
                out[SLOTS + pair] = total.astype(low)

    shape = jax.ShapeDtypeStruct((SLOTS + half, span, D), low)
    return local_call(kernel, [shape] * copies, [], "pack_last", where, qkv_full, *near, far, sums)


def sum_last(where, pieces, count, cols):
    number = len(pieces)
    half = count // 2
    span = pieces[0].shape[1]
    spare = count // SLOTS * cols

    def kernel(where_ref, *refs):
        outs = refs[number:]
        for slot in range(SLOTS + half):
            total = refs[0][slot].astype(full)
            for piece in refs[1:number]:
                total = total + piece[slot].astype(full)
            total = total.astype(low)
            if slot >= SLOTS:
                outs[slot - SLOTS][1] = total
                continue
            for bits in range(slot, count, SLOTS):
                lane, row, side = lane_of(bits, cols), bits // SLOTS * 16, bits % 2
                out = outs[bits // 2]
                out[0, :, side * cols : (side + 1) * cols] = total[:, lane : lane + cols]
                out[0, side * 16 : side * 16 + 16, 2 * cols : 2 * cols + 64] = total[
                    row : row + 16, spare : spare + 64
                ]

    shape = jax.ShapeDtypeStruct((2, span, D), low)
    return local_call(kernel, [shape] * half, [], "sum_last", where, *pieces)


def odd_last(where, got, cols):
    half = len(got)
    span = got[0].shape[1]

    def kernel(where_ref, *refs):
        out = refs[half]
        for pair in range(half):
            out[pair, :, :cols] = refs[pair][0, :, cols : 2 * cols]
            out[pair, :16, cols : cols + 64] = refs[pair][0, 16:32, 2 * cols : 2 * cols + 64]

    shape = jax.ShapeDtypeStruct((half, span, cols + 64), low)
    return local_call(kernel, shape, [], "odd_last", where, *got)


def join_last(where, got, far):
    half = len(got)
    _, span, wide = far.shape
    cols = wide - 64
    spare = 2 * half // SLOTS * cols

    def kernel(where_ref, *refs):
        far_ref, out = refs[half], refs[half + 1]
        sums = jnp.zeros((16, 64), full)
        total = jnp.zeros((span, D), full)
        for pair in range(half):
            for side in range(2):
                lane = lane_of(2 * pair + side, cols)
                block = far_ref[pair, :, :cols] if side else refs[pair][0, :, :cols]
                out[(2 * pair + side) % SLOTS, :, lane : lane + cols] = block
            sums = sums + refs[pair][0, :16, 2 * cols : 2 * cols + 64].astype(full)
            sums = sums + far_ref[pair, :16, cols : cols + 64].astype(full)
            total = total + refs[pair][1].astype(full)
        out[SLOTS] = total.astype(low)
        out[0, :16, spare : spare + 64] = sums.astype(low)

    shape = jax.ShapeDtypeStruct((SLOTS + 1, span, D), low)
    return local_call(kernel, shape, [], "join_last", where, *got, far)


def finish_last(where, stacks, count, rows, width):
    copies = len(stacks)
    span = stacks[0].shape[1]
    step, _ = windows(rows, copies, 16)
    cols = 3 * width
    spare = count // SLOTS * cols

    def kernel(where_ref, *refs):
        qkv_out, outw_out, sums_out = refs[copies:]
        for index in range(copies):
            piece, copy = refs[index], where_ref[1] ^ index
            start = pl.multiple_of(copy * step, 16)
            sums_out[copy] = piece[0, :16, spare : spare + 64].astype(full)
            if index and not step:
                continue
            outw_out[pl.ds(start, span), :] = piece[SLOTS].astype(full)
            for other in range(count):
                have = min(width, D - other * width)
                if have <= 0:
                    continue
                block = own_block(piece, where_ref[0] ^ other, cols, count // SLOTS)
                for third in range(3):
                    target = third * D + other * width
                    qkv_out[pl.ds(start, span), target : target + have] = block[
                        :, third * width : third * width + have
                    ]

    shapes = [
        jax.ShapeDtypeStruct((rows, 3 * D), full),
        jax.ShapeDtypeStruct((rows, D), full),
        jax.ShapeDtypeStruct((copies, 16, 64), full),
    ]
    return local_call(kernel, shapes, [], "finish_last", where, *stacks)


def on_device(
    tokens,
    offsets,
    qkv_weight,
    out_weight,
    fc_weight,
    proj_weight,
    query_bias,
    value_bias,
    out_bias,
    fc_bias,
    proj_bias,
    gain_first,
    shift_first,
    gain_second,
    shift_second,
    cotangent,
):
    count = lax.axis_size("shard")
    copies = lax.axis_size("replica")
    place = lax.axis_index("shard")
    copy = lax.axis_index("replica")
    where = jnp.stack([place, copy]).astype(jnp.int32)
    evens = list(range(0, count, 2))
    bits_of = ranks(count)
    half = count // 2
    heads = -(-H // count)
    span = windows(D // count, copies, 16)[1]
    width = heads * HD
    own_rows = D // count
    ff_cols = fc_weight.shape[1] // count

    def gather_rows(block):
        return lax.all_gather(block, "shard", axis=0, tiled=True)

    def scatter_rows(blocks):
        blocks = with_layout_constraint(blocks, Layout((0, 1)))
        return lax.psum_scatter(blocks, "shard", scatter_dimension=0, tiled=True)

    def exchange(pairs):
        got = [pairs[0]] + [xor_send(pairs[j], "shard", evens[j]) for j in range(1, half)]
        return got, xor_send(jnp.concatenate([pair[1:] for pair in got], 0), "shard", 1)

    def by_rank(got, far):
        return jnp.concatenate([pair[:1] for pair in got] + [far], 0)

    def from_copies(block):
        return [block] + [xor_send(block, "replica", bits) for bits in range(1, copies)]

    def to_copies(pieces):
        return [pieces[0]] + [xor_send(pieces[bits], "replica", bits) for bits in range(1, copies)]

    def tie(value, *others):
        return lax.optimization_barrier((value,) + others)[0]

    vectors = (
        query_bias,
        value_bias,
        out_bias,
        proj_bias,
        gain_first,
        shift_first,
        gain_second,
        shift_second,
    )
    token_all = gather_rows(tokens)
    qkv_got, qkv_far = exchange(pack_heads(where, qkv_weight, copies, count, width))
    qkv_stack = by_rank(qkv_got, qkv_far)
    vectors = tie(jnp.concatenate(vectors), qkv_stack, token_all)
    vectors = jnp.pad(vectors[None], ((0, 7), (0, D - 8 * own_rows)))
    fc_pairs = pack_columns(where, fc_weight, out_weight, vectors, copies, count)
    fc_got = [fc_pairs[0]] + [xor_send(fc_pairs[j], "shard", evens[j]) for j in range(1, half)]
    fc_odd, out_near = split_columns(where, fc_got, span, ff_cols)
    fc_far = xor_send(fc_odd, "shard", 1)
    vectors = jnp.concatenate([got[2 * slot_rows(span) :][:1] for got in fc_got], 0)
    vectors = jnp.concatenate([vectors, xor_send(vectors, "shard", 1)], 0)
    vectors = vectors[:, : 8 * own_rows].astype(full)
    chosen = (jnp.arange(count)[:, None] ^ place == jnp.array(bits_of)[None, :]).astype(full)
    vectors = lax.dot(chosen, vectors, precision=lax.Precision.HIGHEST)
    vectors = vectors.reshape(count, 8, own_rows).transpose(1, 0, 2).reshape(8, D)
    b_query, b_value, b_out, b_proj, g_first, s_first, g_second, s_second = vectors
    qkv_stacks = lax.all_gather(qkv_stack.reshape(count * span, 3 * width), "replica")
    qkv_stacks = qkv_stacks.reshape(copies, count, span, 3 * width)
    w_qkv = assemble_copies(where, tie(qkv_stacks, *fc_got), own_rows)
    w_qkv = w_qkv.reshape(D, 3 * width)

    out_near = from_copies(out_near)
    out_far = [xor_send(block, "shard", 1) for block in out_near]
    w_out = assemble_rows(where, list(zip(out_near, out_far)), own_rows).reshape(D, D)
    fc_stack = jnp.concatenate(
        [got[:span, :ff_cols][None] for got in fc_got] + [fc_far], 0
    )
    fc_stacks = from_copies(fc_stack)
    w_fc = assemble_rows(where, [[stack] for stack in fc_stacks], own_rows).reshape(D, ff_cols)

    def own_heads(vector):
        vector = jnp.pad(vector, (0, count * width - D))
        return lax.dynamic_slice_in_dim(vector, place * width, width, 0)

    seqs = count // CP
    starts = lax.dynamic_slice_in_dim(offsets, copy * seqs, seqs, 0)[:, :, 0] // STRETCH
    is_at = starts[:, None, :] == jnp.arange(CP)[None, :, None]
    order = jnp.sum(jnp.where(is_at, jnp.arange(CP)[None, None, :], 0), axis=2)
    order = order + CP * jnp.arange(seqs)[:, None]
    bits = order ^ place
    order = jnp.concatenate([order, bits, rank_of(bits, count)], 0).astype(jnp.int32)

    normed_low = layer_norm(token_all.astype(full), g_first, s_first).astype(low)
    projected = mm(normed_low, w_qkv, 1, 0)
    queries = (projected[:, :width] + own_heads(b_query)).astype(low)
    keys = tie(projected, fc_stack)[:, width : 2 * width].astype(low)
    values = (projected[:, 2 * width :] + own_heads(b_value)).astype(low)
    cot_all = gather_rows(tie(cotangent, w_qkv))
    attended, log_total = attend_forward(order, queries, keys, values, heads)

    attended = tie(attended, *out_near)
    attended_own = order_heads(where, *exchange(list(attended.reshape(half, 2, STRETCH, width))))
    attended_own = attended_own[:, :D]
    in_rows = tokens.astype(full)
    middle = in_rows + mm(attended_own, w_out, 1, 0) + b_out
    second_own = layer_norm(middle, g_second, s_second).astype(low)
    second_all = gather_rows(tie(second_own, cot_all, fc_stacks[1]))
    hidden = mm(second_all, w_fc, 1, 0) + fc_bias.astype(full)
    active, pull_gelu = jax.vjp(gelu_tanh, hidden)
    active_low = active.astype(low)

    (hidden_grad,) = pull_gelu(mm(cot_all, proj_weight, 1, 1))
    hidden_low = hidden_grad.astype(low)
    second_part = mm(hidden_low, w_fc, 1, 1).astype(low)
    second_grad = scatter_rows(second_part).astype(full)

    proj_full = mm(tie(active_low, second_part), cot_all, 0, 0)
    fc_full = mm(tie(second_all, second_part), hidden_low, 0, 0)
    hidden_sums = jnp.sum(hidden_low.astype(full), axis=0).reshape(copies, 1, ff_cols // copies)
    hidden_sums = jnp.pad(hidden_sums, ((0, 0), (0, 15), (0, -ff_cols // copies % 128)))
    hidden_pieces = pack_hidden(
        where, fc_full.reshape(count, own_rows, ff_cols), proj_full, hidden_sums, copies
    )
    second_grad = tie(second_grad, hidden_pieces)
    hidden_shape = hidden_pieces.shape[1:]
    hidden_sum = lax.psum_scatter(
        hidden_pieces.reshape(-1, D), "replica", scatter_dimension=0, tiled=True
    ).reshape(hidden_shape)
    grad_rows = cotangent.astype(full)
    _, pull_second = jax.vjp(layer_norm, middle, g_second, s_second)
    middle_part, gsecond_part, ssecond_part = pull_second(second_grad)
    middle_grad = grad_rows + middle_part
    branch_low = middle_grad.astype(low)
    attended_grad = mm(branch_low, w_out, 1, 1).astype(low)
    attended_pairs = split_heads(where, attended_grad, count, width)
    outw_full = mm(attended_own, tie(branch_low, attended_pairs[0]), 0, 0)
    outw_near, outw_far = split_outw(where, outw_full.reshape(count, own_rows, D), copies)
    attended_grad = by_rank(*exchange(attended_pairs)).reshape(count * STRETCH, width)
    outw_far = xor_send(outw_far, "shard", 1)
    early = jnp.stack(
        [jnp.sum(branch_low.astype(full), axis=0), jnp.sum(grad_rows, axis=0), gsecond_part, ssecond_part]
    )

    query_grads, key_grads, value_grads = attend_backward(
        order, queries, keys, values, attended_grad, log_total, heads
    )
    projected_grad = jnp.concatenate([query_grads, key_grads, value_grads], 1)
    first_part = mm(projected_grad, w_qkv, 1, 1)
    first_part = with_layout_constraint(first_part, Layout((0, 1)))

    def head_sums(block):
        sums = jnp.sum(block.astype(full), axis=0)
        placed = lax.dynamic_update_slice_in_dim(
            jnp.zeros((count * width,), full), sums, place * width, 0
        )
        return placed[:D]

    norms = normed(token_all.astype(full))
    sums = jnp.stack(
        [
            head_sums(query_grads),
            head_sums(value_grads),
            early[0],
            early[1],
            jnp.sum(first_part * norms, axis=0),
            jnp.sum(first_part, axis=0),
            early[2],
            early[3],
        ]
    )
    sums = sums.reshape(8, count, own_rows).transpose(1, 0, 2).reshape(count, 8 * own_rows)
    by_bits = (jnp.arange(count)[:, None] ^ place == jnp.arange(count)[None, :]).astype(full)
    sums = lax.dot(by_bits, sums, precision=lax.Precision.HIGHEST)
    share = 8 * own_rows // copies
    sums = sums.reshape(count, copies, share).transpose(1, 0, 2)
    sums = jnp.pad(sums, ((0, 0), (0, 0), (0, 16 * 64 - share))).reshape(copies, count, 16, 64)
    first_grad = scatter_rows(first_part.astype(low)).astype(full)
    qkv_full = mm(normed_low, projected_grad, 0, 0).reshape(count, own_rows, 3 * width)
    last = pack_last(where, qkv_full, outw_near, outw_far, sums)
    first_grad = tie(first_grad, last[0])
    hidden_sum = tie(hidden_sum, last[0])
    last = to_copies(last)

    fc_sums, rest = sum_hidden(where, [hidden_sum], count, ff_cols)
    hidden_joined = join_hidden(where, *exchange(fc_sums), rest)
    hidden_stacks = from_copies(hidden_joined)
    fc_grad, proj_grad, fbias = finish_hidden(
        where, hidden_stacks, count, own_rows, ff_cols, ff_cols, hidden_sums.shape[2]
    )
    fbias = fbias[:, 0, : ff_cols // copies].reshape(ff_cols)

    last[0] = tie(last[0], hidden_joined)
    last = sum_last(where, last, count, 3 * width)
    output_low = tie(active_low, last[0])
    last = [last[0]] + [xor_send(last[j], "shard", evens[j]) for j in range(1, half)]
    _, pull_first = jax.vjp(lambda rows: layer_norm(rows, g_first, s_first), in_rows)
    (input_part,) = pull_first(first_grad)
    tokens_grad = (middle_grad + input_part).astype(low)
    last[1] = tie(last[1], tokens_grad)
    far = xor_send(odd_last(where, last, 3 * width), "shard", 1)
    last = from_copies(join_last(where, last, tie(far, hidden_stacks[1])))
    output_part = mm(output_low, proj_weight, 1, 0).astype(low)
    output = middle + b_proj + scatter_rows(output_part).astype(full)

    output = output.astype(low)
    last[0] = tie(last[0], output)

    qkv_grad, outw_grad, sums = finish_last(where, last, count, own_rows, width)
    sums = sums.reshape(copies, 16 * 64)[:, :share].reshape(8, own_rows)
    qbias, vbias, obias, pbias, gfirst, sfirst, gsecond, ssecond = sums
    return (
        output,
        tokens_grad,
        qkv_grad,
        outw_grad,
        fc_grad,
        proj_grad,
        qbias,
        vbias,
        obias,
        fbias,
        pbias,
        gfirst,
        sfirst,
        gsecond,
        ssecond,
    )


def solution(mesh):
    rows = P(("replica", "shard"), None)
    matrix = P("shard", None)
    vector = P("shard")
    return jax.shard_map(
        on_device,
        mesh=mesh,
        in_specs=(rows, P()) + (matrix,) * 4 + (vector,) * 9 + (rows,),
        out_specs=(rows, rows) + (matrix,) * 4 + (vector,) * 9,
        check_vma=False,
    )
```

```python
import functools

import jax
import jax.numpy as jnp
from jax import lax
from jax.experimental import pallas as pl
from jax.experimental.pallas import tpu as pltpu
from jax.experimental.layout import Layout, with_layout_constraint
from jax.sharding import PartitionSpec as P

D = 1600
H = 25
HD = 64
CP = 8
STRETCH = 128
SEQ = CP * STRETCH
TILE = 256

norm_eps = 1e-05
masked_score = -1e30
gelu_coeff = 0.7978845608028654
low = jnp.bfloat16
full = jnp.float32


def xor_send(block, axis, bits):
    count = lax.axis_size(axis)
    return lax.ppermute(block, axis, [(i, i ^ bits) for i in range(count)])


def normed(values):
    average = jnp.mean(values, axis=-1, keepdims=True)
    centred = values - average
    variance = jnp.mean(centred * centred, axis=-1, keepdims=True)
    return centred * lax.rsqrt(variance + norm_eps)


def layer_norm(values, gain_vec, shift_vec):
    return normed(values) * gain_vec + shift_vec


def gelu_tanh(values):
    return (
        0.5 * values * (1.0 + jnp.tanh(gelu_coeff * (values + 0.044715 * values * values * values)))
    )


def mm(left_side, right_side, left_dim, right_dim):
    return lax.dot_general(
        left_side,
        right_side,
        (((left_dim,), (right_dim,)), ((), ())),
        preferred_element_type=full,
    )


def sort_blocks(order_ref, seq, source, target):
    for place in range(CP):
        start = pl.multiple_of(order_ref[seq, place] * STRETCH, STRETCH)
        target[place * STRETCH : (place + 1) * STRETCH, :] = source[pl.ds(start, STRETCH), :]


def unsort_tile(order_ref, seq, tile, value, target):
    for part in range(TILE // STRETCH):
        place = tile * (TILE // STRETCH) + part
        start = pl.multiple_of(order_ref[seq, place] * STRETCH, STRETCH)
        target[pl.ds(start, STRETCH), :] = value[part * STRETCH : (part + 1) * STRETCH, :]


def causal(scores):
    key_row = lax.broadcasted_iota(jnp.int32, scores.shape, 0)
    query_col = lax.broadcasted_iota(jnp.int32, scores.shape, 1)
    return jnp.where(key_row <= query_col, scores, masked_score)


def forward_kernel(heads, seqs, order_ref, q_ref, k_ref, v_ref, a_ref, lse_ref, qs, ks, vs, qt, vt):
    width = heads * HD
    for seq in range(seqs):
        sort_blocks(order_ref, seq, q_ref, qs)
        sort_blocks(order_ref, seq, k_ref, ks)
        sort_blocks(order_ref, seq, v_ref, vs)
        qt[...] = (qs[...].astype(full).T * HD ** (-0.5)).astype(low)
        vt[...] = vs[...].astype(full).T.astype(low)
        for tile in range(SEQ // TILE):
            cols = slice(tile * TILE, (tile + 1) * TILE)
            before = tile * TILE
            pieces = []
            for head in range(heads):
                row = lax.broadcasted_iota(jnp.int32, (width, TILE), 0)
                mine = (row >= head * HD) & (row < (head + 1) * HD)
                query = jnp.where(mine, qt[:, cols], jnp.zeros((), low))
                diag = causal(mm(ks[cols, :], query, 1, 0))
                high = jnp.max(diag, axis=0, keepdims=True)
                if tile:
                    past = mm(ks[:before, :], query, 1, 0)
                    high = jnp.maximum(high, jnp.max(past, axis=0, keepdims=True))
                    past = jnp.exp(past - high)
                diag = jnp.exp(diag - high)
                total = jnp.sum(diag, axis=0, keepdims=True)
                if tile:
                    total = total + jnp.sum(past, axis=0, keepdims=True)
                share = 1.0 / total
                own = slice(head * HD, (head + 1) * HD)
                mixed = mm(vt[own, cols], (diag * share).astype(low), 1, 0)
                if tile:
                    mixed = mixed + mm(vt[own, :before], (past * share).astype(low), 1, 0)
                pieces.append(mixed)
                lse_ref[seq, head : head + 1, cols] = high + jnp.log(total)
            mixed = jnp.concatenate(pieces, 0).T.astype(low)
            unsort_tile(order_ref, seqs + seq, tile, mixed, a_ref)


def backward_kernel(
    heads, seqs, order_ref, q_ref, k_ref, v_ref, da_ref, lse_ref,
    dq_ref, dk_ref, dv_ref, qs, ks, vs, das, qt, kt, dat, dks, dvs,
):
    width = heads * HD
    scale = HD ** (-0.5)
    for seq in range(seqs):
        sort_blocks(order_ref, seq, q_ref, qs)
        sort_blocks(order_ref, seq, k_ref, ks)
        sort_blocks(order_ref, seq, v_ref, vs)
        sort_blocks(order_ref, 2 * seqs + seq, da_ref, das)
        qt[...] = (qs[...].astype(full).T * scale).astype(low)
        kt[...] = (ks[...].astype(full).T * scale).astype(low)
        dat[...] = das[...].astype(full).T.astype(low)
        dks[...] = jnp.zeros_like(dks)
        dvs[...] = jnp.zeros_like(dvs)
        for tile in range(SEQ // TILE):
            cols = slice(tile * TILE, (tile + 1) * TILE)
            before = tile * TILE
            pieces = []
            for head in range(heads):
                own = slice(head * HD, (head + 1) * HD)
                row = lax.broadcasted_iota(jnp.int32, (width, TILE), 0)
                mine = (row >= head * HD) & (row < (head + 1) * HD)
                lane = lax.broadcasted_iota(jnp.int32, (TILE, width), 1)
                mine_lane = (lane >= head * HD) & (lane < (head + 1) * HD)
                none = jnp.zeros((), low)
                query_t = jnp.where(mine, qt[:, cols], none)
                grad_t = jnp.where(mine, dat[:, cols], none)
                query = jnp.where(mine_lane, qs[cols, :], none)
                grad = jnp.where(mine_lane, das[cols, :], none)
                log_total = lse_ref[seq, head : head + 1, cols]

                spans = [(cols, True)] + ([(slice(0, before), False)] if tile else [])
                kept = []
                dot = None
                for span, edge in spans:
                    scores = mm(ks[span, :], query_t, 1, 0)
                    if edge:
                        scores = causal(scores)
                    weights = jnp.exp(scores - log_total)
                    weight_grads = mm(vs[span, :], grad_t, 1, 0)
                    part = jnp.sum(weights * weight_grads, axis=0, keepdims=True)
                    dot = part if dot is None else dot + part
                    dvs[span, :] += mm(weights.astype(low), grad, 1, 0)
                    kept.append((span, weights, weight_grads))
                total = None
                for span, weights, weight_grads in kept:
                    score_grads = (weights * (weight_grads - dot)).astype(low)
                    dks[span, :] += mm(score_grads, query, 1, 0)
                    part = mm(kt[own, span], score_grads, 1, 0)
                    total = part if total is None else total + part
                pieces.append(total)
            unsort_tile(order_ref, seq, tile, jnp.concatenate(pieces, 0).T.astype(low), dq_ref)
        for tile in range(SEQ // TILE):
            cols = slice(tile * TILE, (tile + 1) * TILE)
            unsort_tile(order_ref, seq, tile, (dks[cols, :] * scale).astype(low), dk_ref)
            unsort_tile(order_ref, seq, tile, dvs[cols, :].astype(low), dv_ref)


vmem = pl.BlockSpec(memory_space=pltpu.VMEM)
smem = pl.BlockSpec(memory_space=pltpu.SMEM)


def attend_forward(order, queries, keys, values, heads):
    rows, width = queries.shape
    seqs = rows // SEQ
    return pl.pallas_call(
        functools.partial(forward_kernel, heads, seqs),
        out_shape=(
            jax.ShapeDtypeStruct((rows, width), low),
            jax.ShapeDtypeStruct((seqs, heads, SEQ), full),
        ),
        in_specs=[smem, vmem, vmem, vmem],
        out_specs=(vmem, vmem),
        scratch_shapes=[pltpu.VMEM((SEQ, width), low)] * 3 + [pltpu.VMEM((width, SEQ), low)] * 2,
        compiler_params=pltpu.CompilerParams(vmem_limit_bytes=40 * 2**20),
        cost_estimate=pl.CostEstimate(
            flops=seqs * heads * 2 * 2 * SEQ * SEQ * 256,
            bytes_accessed=8 * rows * width,
            transcendentals=seqs * heads * SEQ * SEQ,
        ),
        name="attend_forward",
    )(order, queries, keys, values)


def attend_backward(order, queries, keys, values, grads, log_total, heads):
    rows, width = queries.shape
    seqs = rows // SEQ
    shape = jax.ShapeDtypeStruct((rows, width), low)
    return pl.pallas_call(
        functools.partial(backward_kernel, heads, seqs),
        out_shape=(shape, shape, shape),
        in_specs=[smem, vmem, vmem, vmem, vmem, vmem],
        out_specs=(vmem, vmem, vmem),
        scratch_shapes=[pltpu.VMEM((SEQ, width), low)] * 4
        + [pltpu.VMEM((width, SEQ), low)] * 3
        + [pltpu.VMEM((SEQ, width), full)] * 2,
        compiler_params=pltpu.CompilerParams(vmem_limit_bytes=48 * 2**20),
        cost_estimate=pl.CostEstimate(
            flops=seqs * heads * 2 * 5 * SEQ * SEQ * 256,
            bytes_accessed=14 * rows * width,
            transcendentals=seqs * heads * SEQ * SEQ,
        ),
        name="attend_backward",
    )(order, queries, keys, values, grads, log_total)


def ranks(count):
    return list(range(0, count, 2)) + list(range(1, count, 2))


def rank_of(bits, count):
    return (bits & 1) * (count // 2) + (bits >> 1)


def windows(rows, copies, unit):
    step = rows // copies // unit * unit
    return step, rows - step * (copies - 1)


def local_call(kernel, shapes, scratch, name, where, *operands, after=()):
    operands = operands + tuple(after)
    many = isinstance(shapes, (list, tuple))
    size = sum(x.size * x.dtype.itemsize for x in operands)
    free = pl.BlockSpec(memory_space=pl.ANY)
    used = len(operands) - len(after)
    return pl.pallas_call(
        kernel,
        out_shape=tuple(shapes) if many else shapes,
        in_specs=[smem] + [vmem] * used + [free] * len(after),
        out_specs=tuple(vmem for _ in shapes) if many else vmem,
        scratch_shapes=scratch,
        compiler_params=pltpu.CompilerParams(vmem_limit_bytes=56 * 2**20),
        cost_estimate=pl.CostEstimate(flops=0, bytes_accessed=3 * size, transcendentals=0),
        name=name,
    )(where, *operands)


def pack_heads(where, weight, copies, count, width):
    step, span = windows(weight.shape[0], copies, 16)

    def kernel(where_ref, weight_ref, *refs):
        outs, pieces = refs[: count // 2], refs[count // 2]
        start = pl.multiple_of(where_ref[1] * step, 16)
        for other in range(count):
            low_col, high_col = other * width, min(D, (other + 1) * width)
            for third in range(3):
                have = max(0, high_col - low_col)
                at = third * width
                if have:
                    pieces[other, :, at : at + have] = weight_ref[
                        pl.ds(start, span), third * D + low_col : third * D + high_col
                    ]
                if have < width:
                    pieces[other, :, at + have : at + width] = jnp.zeros((span, width - have), low)
        for bits in range(count):
            outs[bits // 2][bits % 2] = pieces[where_ref[0] ^ bits]

    shape = jax.ShapeDtypeStruct((2, span, 3 * width), low)
    scratch = [pltpu.VMEM((count, span, 3 * width), low)]
    return local_call(kernel, [shape] * (count // 2), scratch, "pack_heads", where, weight)


def slot_rows(span):
    return -(-span // 8) * 8


def pack_columns(where, weight, out_weight, vectors, copies, count):
    step, span = windows(weight.shape[0], copies, 16)
    cols = weight.shape[1] // count
    slot = slot_rows(span)

    def kernel(where_ref, weight_ref, out_ref, vectors_ref, *refs):
        outs, pieces = refs[: count // 2], refs[count // 2]
        start = pl.multiple_of(where_ref[1] * step, 16)
        for other in range(count):
            pieces[other] = weight_ref[pl.ds(start, span), other * cols : (other + 1) * cols]
        for pair, out in enumerate(outs):
            for side in range(2):
                out[:span, side * cols : (side + 1) * cols] = pieces[
                    where_ref[0] ^ (2 * pair + side)
                ]
            out[slot : slot + span, :] = out_ref[pl.ds(start, span), :]
            out[2 * slot :, :] = vectors_ref[...]

    shape = jax.ShapeDtypeStruct((2 * slot + 8, D), low)
    scratch = [pltpu.VMEM((count, span, cols), low)]
    return local_call(
        kernel, [shape] * (count // 2), scratch, "pack_columns", where, weight, out_weight, vectors
    )


def split_columns(where, got, span, cols):
    half = len(got)
    slot = slot_rows(span)

    def kernel(where_ref, *refs):
        odd, rows = refs[half:]
        for pair in range(half):
            odd[pair] = refs[pair][:span, cols : 2 * cols]
            rows[pair] = refs[pair][slot : slot + span, :]

    shapes = [
        jax.ShapeDtypeStruct((half, span, cols), low),
        jax.ShapeDtypeStruct((half, span, D), low),
    ]
    return local_call(kernel, shapes, [], "split_columns", where, *got)


def assemble_rows(where, stacks, own_rows):
    each = len(stacks[0])
    count = sum(array.shape[0] for array in stacks[0])
    span, cols = stacks[0][0].shape[1:]
    step, _ = windows(own_rows, len(stacks), 16)
    stacks = stacks if step else stacks[:1]
    copies = len(stacks)
    arrays = [array for stack in stacks for array in stack]

    def kernel(where_ref, *refs):
        out = refs[-1]
        for bits_copy in range(copies):
            start = pl.multiple_of((where_ref[1] ^ bits_copy) * step, 16)
            blocks = [
                ref.at[row]
                for ref in refs[bits_copy * each : (bits_copy + 1) * each]
                for row in range(ref.shape[0])
            ]
            for block, bits in zip(blocks, ranks(count)):
                out[where_ref[0] ^ bits, pl.ds(start, span), :] = block[...]

    shape = jax.ShapeDtypeStruct((count, own_rows, cols), low)
    return local_call(kernel, shape, [], "assemble_rows", where, *arrays)


def assemble_copies(where, stacks, own_rows):
    copies, count, span, cols = stacks.shape
    step, _ = windows(own_rows, copies, 16)

    def kernel(where_ref, stacks_ref, out):
        for copy in range(copies if step else 1):
            for rank, bits in enumerate(ranks(count)):
                out[where_ref[0] ^ bits, copy * step : copy * step + span, :] = stacks_ref[
                    copy, rank
                ]

    shape = jax.ShapeDtypeStruct((count, own_rows, cols), low)
    return local_call(kernel, shape, [], "assemble_copies", where, stacks)


def split_heads(where, block, count, width):
    rows, cols = block.shape

    def kernel(where_ref, block_ref, *refs):
        outs, pieces = refs[: count // 2], refs[count // 2]
        for other in range(count):
            start, stop = min(cols, other * width), min(cols, (other + 1) * width)
            if start < stop:
                pieces[other, :, : stop - start] = block_ref[:, start:stop]
            if stop - start < width:
                pieces[other, :, stop - start :] = jnp.zeros((rows, width - stop + start), low)
        for bits in range(count):
            outs[bits // 2][bits % 2] = pieces[where_ref[0] ^ bits]

    shape = jax.ShapeDtypeStruct((2, rows, width), low)
    scratch = [pltpu.VMEM((count, rows, width), low)]
    return local_call(kernel, [shape] * (count // 2), scratch, "split_heads", where, block)


def order_heads(where, pairs, far):
    half = len(pairs)
    count = 2 * half
    _, rows, width = far.shape

    def kernel(where_ref, *refs):
        out, pieces = refs[-2], refs[-1]
        for pair in range(half):
            pieces[2 * pair] = refs[pair][0]
            pieces[2 * pair + 1] = refs[half][pair]
        for other in range(count):
            out[:, other * width : (other + 1) * width] = pieces[where_ref[0] ^ other]

    shape = jax.ShapeDtypeStruct((rows, count * width), low)
    scratch = [pltpu.VMEM((count, rows, width), low)]
    return local_call(kernel, shape, scratch, "order_heads", where, *pairs, far)


SLOTS = 4


def lane_of(bits, cols):
    return bits // SLOTS * cols


def own_block(ref, bits, cols, groups):
    slot, group = lax.rem(bits, SLOTS), lax.div(bits, SLOTS)
    value = ref[slot, :, :cols].astype(full)
    for index in range(1, groups):
        other = ref[slot, :, index * cols : (index + 1) * cols].astype(full)
        value = jnp.where(group == index, other, value)
    return value


def pack_hidden(where, fc_full, proj_full, sums, copies):
    count, rows, cols = fc_full.shape
    step, span = windows(rows, copies, 16)
    proj_step, proj_span = windows(proj_full.shape[0], copies, 8)
    extra = -(-(proj_span + 16) // span)
    after = slot_rows(proj_span) - (extra - 1) * span

    def kernel(where_ref, fc_ref, proj_ref, sums_ref, out_ref):
        for copy in range(copies):
            out = out_ref.at[copy]
            for bits in range(count):
                lane = lane_of(bits, cols)
                out[bits % SLOTS, :, lane : lane + cols] = fc_ref[
                    where_ref[0] ^ bits, copy * step : copy * step + span, :
                ].astype(low)
            for slot in range(extra):
                length = min(span, proj_span - slot * span)
                if length > 0:
                    at = copy * proj_step + slot * span
                    out[SLOTS + slot, :length, :] = proj_ref[at : at + length, :].astype(low)
            out[SLOTS + extra - 1, after : after + 16, : sums.shape[2]] = sums_ref[copy].astype(low)

    shape = jax.ShapeDtypeStruct((copies, SLOTS + extra, span, D), low)
    return local_call(kernel, shape, [], "pack_hidden", where, fc_full, proj_full, sums)


def sum_hidden(where, pieces, count, cols):
    number = len(pieces)
    slots, span, _ = pieces[0].shape

    def kernel(where_ref, *refs):
        outs, rest = refs[number:-1], refs[-1]
        for slot in range(slots):
            total = refs[0][slot].astype(full)
            for piece in refs[1:number]:
                total = total + piece[slot].astype(full)
            total = total.astype(low)
            if slot >= SLOTS:
                rest[slot - SLOTS] = total
                continue
            for bits in range(slot, count, SLOTS):
                lane = lane_of(bits, cols)
                outs[bits // 2][bits % 2] = total[:, lane : lane + cols]

    shapes = [jax.ShapeDtypeStruct((2, span, cols), low)] * (count // 2)
    shapes.append(jax.ShapeDtypeStruct((slots - SLOTS, span, D), low))
    outs = local_call(kernel, shapes, [], "sum_hidden", where, *pieces)
    return outs[:-1], outs[-1]


def join_hidden(where, got, far, rest):
    half = len(got)
    _, span, cols = far.shape

    def kernel(where_ref, *refs):
        out = refs[-1]
        for bits in range(2 * half):
            block = refs[half][bits // 2] if bits % 2 else refs[bits // 2][0]
            lane = lane_of(bits, cols)
            out[bits % SLOTS, :, lane : lane + cols] = block
        for slot in range(rest.shape[0]):
            out[SLOTS + slot] = refs[half + 1][slot]

    shape = jax.ShapeDtypeStruct((SLOTS + rest.shape[0], span, D), low)
    return local_call(kernel, shape, [], "join_hidden", where, *got, far, rest)


def finish_hidden(where, stacks, count, rows, cols, proj_rows, lanes):
    copies = len(stacks)
    slots, span, _ = stacks[0].shape
    step, _ = windows(rows, copies, 16)
    proj_step, proj_span = windows(proj_rows, copies, 8)
    extra = slots - SLOTS
    after = slot_rows(proj_span) - (extra - 1) * span

    def kernel(where_ref, *refs):
        fc_out, proj_out, sums_out = refs[copies:]
        for index in range(copies):
            piece, copy = refs[index], where_ref[1] ^ index
            start = pl.multiple_of(copy * step, 16)
            if step or index == 0:
                for other in range(count):
                    fc_out[pl.ds(start, span), other * cols : (other + 1) * cols] = own_block(
                        piece, where_ref[0] ^ other, cols, count // SLOTS
                    )
            for slot in range(extra):
                length = min(span, proj_span - slot * span)
                if length > 0:
                    at = copy * proj_step
                    at = pl.multiple_of(at + slot * span, 8) if span % 8 == 0 else at
                    proj_out[pl.ds(at, length), :] = piece[SLOTS + slot, :length, :].astype(full)
            sums_out[copy] = piece[SLOTS + extra - 1, after : after + 16, :lanes].astype(full)

    shapes = [
        jax.ShapeDtypeStruct((rows, count * cols), full),
        jax.ShapeDtypeStruct((proj_rows, D), full),
        jax.ShapeDtypeStruct((copies, 16, lanes), full),
    ]
    return local_call(kernel, shapes, [], "finish_hidden", where, *stacks)


def split_outw(where, grad, copies):
    count, rows, cols = grad.shape
    half = count // 2
    step, span = windows(rows, copies, 16)
    parts = copies if step else 1

    def kernel(where_ref, grad_ref, *refs):
        far = refs[parts]
        for index in range(parts):
            start = pl.multiple_of((where_ref[1] ^ index) * step, 16)
            for pair in range(half):
                for side, out in enumerate((refs[index], far.at[index])):
                    out[pair] = grad_ref[
                        where_ref[0] ^ (2 * pair + side), pl.ds(start, span), :
                    ].astype(low)

    shapes = [jax.ShapeDtypeStruct((half, span, cols), low)] * parts
    shapes.append(jax.ShapeDtypeStruct((parts, half, span, cols), low))
    outs = local_call(kernel, shapes, [], "split_outw", where, grad)
    return outs[:-1], outs[-1]


def pack_last(where, qkv_full, near, far, sums):
    copies, parts = sums.shape[0], len(near)
    count, rows, cols = qkv_full.shape
    half = count // 2
    step, span = windows(rows, copies, 16)
    spare = count // SLOTS * cols

    def kernel(where_ref, qkv_ref, *refs):
        far_ref, sums_ref = refs[parts], refs[parts + 1]
        for index, out in enumerate(refs[parts + 2 :]):
            copy = where_ref[1] ^ index
            start = pl.multiple_of(copy * step, 16)
            for bits in range(count):
                lane = lane_of(bits, cols)
                out[bits % SLOTS, :, lane : lane + cols] = qkv_ref[
                    where_ref[0] ^ bits, pl.ds(start, span), :
                ].astype(low)
                row = bits // SLOTS * 16
                out[bits % SLOTS, row : row + 16, spare : spare + 64] = sums_ref[copy, bits].astype(
                    low
                )
            for pair in range(half):
                total = refs[index % parts][pair].astype(full)
                total = total + far_ref[index % parts, pair].astype(full)
                out[SLOTS + pair] = total.astype(low)

    shape = jax.ShapeDtypeStruct((SLOTS + half, span, D), low)
    return local_call(kernel, [shape] * copies, [], "pack_last", where, qkv_full, *near, far, sums)


def sum_last(where, pieces, count, cols):
    number = len(pieces)
    half = count // 2
    span = pieces[0].shape[1]
    spare = count // SLOTS * cols

    def kernel(where_ref, *refs):
        outs = refs[number:]
        for slot in range(SLOTS + half):
            total = refs[0][slot].astype(full)
            for piece in refs[1:number]:
                total = total + piece[slot].astype(full)
            total = total.astype(low)
            if slot >= SLOTS:
                outs[slot - SLOTS][1] = total
                continue
            for bits in range(slot, count, SLOTS):
                lane, row, side = lane_of(bits, cols), bits // SLOTS * 16, bits % 2
                out = outs[bits // 2]
                out[0, :, side * cols : (side + 1) * cols] = total[:, lane : lane + cols]
                out[0, side * 16 : side * 16 + 16, 2 * cols : 2 * cols + 64] = total[
                    row : row + 16, spare : spare + 64
                ]

    shape = jax.ShapeDtypeStruct((2, span, D), low)
    return local_call(kernel, [shape] * half, [], "sum_last", where, *pieces)


def odd_last(where, got, cols):
    half = len(got)
    span = got[0].shape[1]

    def kernel(where_ref, *refs):
        out = refs[half]
        for pair in range(half):
            out[pair, :, :cols] = refs[pair][0, :, cols : 2 * cols]
            out[pair, :16, cols : cols + 64] = refs[pair][0, 16:32, 2 * cols : 2 * cols + 64]

    shape = jax.ShapeDtypeStruct((half, span, cols + 64), low)
    return local_call(kernel, shape, [], "odd_last", where, *got)


def join_last(where, got, far):
    half = len(got)
    _, span, wide = far.shape
    cols = wide - 64
    spare = 2 * half // SLOTS * cols

    def kernel(where_ref, *refs):
        far_ref, out = refs[half], refs[half + 1]
        sums = jnp.zeros((16, 64), full)
        total = jnp.zeros((span, D), full)
        for pair in range(half):
            for side in range(2):
                lane = lane_of(2 * pair + side, cols)
                block = far_ref[pair, :, :cols] if side else refs[pair][0, :, :cols]
                out[(2 * pair + side) % SLOTS, :, lane : lane + cols] = block
            sums = sums + refs[pair][0, :16, 2 * cols : 2 * cols + 64].astype(full)
            sums = sums + far_ref[pair, :16, cols : cols + 64].astype(full)
            total = total + refs[pair][1].astype(full)
        out[SLOTS] = total.astype(low)
        out[0, :16, spare : spare + 64] = sums.astype(low)

    shape = jax.ShapeDtypeStruct((SLOTS + 1, span, D), low)
    return local_call(kernel, shape, [], "join_last", where, *got, far)


def finish_last(where, stacks, count, rows, width):
    copies = len(stacks)
    span = stacks[0].shape[1]
    step, _ = windows(rows, copies, 16)
    cols = 3 * width
    spare = count // SLOTS * cols

    def kernel(where_ref, *refs):
        qkv_out, outw_out, sums_out = refs[copies:]
        for index in range(copies):
            piece, copy = refs[index], where_ref[1] ^ index
            start = pl.multiple_of(copy * step, 16)
            sums_out[copy] = piece[0, :16, spare : spare + 64].astype(full)
            if index and not step:
                continue
            outw_out[pl.ds(start, span), :] = piece[SLOTS].astype(full)
            for other in range(count):
                have = min(width, D - other * width)
                if have <= 0:
                    continue
                block = own_block(piece, where_ref[0] ^ other, cols, count // SLOTS)
                for third in range(3):
                    target = third * D + other * width
                    qkv_out[pl.ds(start, span), target : target + have] = block[
                        :, third * width : third * width + have
                    ]

    shapes = [
        jax.ShapeDtypeStruct((rows, 3 * D), full),
        jax.ShapeDtypeStruct((rows, D), full),
        jax.ShapeDtypeStruct((copies, 16, 64), full),
    ]
    return local_call(kernel, shapes, [], "finish_last", where, *stacks)


def on_device(
    tokens,
    offsets,
    qkv_weight,
    out_weight,
    fc_weight,
    proj_weight,
    query_bias,
    value_bias,
    out_bias,
    fc_bias,
    proj_bias,
    gain_first,
    shift_first,
    gain_second,
    shift_second,
    cotangent,
):
    count = lax.axis_size("shard")
    copies = lax.axis_size("replica")
    place = lax.axis_index("shard")
    copy = lax.axis_index("replica")
    where = jnp.stack([place, copy]).astype(jnp.int32)
    evens = list(range(0, count, 2))
    bits_of = ranks(count)
    half = count // 2
    heads = -(-H // count)
    span = windows(D // count, copies, 16)[1]
    width = heads * HD
    own_rows = D // count
    ff_cols = fc_weight.shape[1] // count

    def gather_rows(block):
        return lax.all_gather(block, "shard", axis=0, tiled=True)

    def scatter_rows(blocks):
        blocks = with_layout_constraint(blocks, Layout((0, 1)))
        return lax.psum_scatter(blocks, "shard", scatter_dimension=0, tiled=True)

    def exchange(pairs):
        got = [pairs[0]] + [xor_send(pairs[j], "shard", evens[j]) for j in range(1, half)]
        return got, xor_send(jnp.concatenate([pair[1:] for pair in got], 0), "shard", 1)

    def by_rank(got, far):
        return jnp.concatenate([pair[:1] for pair in got] + [far], 0)

    def from_copies(block):
        return [block] + [xor_send(block, "replica", bits) for bits in range(1, copies)]

    def to_copies(pieces):
        return [pieces[0]] + [xor_send(pieces[bits], "replica", bits) for bits in range(1, copies)]

    def tie(value, *others):
        return lax.optimization_barrier((value,) + others)[0]

    vectors = (
        query_bias,
        value_bias,
        out_bias,
        proj_bias,
        gain_first,
        shift_first,
        gain_second,
        shift_second,
    )
    token_all = gather_rows(tokens)
    qkv_got, qkv_far = exchange(pack_heads(where, qkv_weight, copies, count, width))
    qkv_stack = by_rank(qkv_got, qkv_far)
    vectors = tie(jnp.concatenate(vectors), qkv_stack, token_all)
    vectors = jnp.pad(vectors[None], ((0, 7), (0, D - 8 * own_rows)))
    fc_pairs = pack_columns(where, fc_weight, out_weight, vectors, copies, count)
    fc_got = [fc_pairs[0]] + [xor_send(fc_pairs[j], "shard", evens[j]) for j in range(1, half)]
    fc_odd, out_near = split_columns(where, fc_got, span, ff_cols)
    fc_far = xor_send(fc_odd, "shard", 1)
    vectors = jnp.concatenate([got[2 * slot_rows(span) :][:1] for got in fc_got], 0)
    vectors = jnp.concatenate([vectors, xor_send(vectors, "shard", 1)], 0)
    vectors = vectors[:, : 8 * own_rows].astype(full)
    chosen = (jnp.arange(count)[:, None] ^ place == jnp.array(bits_of)[None, :]).astype(full)
    vectors = lax.dot(chosen, vectors, precision=lax.Precision.HIGHEST)
    vectors = vectors.reshape(count, 8, own_rows).transpose(1, 0, 2).reshape(8, D)
    b_query, b_value, b_out, b_proj, g_first, s_first, g_second, s_second = vectors
    qkv_stacks = lax.all_gather(qkv_stack.reshape(count * span, 3 * width), "replica")
    qkv_stacks = qkv_stacks.reshape(copies, count, span, 3 * width)
    w_qkv = assemble_copies(where, tie(qkv_stacks, *fc_got), own_rows)
    w_qkv = w_qkv.reshape(D, 3 * width)

    out_near = from_copies(out_near)
    out_far = [xor_send(block, "shard", 1) for block in out_near]
    w_out = assemble_rows(where, list(zip(out_near, out_far)), own_rows).reshape(D, D)
    fc_stack = jnp.concatenate(
        [got[:span, :ff_cols][None] for got in fc_got] + [fc_far], 0
    )
    fc_stacks = from_copies(fc_stack)
    w_fc = assemble_rows(where, [[stack] for stack in fc_stacks], own_rows).reshape(D, ff_cols)

    def own_heads(vector):
        vector = jnp.pad(vector, (0, count * width - D))
        return lax.dynamic_slice_in_dim(vector, place * width, width, 0)

    seqs = count // CP
    starts = lax.dynamic_slice_in_dim(offsets, copy * seqs, seqs, 0)[:, :, 0] // STRETCH
    is_at = starts[:, None, :] == jnp.arange(CP)[None, :, None]
    order = jnp.sum(jnp.where(is_at, jnp.arange(CP)[None, None, :], 0), axis=2)
    order = order + CP * jnp.arange(seqs)[:, None]
    bits = order ^ place
    order = jnp.concatenate([order, bits, rank_of(bits, count)], 0).astype(jnp.int32)

    normed_low = layer_norm(token_all.astype(full), g_first, s_first).astype(low)
    projected = mm(normed_low, w_qkv, 1, 0)
    queries = (projected[:, :width] + own_heads(b_query)).astype(low)
    keys = tie(projected, fc_stack)[:, width : 2 * width].astype(low)
    values = (projected[:, 2 * width :] + own_heads(b_value)).astype(low)
    cot_all = gather_rows(tie(cotangent, w_qkv))
    attended, log_total = attend_forward(order, queries, keys, values, heads)

    attended = tie(attended, *out_near)
    attended_own = order_heads(where, *exchange(list(attended.reshape(half, 2, STRETCH, width))))
    attended_own = attended_own[:, :D]
    in_rows = tokens.astype(full)
    middle = in_rows + mm(attended_own, w_out, 1, 0) + b_out
    second_own = layer_norm(middle, g_second, s_second).astype(low)
    second_all = gather_rows(tie(second_own, cot_all, fc_stacks[1]))
    hidden = mm(second_all, w_fc, 1, 0) + fc_bias.astype(full)
    active, pull_gelu = jax.vjp(gelu_tanh, hidden)
    active_low = active.astype(low)

    (hidden_grad,) = pull_gelu(mm(cot_all, proj_weight, 1, 1))
    hidden_low = hidden_grad.astype(low)
    second_part = mm(hidden_low, w_fc, 1, 1).astype(low)
    second_grad = scatter_rows(second_part).astype(full)

    proj_full = mm(tie(active_low, second_part), cot_all, 0, 0)
    fc_full = mm(tie(second_all, second_part), hidden_low, 0, 0)
    hidden_sums = jnp.sum(hidden_low.astype(full), axis=0).reshape(copies, 1, ff_cols // copies)
    hidden_sums = jnp.pad(hidden_sums, ((0, 0), (0, 15), (0, -ff_cols // copies % 128)))
    hidden_pieces = pack_hidden(
        where, fc_full.reshape(count, own_rows, ff_cols), proj_full, hidden_sums, copies
    )
    second_grad = tie(second_grad, hidden_pieces)
    hidden_shape = hidden_pieces.shape[1:]
    hidden_sum = lax.psum_scatter(
        hidden_pieces.reshape(-1, D), "replica", scatter_dimension=0, tiled=True
    ).reshape(hidden_shape)
    grad_rows = cotangent.astype(full)
    _, pull_second = jax.vjp(layer_norm, middle, g_second, s_second)
    middle_part, gsecond_part, ssecond_part = pull_second(second_grad)
    middle_grad = grad_rows + middle_part
    branch_low = middle_grad.astype(low)
    attended_grad = mm(branch_low, w_out, 1, 1).astype(low)
    attended_pairs = split_heads(where, attended_grad, count, width)
    outw_full = mm(attended_own, tie(branch_low, attended_pairs[0]), 0, 0)
    outw_near, outw_far = split_outw(where, outw_full.reshape(count, own_rows, D), copies)
    attended_grad = by_rank(*exchange(attended_pairs)).reshape(count * STRETCH, width)
    outw_far = xor_send(outw_far, "shard", 1)
    early = jnp.stack(
        [jnp.sum(branch_low.astype(full), axis=0), jnp.sum(grad_rows, axis=0), gsecond_part, ssecond_part]
    )

    query_grads, key_grads, value_grads = attend_backward(
        order, queries, keys, values, attended_grad, log_total, heads
    )
    projected_grad = jnp.concatenate([query_grads, key_grads, value_grads], 1)
    first_part = mm(projected_grad, w_qkv, 1, 1)
    first_part = with_layout_constraint(first_part, Layout((0, 1)))

    def head_sums(block):
        sums = jnp.sum(block.astype(full), axis=0)
        placed = lax.dynamic_update_slice_in_dim(
            jnp.zeros((count * width,), full), sums, place * width, 0
        )
        return placed[:D]

    norms = normed(token_all.astype(full))
    sums = jnp.stack(
        [
            head_sums(query_grads),
            head_sums(value_grads),
            early[0],
            early[1],
            jnp.sum(first_part * norms, axis=0),
            jnp.sum(first_part, axis=0),
            early[2],
            early[3],
        ]
    )
    sums = sums.reshape(8, count, own_rows).transpose(1, 0, 2).reshape(count, 8 * own_rows)
    by_bits = (jnp.arange(count)[:, None] ^ place == jnp.arange(count)[None, :]).astype(full)
    sums = lax.dot(by_bits, sums, precision=lax.Precision.HIGHEST)
    share = 8 * own_rows // copies
    sums = sums.reshape(count, copies, share).transpose(1, 0, 2)
    sums = jnp.pad(sums, ((0, 0), (0, 0), (0, 16 * 64 - share))).reshape(copies, count, 16, 64)
    first_grad = scatter_rows(first_part.astype(low)).astype(full)
    qkv_full = mm(normed_low, projected_grad, 0, 0).reshape(count, own_rows, 3 * width)
    last = pack_last(where, qkv_full, outw_near, outw_far, sums)
    first_grad = tie(first_grad, last[0])
    hidden_sum = tie(hidden_sum, last[0])
    last = to_copies(last)

    fc_sums, rest = sum_hidden(where, [hidden_sum], count, ff_cols)
    hidden_joined = join_hidden(where, *exchange(fc_sums), rest)
    hidden_stacks = from_copies(hidden_joined)
    fc_grad, proj_grad, fbias = finish_hidden(
        where, hidden_stacks, count, own_rows, ff_cols, ff_cols, hidden_sums.shape[2]
    )
    fbias = fbias[:, 0, : ff_cols // copies].reshape(ff_cols)

    last[0] = tie(last[0], hidden_joined)
    last = sum_last(where, last, count, 3 * width)
    last = [last[0]] + [xor_send(last[j], "shard", evens[j]) for j in range(1, half)]
    output_low = tie(active_low, last[1])
    _, pull_first = jax.vjp(lambda rows: layer_norm(rows, g_first, s_first), in_rows)
    (input_part,) = pull_first(first_grad)
    tokens_grad = (middle_grad + input_part).astype(low)
    last[1] = tie(last[1], tokens_grad)
    far = xor_send(odd_last(where, last, 3 * width), "shard", 1)
    last = from_copies(join_last(where, last, tie(far, hidden_stacks[1])))
    output_part = mm(output_low, proj_weight, 1, 0).astype(low)
    output = middle + b_proj + scatter_rows(output_part).astype(full)

    output = output.astype(low)
    last[0] = tie(last[0], output)

    qkv_grad, outw_grad, sums = finish_last(where, last, count, own_rows, width)
    sums = sums.reshape(copies, 16 * 64)[:, :share].reshape(8, own_rows)
    qbias, vbias, obias, pbias, gfirst, sfirst, gsecond, ssecond = sums
    return (
        output,
        tokens_grad,
        qkv_grad,
        outw_grad,
        fc_grad,
        proj_grad,
        qbias,
        vbias,
        obias,
        fbias,
        pbias,
        gfirst,
        sfirst,
        gsecond,
        ssecond,
    )


def solution(mesh):
    rows = P(("replica", "shard"), None)
    matrix = P("shard", None)
    vector = P("shard")
    return jax.shard_map(
        on_device,
        mesh=mesh,
        in_specs=(rows, P()) + (matrix,) * 4 + (vector,) * 9 + (rows,),
        out_specs=(rows, rows) + (matrix,) * 4 + (vector,) * 9,
        check_vma=False,
    )
```
